32 devices in a mesh: group: 2 (over y), gz: 4 (over z), gx: 2 (over x), af: 2 (over core).
Axes of the slice: x: 2, y: 2, z: 4, core: 2. Of those that a mesh axis runs over, the one named last changes fastest.
Arguments:
- voltage_lateral_component: float32 [2, 256, 64, 128], P('af', ('group', 'gz'), 'gx'), parts along dimension 1, may hold values from -6 to 6
- voltage_vertical_component: float32 [2, 256, 64, 128], P('af', ('group', 'gz'), 'gx'), parts along dimension 1, may hold values from -6 to 6
- voltage_forward_component: float32 [2, 256, 64, 128], P('af', ('group', 'gz'), 'gx'), parts along dimension 1, may hold values from -6 to 6
- induction_lateral_component: float32 [2, 256, 64, 128], P('af', ('group', 'gz'), 'gx'), parts along dimension 1, may hold values from -6 to 6
- induction_vertical_component: float32 [2, 256, 64, 128], P('af', ('group', 'gz'), 'gx'), parts along dimension 1, may hold values from -6 to 6
- induction_forward_component: float32 [2, 256, 64, 128], P('af', ('group', 'gz'), 'gx'), parts along dimension 1, may hold values from -6 to 6
- medium_code: int32 [256, 64, 128], P(('group', 'gz'), 'gx'), parts along dimension 0, may hold values from 0 to 2
- nonlinear_coefficient_matrix: float32 [2, 3], replicated, may hold values from 0.3 to 3
- mobile_charge_density: float32 [64, 16], P(('group', 'gz', 'gx')), parts along dimension 0, may hold values from 0.5 to 2
Outputs:
- electric_x_out: float32 [2, 256, 64, 128], P('af', ('group', 'gz'), 'gx'), parts along dimension 1
- electric_y_out: float32 [2, 256, 64, 128], P('af', ('group', 'gz'), 'gx'), parts along dimension 1
- electric_z_out: float32 [2, 256, 64, 128], P('af', ('group', 'gz'), 'gx'), parts along dimension 1
- magnetic_x_out: float32 [2, 256, 64, 128], P('af', ('group', 'gz'), 'gx'), parts along dimension 1
- magnetic_y_out: float32 [2, 256, 64, 128], P('af', ('group', 'gz'), 'gx'), parts along dimension 1
- magnetic_z_out: float32 [2, 256, 64, 128], P('af', ('group', 'gz'), 'gx'), parts along dimension 1
- density_out: float32 [64, 16], P(('group', 'gz', 'gx')), parts along dimension 0
The draws below stay inside these ranges and needn't reach their ends.
There are 2 independent parts, one for each index of `group`. The reference program is written for one: setup_inputs(seed, part) draws one part's arguments, and reference() takes and returns one part's arrays. A program takes and returns all parts, laid end to end along the dimension named above; an argument that names none is the same for every part. Nothing has to cross between parts.
All inputs are finite; a program needn't handle non-finite values.
Results may differ from the reference program's by a relative error of at most 0.0001.
Values sent between devices are 32-bit elements; how exact they have to be, the bound alone decides.
No kernel may reach another device: no remote copies, remote signals or barrier semaphores. Data moves between devices by JAX's collectives and lax.ppermute only.
A program may use at most 64 MiB of HBM per device.

```python
import math
import jax
import jax.numpy as jnp

CY = 128
BLOCK_FACTOR = 4
SUBSTEPS = 4
ROUNDS = 2
CSTEPS = 8
NZ = 128
NX = 64
DOPANT_SPAN_CELLS = 32
DOPANT_CROSS = 16


def plant(values, stream_key, smallest, largest):
    extent = values.shape
    place = [jax.random.randint(jax.random.fold_in(stream_key, axis), (), 0, extent[axis]) for axis in range(len(extent))]
    values = values.at[tuple(place)].set(smallest)
    longest = extent.index(max(extent))
    place[longest] = (place[longest] + 1) % extent[longest]
    return values.at[tuple(place)].set(largest)


def block_scale(key, extent, pieces, least, top_value):
    def one(dim, parts):
        heights = jax.random.uniform(jax.random.fold_in(jax.random.fold_in(key, 6), dim), (parts,), jnp.float32, least / len(pieces), top_value / len(pieces))
        return jnp.repeat(jnp.exp(heights), extent[dim] // parts).reshape((-1,) + (1,) * (len(extent) - dim - 1))

    level = one(*pieces[0])
    for cut in pieces[1:]:
        level = level * one(*cut)
    return level


def bell_draw(own_key, shape, deviation, limit, pieces=(), kind=jnp.bfloat16):
    drawn = deviation * jax.random.normal(own_key, shape, jnp.float32)
    if pieces:
        drawn = drawn * block_scale(own_key, shape, pieces, -0.22, 0.18)
    return jnp.clip(drawn, -limit, limit).astype(kind)


def setup_inputs(seed: int = 0, part: int = 0) -> dict:
    key_of = jax.random.split(jax.random.key(seed), 10)
    own_keys = jax.random.split(jax.random.fold_in(key_of[9], part), 10)
    return {
        "voltage_lateral_component": bell_draw(own_keys[0], (2, NZ, NX, CY), 1.0, 6.0, ((0, 2), (1, 4), (2, 2)), jnp.float32),
        "voltage_vertical_component": bell_draw(own_keys[1], (2, NZ, NX, CY), 1.0, 6.0, ((0, 2), (1, 4), (2, 2)), jnp.float32),
        "voltage_forward_component": bell_draw(own_keys[2], (2, NZ, NX, CY), 1.0, 6.0, ((0, 2), (1, 4), (2, 2)), jnp.float32),
        "induction_lateral_component": bell_draw(own_keys[3], (2, NZ, NX, CY), 1.0, 6.0, ((0, 2), (1, 4), (2, 2)), jnp.float32),
        "induction_vertical_component": bell_draw(own_keys[4], (2, NZ, NX, CY), 1.0, 6.0, ((0, 2), (1, 4), (2, 2)), jnp.float32),
        "induction_forward_component": bell_draw(own_keys[5], (2, NZ, NX, CY), 1.0, 6.0, ((0, 2), (1, 4), (2, 2)), jnp.float32),
        "medium_code": plant(jax.random.randint(own_keys[6], (NZ, NX, CY), 0, 3), jax.random.fold_in(own_keys[6], 1), 0, 2).astype(jnp.int32),
        "nonlinear_coefficient_matrix": jnp.clip(jnp.exp(jax.random.uniform(key_of[7], (2, 3), jnp.float32, math.log(0.3), math.log(3.0))), 0.3, 3.0),
        "mobile_charge_density": jnp.clip(0.5 + 1.5 * jax.random.uniform(own_keys[8], (DOPANT_SPAN_CELLS, DOPANT_CROSS), jnp.float32) ** block_scale(own_keys[8], (DOPANT_SPAN_CELLS, DOPANT_CROSS), ((0, 8),), -0.2, 0.2), 0.5, 2.0),
    }


COURANT = 0.5
SILICON_PERM = 12.1
OXIDE_PERM = 2.1
SPREAD_COEFF = 0.2
MOBILITY_TERM = 0.1
LIFETIME_DECAY = 0.05
SOURCE_FACTOR = 0.02


def next_cell(field, axis):
    size = field.shape[axis]
    inner = jax.lax.slice_in_dim(field, 1, size, axis=axis)
    edge = jnp.zeros_like(jax.lax.slice_in_dim(field, 0, 1, axis=axis))
    return jnp.concatenate([inner, edge], axis)


def prev_cell(field, axis):
    size = field.shape[axis]
    inner = jax.lax.slice_in_dim(field, 0, size - 1, axis=axis)
    edge = jnp.zeros_like(jax.lax.slice_in_dim(field, 0, 1, axis=axis))
    return jnp.concatenate([edge, inner], axis)


def evolve_charges(charge_density_step, blocky_pair_creation):
    for upsample_copy in range(CSTEPS):
        bordered_array = jnp.pad(charge_density_step, 1)
        upward_neighbor = bordered_array[2:, 1:-1]
        downward_neighbor = bordered_array[:-2, 1:-1]
        second_derivative_sum = upward_neighbor + downward_neighbor + bordered_array[1:-1, 2:] + bordered_array[1:-1, :-2] - 4.0 * charge_density_step
        charge_density_step = charge_density_step + SPREAD_COEFF * second_derivative_sum - MOBILITY_TERM * (charge_density_step - downward_neighbor) - LIFETIME_DECAY * charge_density_step + SOURCE_FACTOR * blocky_pair_creation
    return charge_density_step


def reference(voltage_lateral_component, voltage_vertical_component, voltage_forward_component, induction_lateral_component, induction_vertical_component, induction_forward_component, medium_code, nonlinear_coefficient_matrix, mobile_charge_density):
    silicon = (medium_code == 0).astype(jnp.float32)
    base_perm = jnp.where(medium_code == 0, SILICON_PERM, jnp.where(medium_code == 1, OXIDE_PERM, 1.0)).astype(jnp.float32)
    kerr_gain = nonlinear_coefficient_matrix[:, 0][:, None, None, None]
    absorb_two = nonlinear_coefficient_matrix[:, 1][:, None, None, None]
    absorb_free = nonlinear_coefficient_matrix[:, 2][:, None, None, None]
    forward_voltage_x, lateral_voltage_y, vertical_voltage_z = voltage_lateral_component, voltage_vertical_component, voltage_forward_component
    induction_forward_x, induction_lateral_y, induction_vertical_z = induction_lateral_component, induction_vertical_component, induction_forward_component
    charge_density_step = mobile_charge_density
    for rounds in range(ROUNDS):
        optical_grid_charge = jnp.repeat(jnp.repeat(charge_density_step, BLOCK_FACTOR, 0), BLOCK_FACTOR, 1)[:, :, None]
        generation = jnp.zeros(medium_code.shape, jnp.float32)
        for upsample_copy in range(SUBSTEPS):
            intensity = forward_voltage_x * forward_voltage_x + lateral_voltage_y * lateral_voltage_y + vertical_voltage_z * vertical_voltage_z
            inten_sum = intensity[0] + intensity[1]
            generation = generation + silicon * jnp.sum(absorb_two * intensity, 0) * inten_sum
            induction_forward_x = induction_forward_x - COURANT * ((next_cell(vertical_voltage_z, 3) - vertical_voltage_z) - (next_cell(lateral_voltage_y, 1) - lateral_voltage_y))
            induction_lateral_y = induction_lateral_y - COURANT * ((next_cell(forward_voltage_x, 1) - forward_voltage_x) - (next_cell(vertical_voltage_z, 2) - vertical_voltage_z))
            induction_vertical_z = induction_vertical_z - COURANT * ((next_cell(lateral_voltage_y, 2) - lateral_voltage_y) - (next_cell(forward_voltage_x, 3) - forward_voltage_x))
            curl_x = (induction_vertical_z - prev_cell(induction_vertical_z, 3)) - (induction_lateral_y - prev_cell(induction_lateral_y, 1))
            curl_y = (induction_forward_x - prev_cell(induction_forward_x, 1)) - (induction_vertical_z - prev_cell(induction_vertical_z, 2))
            curl_z = (induction_lateral_y - prev_cell(induction_lateral_y, 2)) - (induction_forward_x - prev_cell(induction_forward_x, 3))
            permit = base_perm + silicon * kerr_gain * inten_sum
            losses = silicon * (absorb_two * inten_sum + absorb_free * optical_grid_charge)
            keeping = permit - 0.5 * losses
            divisor = permit + 0.5 * losses
            forward_voltage_x = (keeping * forward_voltage_x + COURANT * curl_x) / divisor
            lateral_voltage_y = (keeping * lateral_voltage_y + COURANT * curl_y) / divisor
            vertical_voltage_z = (keeping * vertical_voltage_z + COURANT * curl_z) / divisor
        rows = generation.shape[0] // BLOCK_FACTOR
        cols = generation.shape[1] // BLOCK_FACTOR
        blocky_pair_creation = generation.reshape(rows, BLOCK_FACTOR, cols, BLOCK_FACTOR, generation.shape[2]).mean(axis=(1, 3, 4))
        charge_density_step = evolve_charges(charge_density_step, blocky_pair_creation)
    return forward_voltage_x, lateral_voltage_y, vertical_voltage_z, induction_forward_x, induction_lateral_y, induction_vertical_z, charge_density_step
```

```python
import functools

import jax
import jax.numpy as jnp
from jax import lax
from jax.experimental import pallas as pl
from jax.experimental.pallas import tpu as pltpu
from jax.sharding import PartitionSpec as P

BLOCK_FACTOR = 4
SUBSTEPS = 4
ROUNDS = 2
CSTEPS = 8

COURANT = 0.5
SILICON_PERM = 12.1
OXIDE_PERM = 2.1
SPREAD_COEFF = 0.2
MOBILITY_TERM = 0.1
LIFETIME_DECAY = 0.05
SOURCE_FACTOR = 0.02

DEEP = SUBSTEPS
LINE = ("gz", "gx", "af")
HBM = pl.BlockSpec(memory_space=pltpu.HBM)
SMEM = pl.BlockSpec(memory_space=pltpu.SMEM)
VMEM_LIMIT = 32 * 1024 * 1024
F32 = jnp.float32


class Plan:
    def __init__(self, planes, cols, lanes, slab):
        self.gz = lax.axis_size("gz")
        self.gx = lax.axis_size("gx")
        self.planes, self.cols, self.lanes, self.slab = planes, cols, lanes, slab
        self.own = planes // 2
        self.part = self.own + DEEP
        self.ext = self.own + 2 * DEEP
        self.paired = self.gx == 2
        self.sides = ("face",) if self.paired else ("low", "high")
        self.width = cols + (8 if self.paired else 16)
        self.rows = self.width + 8
        self.tiles = self.width // 8
        self.grid_rows = planes * self.gz // BLOCK_FACTOR
        self.grid_cols = cols * self.gx // BLOCK_FACTOR
        self.devices = self.gz * self.gx * 2

    def first_row(self):
        return 8 * lax.axis_index("gx") if self.paired else 8

    def own_rows(self):
        return pl.ds(pl.multiple_of(self.first_row(), 8), self.cols)


def each_side(plan, act):
    if plan.paired:
        across = lax.axis_index("gx")

        @pl.when(across == 0)
        def _():
            act(0, "high")

        @pl.when(across == 1)
        def _():
            act(0, "low")
    else:
        act(0, "low")
        act(1, "high")


def line_pairs(plan, target):
    pairs = []
    for z in range(plan.gz):
        for x in range(plan.gx):
            for k in range(2):
                tz, tx, tk = target(z, x, k)
                if 0 <= tz < plan.gz and 0 <= tx < plan.gx:
                    pairs.append(((z * plan.gx + x) * 2 + k, (tz * plan.gx + tx) * 2 + tk))
    return pairs


def across_step(side, x):
    if side == "face":
        return 1 - x
    return x + 1 if side == "low" else x - 1


class Copies:
    def __init__(self, sems):
        self.sems, self.made = sems, 0

    def start(self, source, target):
        copy = pltpu.make_async_copy(source, target, self.sems.at[self.made])
        self.made += 1
        copy.start()
        return copy


def wait(copies):
    for copy in copies:
        copy.wait()


def call(plan, body, name, shapes, in_specs, scratch, copies, flops=0, moved=0, aliases=None):
    return pl.pallas_call(
        functools.partial(body, plan),
        out_shape=[jax.ShapeDtypeStruct(s, F32) for s in shapes],
        in_specs=in_specs,
        out_specs=[HBM] * len(shapes),
        scratch_shapes=scratch + [pltpu.SemaphoreType.DMA((copies,))],
        input_output_aliases=aliases or {},
        compiler_params=pltpu.CompilerParams(vmem_limit_bytes=VMEM_LIMIT),
        cost_estimate=pl.CostEstimate(flops=flops, bytes_accessed=moved, transcendentals=0),
        name=name,
    )


def pack_kernel(plan, *refs):
    raw, medium = refs[:6], refs[6]
    z_same, z_cross = refs[7:9]
    nside = len(plan.sides)
    outs = refs[9 : 9 + 4 * nside]
    edge, edge_code, face_code, face_float, strips, sems = refs[9 + 4 * nside :]
    copies = Copies(sems)
    k = lax.axis_index("af")
    last = plan.planes - DEEP
    to_same = jnp.where(k == 0, last, 0)
    to_cross = jnp.where(k == 0, 0, last)
    if plan.paired:
        tile_rows = [pl.multiple_of((plan.cols - 8) * (1 - lax.axis_index("gx")), 8)]
    else:
        tile_rows = [plan.cols - 8, 0]
    fast, slow = [], []
    for n, row in enumerate(tile_rows):
        for c in range(6):
            fast.append(copies.start(raw[c].at[0, :, pl.ds(row, 8), :], edge.at[n, c]))
        fast.append(copies.start(medium.at[:, pl.ds(row, 8), :], edge_code.at[n]))
    fast.append(copies.start(medium.at[pl.ds(to_same, DEEP)], face_code))
    for c in range(6):
        slow.append(copies.start(raw[c].at[0, pl.ds(to_same, DEEP)], z_same.at[c]))
        slow.append(copies.start(raw[c].at[0, pl.ds(to_cross, DEEP)], z_cross.at[c]))
    wait(fast)
    face_float[...] = face_code[...].astype(F32)
    slow.append(copies.start(face_float, z_same.at[6]))

    def fill(slot, low):
        def rows(q, _):
            for h in range(2):
                half = slice(4 * h, 4 * h + 4)
                for c in range(6):
                    strips[slot, c, q, half, :] = edge[slot, c, 2 * q + h, low : low + 4, :]
                code = edge_code[slot, 2 * q + h, low : low + 4, :]
                strips[slot, 6, q, half, :] = code.astype(F32)
            return 0

        lax.fori_loop(0, plan.planes // 2, rows, 0)

    each_side(plan, lambda slot, side: fill(slot, 4 if plan.paired == (side == "high") else 0))
    quarter = (plan.own - DEEP) // 2
    for n in range(nside):
        x_same, x_cross, d_same, d_cross = outs[4 * n : 4 * n + 4]
        pairs, six = plan.part // 2, pl.ds(0, 6)
        for source, target in (
            (strips.at[n, :, pl.ds(quarter * k, pairs)], x_same),
            (strips.at[n, six, pl.ds(quarter * (1 - k), pairs)], x_cross),
            (strips.at[n, :, pl.ds(to_same // 2, DEEP // 2)], d_same),
            (strips.at[n, six, pl.ds(to_cross // 2, DEEP // 2)], d_cross),
        ):
            slow.append(copies.start(source, target))
    wait(slow)


def pack(plan, raw, medium):
    wide = (plan.cols, plan.lanes)
    nside = len(plan.sides)
    shapes = [(7, DEEP) + wide, (6, DEEP) + wide]
    for _ in plan.sides:
        for comps, rows in ((7, plan.part), (6, plan.part), (7, DEEP), (6, DEEP)):
            shapes.append((comps, rows // 2, 8, plan.lanes))
    scratch = [
        pltpu.VMEM((nside, 6, plan.planes, 8, plan.lanes), F32),
        pltpu.VMEM((nside, plan.planes, 8, plan.lanes), jnp.int32),
        pltpu.VMEM((DEEP,) + wide, jnp.int32),
        pltpu.VMEM((DEEP,) + wide, F32),
        pltpu.VMEM((nside, 7, plan.planes // 2, 8, plan.lanes), F32),
    ]
    return call(
        plan, pack_kernel, "pack", shapes, [HBM] * 7, scratch, 11 * nside + 14, moved=4_000_000
    )(*raw, medium)


def clear(plan, old, new, code):
    zero = jnp.zeros((8, plan.lanes), F32)

    def halo(slot, side):
        tile = plan.tiles - 1 if side == "high" else 0

        def one(p, _):
            for ref in list(old) + code:
                ref[p, 8 * tile : 8 * tile + 8, :] = zero
            return 0

        lax.fori_loop(0, plan.ext, one, 0)

    each_side(plan, halo)

    def above(p, _):
        for c in (1, 2, 7, 8):
            for ref in (old[c], new[c]):
                ref[p, plan.width : plan.width + 8, :] = zero
        return 0

    lax.fori_loop(0, plan.ext, above, 0)
    for c, ref in enumerate(new):
        plane = DEEP + plan.own if c % 6 < 3 else DEEP - 1
        for t in range(plan.tiles):
            ref[plane, 8 * t : 8 * t + 8, :] = zero


def strip_row(plan, side):
    if side == "low":
        return 4
    return plan.cols if plan.paired else 8 + plan.cols


def spread_strip(refs, strip, at, plane, pairs):
    def one(q, _):
        for c, ref in refs:
            for h in range(2):
                ref[plane + 2 * q + h, at : at + 4, :] = strip[c, q, 4 * h : 4 * h + 4, :]
        return 0

    lax.fori_loop(0, pairs, one, 0)


def substeps(plan, first, second, base, silicon, charge, gen, coef):
    lanes = plan.lanes
    tile = (8, lanes)
    lane = lax.broadcasted_iota(jnp.int32, tile, 1)
    row = lax.broadcasted_iota(jnp.int32, tile, 0)
    keep_up, keep_down, at_top = lane < lanes - 1, lane > 0, row == 0
    z, x, k = (lax.axis_index(a) for a in LINE)
    at_low = jnp.logical_and(z == 0, k == 0)
    at_high = jnp.logical_and(z == plan.gz - 1, k == 1)

    def up(v):
        return jnp.where(keep_up, pltpu.roll(v, lanes - 1, 1), 0.0)

    def down(v):
        return jnp.where(keep_down, pltpu.roll(v, 1, 1), 0.0)

    def edge_mask(t):
        if plan.paired or t not in (0, plan.tiles - 1):
            return None
        off = (x == 0) if t == 0 else (x == plan.gx - 1)
        return jnp.where(off, 0.0, 1.0)

    kerr, half_two, half_free, two = [], [], [], []
    for s in range(2):
        which = k if s == 0 else 1 - k
        kerr.append(coef[which, 0])
        two.append(coef[which, 1])
        half_two.append(0.5 * coef[which, 1])
        half_free.append(0.5 * coef[which, 2])

    def new_magnetic(old, new, s, p, t):
        ex, ey, ez, hx, hy, hz = old[6 * s : 6 * s + 6]
        here, beside = slice(8 * t, 8 * t + 8), slice(8 * t + 1, 8 * t + 9)
        vx, vy, vz = ex[p, here, :], ey[p, here, :], ez[p, here, :]
        nx = hx[p, here, :] - COURANT * ((up(vz) - vz) - (ey[p + 1, here, :] - vy))
        ny = hy[p, here, :] - COURANT * ((ex[p + 1, here, :] - vx) - (ez[p, beside, :] - vz))
        nz = hz[p, here, :] - COURANT * ((ey[p, beside, :] - vy) - (up(vx) - vx))
        mask = edge_mask(t)
        if mask is not None:
            nx, ny, nz = nx * mask, ny * mask, nz * mask
        new[6 * s + 3][p, here, :] = nx
        new[6 * s + 4][p, here, :] = ny
        new[6 * s + 5][p, here, :] = nz
        return vx, vy, vz, nx, ny, nz

    def full_plane(old, new, p):
        coarse = p // BLOCK_FACTOR
        zero = jnp.zeros(tile, F32)
        rolled = [[zero, zero], [zero, zero]]
        for t in range(plan.tiles):
            here = slice(8 * t, 8 * t + 8)
            back = [[new[6 * s + c][p - 1, here, :] for c in (3, 4)] for s in range(2)]
            vals = [new_magnetic(old, new, s, p, t) for s in range(2)]
            strength = [v[0] * v[0] + v[1] * v[1] + v[2] * v[2] for v in vals]
            is_silicon = silicon[p, here, :]
            total = (strength[0] + strength[1]) * is_silicon
            carriers = charge[coarse, here, :] * is_silicon
            ground = base[p, here, :]
            gen[p, here, :] += (two[0] * strength[0] + two[1] * strength[1]) * total
            mask = edge_mask(t)
            for s in range(2):
                vx, vy, vz, nx, ny, nz = vals[s]
                loss = half_two[s] * total + half_free[s] * carriers
                perm = ground + kerr[s] * total
                divisor = perm + loss
                inv = pl.reciprocal(divisor, approx=True)
                inv = inv * (2.0 - divisor * inv)
                keep = (perm - loss) * inv
                push = COURANT * inv
                if mask is not None:
                    push = push * mask
                turn_y, turn_z = pltpu.roll(ny, 1, 0), pltpu.roll(nz, 1, 0)
                left_y = jnp.where(at_top, rolled[s][0], turn_y)
                left_z = jnp.where(at_top, rolled[s][1], turn_z)
                rolled[s] = [turn_y, turn_z]
                curl_x = (nz - down(nz)) - (ny - back[s][1])
                curl_y = (nx - back[s][0]) - (nz - left_z)
                curl_z = (ny - left_y) - (nx - down(nx))
                new[6 * s][p, here, :] = keep * vx + push * curl_x
                new[6 * s + 1][p, here, :] = keep * vy + push * curl_y
                new[6 * s + 2][p, here, :] = keep * vz + push * curl_z

    def substep(old, new, n):
        @pl.when(jnp.logical_not(at_low))
        def _():
            for t in range(plan.tiles):
                for s in range(2):
                    new_magnetic(old, new, s, n, t)

        begin = jnp.where(at_low, DEEP, n + 1)
        end = jnp.where(at_high, DEEP + plan.own, plan.ext - 1 - n)

        def step(p, _):
            full_plane(old, new, p)
            return 0

        lax.fori_loop(begin, end, step, 0)

    def pair(m, _):
        substep(first, second, 2 * m)
        substep(second, first, 2 * m + 1)
        return 0

    lax.fori_loop(0, SUBSTEPS // 2, pair, 0)


def set_media(plan, code, base, silicon):
    def one(p, _):
        for t in range(plan.tiles):
            here = slice(8 * t, 8 * t + 8)
            v = code[p, here, :]
            base[p, here, :] = jnp.where(v == 0.0, SILICON_PERM, jnp.where(v == 1.0, OXIDE_PERM, 1.0))
            silicon[p, here, :] = jnp.where(v == 0.0, 1.0, 0.0)
        return 0

    lax.fori_loop(0, plan.ext, one, 0)


def clear_generation(plan, gen):
    def one(p, _):
        gen[p] = jnp.zeros((plan.rows, plan.lanes), F32)
        return 0

    lax.fori_loop(DEEP, DEEP + plan.own, one, 0)


def sum_generation(plan, gen, message):
    blocks = plan.cols // BLOCK_FACTOR
    lane = lax.broadcasted_iota(jnp.int32, (blocks, plan.lanes), 1)
    across = plan.own_rows()
    out = jnp.zeros((blocks, plan.lanes), F32)
    for a in range(plan.own // BLOCK_FACTOR):
        p = DEEP + BLOCK_FACTOR * a
        rows = (gen[p, across, :] + gen[p + 1, across, :]) + (
            gen[p + 2, across, :] + gen[p + 3, across, :]
        )
        cells = rows.reshape(blocks, BLOCK_FACTOR, plan.lanes).sum(1)
        mean = cells.sum(1, keepdims=True) * (1.0 / (BLOCK_FACTOR * BLOCK_FACTOR * plan.lanes))
        out = jnp.where(lane == a, mean, out)
    message[...] = out


def round_scratch(plan):
    wide = (plan.ext, plan.rows, plan.lanes)
    return [pltpu.VMEM(wide, F32)] * 27 + [
        pltpu.VMEM((plan.ext // BLOCK_FACTOR, plan.width, plan.lanes), F32),
        pltpu.VMEM((plan.cols // BLOCK_FACTOR, plan.lanes), F32),
    ]


def round_flops(plan):
    return SUBSTEPS * plan.ext * plan.width * plan.lanes * 150


def generation_shape(plan):
    return (plan.devices, plan.cols // BLOCK_FACTOR, plan.lanes)


def first_kernel(plan, *refs):
    nside = len(plan.sides)
    coef, density = refs[:2]
    raw, medium, swap, z_same, z_cross = refs[2:8], refs[8], refs[9:15], refs[15], refs[16]
    strips_in = refs[17 : 17 + 4 * nside]
    outs = refs[17 + 4 * nside : 22 + 7 * nside]
    own_out, z_out, core_out, gen_out, code_out = outs[:5]
    strip_out = outs[5:]
    rest = refs[22 + 7 * nside :]
    old, new, (base, silicon, gen, charge, message) = rest[:12], rest[12:24], rest[24:29]
    code, codes = rest[29:31]
    strips, strip_mine, sems = rest[31 : 31 + 4 * nside], rest[31 + 4 * nside : -1], rest[-1]
    copies = Copies(sems)
    z, x, k = (lax.axis_index(a) for a in LINE)
    near = DEEP * (1 - k)
    far = plan.part * k
    begin = (plan.own - DEEP) * k
    across = plan.own_rows()
    here, there = pl.ds(near, plan.part), pl.ds(far, DEEP)
    mine = pl.ds(begin, plan.part)
    early = [copies.start(medium.at[mine], codes)]
    early.append(copies.start(z_same.at[6], code.at[there, across]))
    for source, target in zip(strips_in, strips):
        early.append(copies.start(source, target))
    late = []
    for c in range(6):
        late.append(copies.start(raw[c].at[0, mine], old[c].at[here, across]))
        late.append(copies.start(swap[c].at[0, mine], old[6 + c].at[here, across]))
        late.append(copies.start(z_same.at[c], old[c].at[there, across]))
        late.append(copies.start(z_cross.at[c], old[6 + c].at[there, across]))
    clear(plan, old, new, [code])
    clear_generation(plan, gen)
    for a in range(plan.ext // BLOCK_FACTOR):
        top = (plan.planes * z + plan.own * k - DEEP) // BLOCK_FACTOR + a
        top = jnp.clip(top, 0, plan.grid_rows - 1)
        for c in range(plan.width // BLOCK_FACTOR):
            left = (plan.cols * x - plan.first_row()) // BLOCK_FACTOR + c
            left = jnp.clip(left, 0, plan.grid_cols - 1)
            value = density[top // plan.slab, top % plan.slab, left]
            charge[a, 4 * c : 4 * c + 4, :] = jnp.full((4, plan.lanes), value)
    wait(early)

    def settle(p, _):
        code[near + p, across, :] = codes[p].astype(F32)
        return 0

    lax.fori_loop(0, plan.part, settle, 0)

    def place(slot, side):
        x_same, x_cross, d_same, d_cross = strips[4 * slot : 4 * slot + 4]
        at = strip_row(plan, side)
        same = list(enumerate(list(old[:6]) + [code]))
        cross = list(enumerate(old[6:]))
        spread_strip(same, x_same, at, near, plan.part // 2)
        spread_strip(cross, x_cross, at, near, plan.part // 2)
        spread_strip(same, d_same, at, far, DEEP // 2)
        spread_strip(cross, d_cross, at, far, DEEP // 2)

    each_side(plan, place)
    set_media(plan, code, base, silicon)
    wait(late)
    substeps(plan, old, new, base, silicon, charge, gen, coef)
    toward = DEEP + (plan.own - DEEP) * k
    inward = DEEP + (plan.own - DEEP) * (1 - k)
    copies = Copies(sems)
    late = []
    for c in range(12):
        late.append(copies.start(old[c].at[pl.ds(toward, DEEP), across], z_out.at[c]))
        late.append(copies.start(old[c].at[pl.ds(inward, DEEP), across], core_out.at[c]))
        late.append(copies.start(old[c].at[pl.ds(DEEP, plan.own), across], own_out.at[c]))
    late.append(copies.start(code, code_out))

    def gather(slot, side):
        high_end = (side == "high") if plan.paired else (side == "low")
        low = 0 if plan.paired and side == "high" else 8
        at = low + plan.cols - 4 if high_end else low

        def one(q, _):
            for c in range(12):
                for h in range(2):
                    strip_mine[slot][c, q, 4 * h : 4 * h + 4, :] = old[c][
                        DEEP + 2 * q + h, at : at + 4, :
                    ]
            return 0

        lax.fori_loop(0, plan.own // 2, one, 0)

    each_side(plan, gather)
    half, top = DEEP // 2, (plan.own - DEEP) // 2
    for n in range(nside):
        whole, inner, corner = strip_out[3 * n : 3 * n + 3]
        late.append(copies.start(strip_mine[n], whole))
        late.append(copies.start(strip_mine[n].at[:, pl.ds(top * (1 - k), half)], inner))
        late.append(copies.start(strip_mine[n].at[:, pl.ds(top * k, half)], corner))
    sum_generation(plan, gen, message)
    for d in range(plan.devices):
        late.append(copies.start(message, gen_out.at[d]))
    wait(late)


def first_round(plan, coef, density, raw, medium, swap, z_same, z_cross, strips):
    wide = (plan.cols, plan.lanes)
    nside = len(plan.sides)
    shapes = [
        (12, plan.own) + wide,
        (12, DEEP) + wide,
        (12, DEEP) + wide,
        generation_shape(plan),
        (plan.ext, plan.rows, plan.lanes),
    ]
    for _ in plan.sides:
        for rows in (plan.own, DEEP, DEEP):
            shapes.append((12, rows // 2, 8, plan.lanes))
    scratch = round_scratch(plan) + [
        pltpu.VMEM((plan.ext, plan.rows, plan.lanes), F32),
        pltpu.VMEM((plan.part,) + wide, jnp.int32),
    ]
    scratch += [pltpu.VMEM(s.shape, F32) for s in strips]
    scratch += [pltpu.VMEM((12, plan.own // 2, 8, plan.lanes), F32)] * nside
    return call(
        plan,
        first_kernel,
        "first_round",
        shapes,
        [SMEM, SMEM] + [HBM] * (15 + 4 * nside),
        scratch,
        37 + 3 * nside + plan.devices,
        round_flops(plan),
        10_000_000,
    )(coef, density, *raw, medium, *swap, z_same, z_cross, *strips)


def second_kernel(plan, *refs):
    nside = len(plan.sides)
    coef, charge_in, code_in, own_in, z_in, core_in = refs[:6]
    strips_in = refs[6 : 6 + 3 * nside]
    outs = refs[6 + 3 * nside : 14 + 3 * nside]
    kept, sent, gen_out = outs[:6], outs[6], outs[7]
    rest = refs[14 + 3 * nside :]
    old, new, (base, silicon, gen, charge, message) = rest[:12], rest[12:24], rest[24:29]
    code, strips, sems = rest[29], rest[30:-1], rest[-1]
    copies = Copies(sems)
    k = lax.axis_index("af")
    across = plan.own_rows()
    outward = plan.part * k
    inner = plan.part * (1 - k)
    early = [copies.start(code_in, code), copies.start(charge_in, charge)]
    for source, target in zip(strips_in, strips):
        early.append(copies.start(source, target))
    late = []
    for c in range(12):
        flip = (c + 6) % 12
        late.append(copies.start(own_in.at[c], old[c].at[pl.ds(DEEP, plan.own), across]))
        late.append(copies.start(z_in.at[flip], old[c].at[pl.ds(outward, DEEP), across]))
        late.append(copies.start(core_in.at[flip], old[c].at[pl.ds(inner, DEEP), across]))
    clear(plan, old, new, [])
    clear_generation(plan, gen)
    wait(early)

    def place(slot, side):
        x_same, x_cross, diag = strips[3 * slot : 3 * slot + 3]
        at = strip_row(plan, side)
        same = list(enumerate(old))
        flipped = list(enumerate(list(old[6:]) + list(old[:6])))
        spread_strip(same, x_same, at, DEEP, plan.own // 2)
        spread_strip(flipped, x_cross, at, inner, DEEP // 2)
        spread_strip(flipped, diag, at, outward, DEEP // 2)

    each_side(plan, place)
    set_media(plan, code, base, silicon)
    wait(late)
    substeps(plan, old, new, base, silicon, charge, gen, coef)
    copies = Copies(sems)
    late = []
    for c in range(6):
        late.append(copies.start(old[6 + c].at[pl.ds(DEEP, plan.own), across], sent.at[c]))
    sum_generation(plan, gen, message)
    for d in range(plan.devices):
        late.append(copies.start(message, gen_out.at[d]))
    for c in range(6):
        target = kept[c].at[0, pl.ds(plan.own * k, plan.own)]
        late.append(copies.start(old[c].at[pl.ds(DEEP, plan.own), across], target))
    wait(late)


def second_round(plan, coef, charge, code, own_in, z_in, core_in, strips):
    wide = (plan.cols, plan.lanes)
    nside = len(plan.sides)
    shapes = [(1, plan.planes) + wide] * 6 + [(6, plan.own) + wide, generation_shape(plan)]
    scratch = round_scratch(plan) + [pltpu.VMEM((plan.ext, plan.rows, plan.lanes), F32)]
    scratch += [pltpu.VMEM(s.shape, F32) for s in strips]
    return call(
        plan,
        second_kernel,
        "second_round",
        shapes,
        [SMEM] + [HBM] * (5 + 3 * nside),
        scratch,
        max(38 + 3 * nside, 12 + plan.devices),
        round_flops(plan),
        10_000_000,
    )(coef, charge, code, own_in, z_in, core_in, *strips)


def join_kernel(plan, *refs):
    got, outs, sems = refs[6], refs[7:13], refs[13]
    copies = Copies(sems)
    k = lax.axis_index("af")
    rows = pl.ds(plan.own * (1 - k), plan.own)
    wait([copies.start(got.at[c], outs[c].at[0, rows]) for c in range(6)])


def join(plan, halves, got):
    shapes = [h.shape for h in halves]
    aliases = {c: c for c in range(6)}
    return call(
        plan, join_kernel, "join", shapes, [HBM] * 7, [], 6, moved=3_000_000, aliases=aliases
    )(*halves, got)


def carrier_kernel(plan, last, *refs):
    density_in, gens_in = refs[:2]
    outs = refs[2:3] if last else refs[2:4]
    gens, one, two, source, charge, sems = refs[2 + len(outs) :]
    copies = Copies(sems)
    rows, cols, lanes = plan.grid_rows, plan.grid_cols, plan.lanes
    z, x, k = (lax.axis_index(a) for a in LINE)
    blocks, own = plan.cols // BLOCK_FACTOR, plan.own // BLOCK_FACTOR
    early = [copies.start(gens_in, gens)]
    if last:
        early.append(copies.start(density_in, one.at[pl.ds(1, rows), pl.ds(8, cols)]))
    zero = jnp.zeros((8, lanes), F32)

    def clean(i, _):
        for ref in (one, two):
            ref[i, 0:8, :] = zero
            ref[i, 8 + cols : 16 + cols, :] = zero
        return 0

    lax.fori_loop(0, rows + 2, clean, 0)
    for ref in (one, two):
        for i in (0, rows + 1):
            for c in range(8, 8 + cols, 8):
                ref[i, c : c + 8, :] = zero
    if not last:

        def read(i, _):
            for c in range(cols):
                value = density_in[i // plan.slab, i % plan.slab, c]
                one[i + 1, 8 + c : 9 + c, :] = jnp.full((1, lanes), value)
            return 0

        lax.fori_loop(0, rows, read, 0)
    wait(early)

    def unpack(line, _):
        for dx in range(plan.gx):
            for dk in range(2):
                tile = gens[(line * plan.gx + dx) * 2 + dk]
                for a in range(own):
                    source[(line * 2 + dk) * own + a, blocks * dx : blocks * dx + blocks, :] = (
                        jnp.broadcast_to(tile[:, a : a + 1], (blocks, lanes))
                    )
        return 0

    lax.fori_loop(0, plan.gz, unpack, 0)

    def step(old, new):
        def row(i, _):
            for c in range(8, 8 + cols, 8):
                now, before = old[i + 1, c : c + 8, :], old[i, c : c + 8, :]
                around = (
                    old[i + 2, c : c + 8, :]
                    + before
                    + old[i + 1, c + 1 : c + 9, :]
                    + old[i + 1, c - 1 : c + 7, :]
                    - 4.0 * now
                )
                new[i + 1, c : c + 8, :] = (
                    now
                    + SPREAD_COEFF * around
                    - MOBILITY_TERM * (now - before)
                    - LIFETIME_DECAY * now
                    + SOURCE_FACTOR * source[i, c - 8 : c, :]
                )
            return 0

        lax.fori_loop(0, rows, row, 0, unroll=4)

    def pair(_, carry):
        step(one, two)
        step(two, one)
        return carry

    lax.fori_loop(0, CSTEPS // 2, pair, 0)
    if last:
        rows_out = pl.ds(1 + (z * plan.gx + x) * plan.slab, plan.slab)
        wait([copies.start(one.at[rows_out, pl.ds(8, cols)], outs[0])])
        return
    late = [copies.start(one.at[pl.ds(1, rows), pl.ds(8, cols)], outs[0])]
    for a in range(plan.ext // BLOCK_FACTOR):
        top = (plan.planes * z + plan.own * k - DEEP) // BLOCK_FACTOR + a
        top = 1 + jnp.clip(top, 0, rows - 1)
        for c in range(plan.width // BLOCK_FACTOR):
            left = (plan.cols * x - plan.first_row()) // BLOCK_FACTOR + c
            left = 8 + jnp.clip(left, 0, cols - 1)
            value = one[top, pl.ds(left, 1), :]
            charge[a, 4 * c : 4 * c + 4, :] = jnp.broadcast_to(value, (4, lanes))
    late.append(copies.start(charge, outs[1]))
    wait(late)


def carriers(plan, last, density, gens):
    rows, cols, lanes = plan.grid_rows, plan.grid_cols, plan.lanes
    charge = (plan.ext // BLOCK_FACTOR, plan.width, lanes)
    shapes = [(plan.slab, cols, lanes)] if last else [(rows, cols, lanes), charge]
    scratch = [
        pltpu.VMEM(gens.shape, F32),
        pltpu.VMEM((rows + 2, cols + 16, lanes), F32),
        pltpu.VMEM((rows + 2, cols + 16, lanes), F32),
        pltpu.VMEM((rows, cols, lanes), F32),
        pltpu.VMEM(charge, F32),
    ]
    return call(
        plan,
        lambda plan, *refs: carrier_kernel(plan, last, *refs),
        "carriers",
        shapes,
        [HBM if last else SMEM, HBM],
        scratch,
        4,
        2_000_000,
        1_000_000,
    )(density, gens)


def local(ex, ey, ez, hx, hy, hz, medium, coef, density):
    raw = (ex, ey, ez, hx, hy, hz)
    plan = Plan(*medium.shape, density.shape[0])

    def send(message, target):
        return lax.ppermute(message, LINE, line_pairs(plan, target))

    def spread(message, axes):
        return lax.all_to_all(message, axes, split_axis=0, concat_axis=0, tiled=True)

    toward = lambda z, goal: z + 1 if goal == 0 else z - 1
    core = lambda z, x, k: (z, x, 1 - k)

    packed = pack(plan, raw, medium)
    z_same, z_cross = packed[:2]
    strips = []
    for n, side in enumerate(plan.sides):
        to = functools.partial(across_step, side)
        x_same, x_cross, d_same, d_cross = packed[2 + 4 * n : 6 + 4 * n]
        strips.append(send(x_same, lambda z, x, k: (z, to(x), k)))
        strips.append(send(x_cross, lambda z, x, k: (z, to(x), 1 - k)))
        strips.append(send(d_same, lambda z, x, k: (toward(z, k), to(x), k)))
        strips.append(send(d_cross, lambda z, x, k: (toward(z, 1 - k), to(x), 1 - k)))
    z_same = send(z_same, lambda z, x, k: (toward(z, k), x, k))
    z_cross = send(z_cross, lambda z, x, k: (toward(z, 1 - k), x, 1 - k))
    swap = [send(r, core) for r in raw]
    tiles = plan.gz * plan.gx
    density = spread(jnp.broadcast_to(density, (tiles,) + density.shape), ("gz", "gx"))
    outs = first_round(plan, coef, density, raw, medium, swap, z_same, z_cross, strips)
    own, z_msg, core_msg, gens, code = outs[:5]
    gens = spread(gens, LINE)
    strips = []
    for n, side in enumerate(plan.sides):
        to = functools.partial(across_step, side)
        whole, inner, corner = outs[5 + 3 * n : 8 + 3 * n]
        strips.append(send(whole, lambda z, x, k: (z, to(x), k)))
        strips.append(send(inner, lambda z, x, k: (z, to(x), 1 - k)))
        strips.append(send(corner, lambda z, x, k: (toward(z, 1 - k), to(x), 1 - k)))
    z_msg = send(z_msg, lambda z, x, k: (toward(z, 1 - k), x, 1 - k))
    core_msg = send(core_msg, core)
    density, charge = carriers(plan, False, density, gens)
    outs = second_round(plan, coef, charge, code, own, z_msg, core_msg, strips)
    halves, sent, gens = outs[:6], outs[6], outs[7]
    gens = spread(gens, LINE)
    got = send(sent, core)
    (slab,) = carriers(plan, True, density, gens)
    return tuple(join(plan, halves, got)) + (slab[:, :, 0],)


def solution(mesh):
    field = P("af", ("group", "gz"), "gx", None)
    slabs = P(("group", "gz", "gx"), None)
    in_specs = (field,) * 6 + (P(("group", "gz"), "gx", None), P(), slabs)
    out_specs = (field,) * 6 + (slabs,)
    return jax.shard_map(local, mesh=mesh, in_specs=in_specs, out_specs=out_specs, check_vma=False)
```

```python
import functools

import jax
import jax.numpy as jnp
from jax import lax
from jax.experimental import pallas as pl
from jax.experimental.pallas import tpu as pltpu
from jax.sharding import PartitionSpec as P

BLOCK_FACTOR = 4
SUBSTEPS = 4
ROUNDS = 2
CSTEPS = 8

COURANT = 0.5
SILICON_PERM = 12.1
OXIDE_PERM = 2.1
SPREAD_COEFF = 0.2
MOBILITY_TERM = 0.1
LIFETIME_DECAY = 0.05
SOURCE_FACTOR = 0.02

DEEP = SUBSTEPS
LINE = ("gz", "gx", "af")
HBM = pl.BlockSpec(memory_space=pltpu.HBM)
SMEM = pl.BlockSpec(memory_space=pltpu.SMEM)
VMEM_LIMIT = 32 * 1024 * 1024
PACK_LIMIT = 60 * 1024 * 1024
F32 = jnp.float32


class Plan:
    def __init__(self, planes, cols, lanes, slab):
        self.gz = lax.axis_size("gz")
        self.gx = lax.axis_size("gx")
        self.planes, self.cols, self.lanes, self.slab = planes, cols, lanes, slab
        self.own = planes // 2
        self.part = self.own + DEEP
        self.ext = self.own + 2 * DEEP
        self.paired = self.gx == 2
        self.sides = ("face",) if self.paired else ("low", "high")
        self.width = cols + (8 if self.paired else 16)
        self.rows = self.width + 8
        self.tiles = self.width // 8
        self.grid_rows = planes * self.gz // BLOCK_FACTOR
        self.grid_cols = cols * self.gx // BLOCK_FACTOR
        self.devices = self.gz * self.gx * 2

    def first_row(self):
        return 8 * lax.axis_index("gx") if self.paired else 8

    def own_rows(self):
        return pl.ds(pl.multiple_of(self.first_row(), 8), self.cols)


def each_side(plan, act):
    if plan.paired:
        across = lax.axis_index("gx")

        @pl.when(across == 0)
        def _():
            act(0, "high")

        @pl.when(across == 1)
        def _():
            act(0, "low")
    else:
        act(0, "low")
        act(1, "high")


def line_pairs(plan, target):
    pairs = []
    for z in range(plan.gz):
        for x in range(plan.gx):
            for k in range(2):
                tz, tx, tk = target(z, x, k)
                if 0 <= tz < plan.gz and 0 <= tx < plan.gx:
                    pairs.append(((z * plan.gx + x) * 2 + k, (tz * plan.gx + tx) * 2 + tk))
    return pairs


def across_step(side, x):
    if side == "face":
        return 1 - x
    return x + 1 if side == "low" else x - 1


class Copies:
    def __init__(self, sems):
        self.sems, self.made = sems, 0

    def start(self, source, target):
        copy = pltpu.make_async_copy(source, target, self.sems.at[self.made])
        self.made += 1
        copy.start()
        return copy


def wait(copies):
    for copy in copies:
        copy.wait()


def call(plan, body, name, shapes, in_specs, scratch, copies, flops=0, moved=0, aliases=None, limit=VMEM_LIMIT):
    return pl.pallas_call(
        functools.partial(body, plan),
        out_shape=[jax.ShapeDtypeStruct(s, F32) for s in shapes],
        in_specs=in_specs,
        out_specs=[HBM] * len(shapes),
        scratch_shapes=scratch + [pltpu.SemaphoreType.DMA((copies,))],
        input_output_aliases=aliases or {},
        compiler_params=pltpu.CompilerParams(vmem_limit_bytes=limit),
        cost_estimate=pl.CostEstimate(flops=flops, bytes_accessed=moved, transcendentals=0),
        name=name,
    )


def pack_strips_kernel(plan, *refs):
    raw, medium = refs[:6], refs[6]
    nside = len(plan.sides)
    outs = refs[7 : 7 + 4 * nside]
    edge, edge_code, strips, sems = refs[7 + 4 * nside :]
    copies = Copies(sems)
    k = lax.axis_index("af")
    if plan.paired:
        tile_rows = [pl.multiple_of((plan.cols - 8) * (1 - lax.axis_index("gx")), 8)]
    else:
        tile_rows = [plan.cols - 8, 0]
    fast = []
    for n, row in enumerate(tile_rows):
        for c in range(6):
            fast.append(copies.start(raw[c].at[0, :, pl.ds(row, 8), :], edge.at[n, c]))
        fast.append(copies.start(medium.at[:, pl.ds(row, 8), :], edge_code.at[n]))
    wait(fast)

    def fill(slot, low):
        def rows(q, _):
            for h in range(2):
                half = slice(4 * h, 4 * h + 4)
                for c in range(6):
                    strips[slot, c, q, half, :] = edge[slot, c, 2 * q + h, low : low + 4, :]
                code = edge_code[slot, 2 * q + h, low : low + 4, :]
                strips[slot, 6, q, half, :] = code.astype(F32)
            return 0

        lax.fori_loop(0, plan.planes // 2, rows, 0)

    each_side(plan, lambda slot, side: fill(slot, 4 if plan.paired == (side == "high") else 0))
    quarter = (plan.own - DEEP) // 2
    last = plan.planes - DEEP
    to_same, to_cross = last * (1 - k), last * k
    late = []
    for n in range(nside):
        x_same, x_cross, d_same, d_cross = outs[4 * n : 4 * n + 4]
        pairs, six = plan.part // 2, pl.ds(0, 6)
        for source, target in (
            (strips.at[n, :, pl.ds(quarter * k, pairs)], x_same),
            (strips.at[n, six, pl.ds(quarter * (1 - k), pairs)], x_cross),
            (strips.at[n, :, pl.ds(to_same // 2, DEEP // 2)], d_same),
            (strips.at[n, six, pl.ds(to_cross // 2, DEEP // 2)], d_cross),
        ):
            late.append(copies.start(source, target))
    wait(late)


def pack_strips(plan, raw, medium):
    nside = len(plan.sides)
    shapes = []
    for _ in plan.sides:
        for comps, rows in ((7, plan.part), (6, plan.part), (7, DEEP), (6, DEEP)):
            shapes.append((comps, rows // 2, 8, plan.lanes))
    scratch = [
        pltpu.VMEM((nside, 6, plan.planes, 8, plan.lanes), F32),
        pltpu.VMEM((nside, plan.planes, 8, plan.lanes), jnp.int32),
        pltpu.VMEM((nside, 7, plan.planes // 2, 8, plan.lanes), F32),
    ]
    return call(
        plan,
        pack_strips_kernel,
        "pack_strips",
        shapes,
        [HBM] * 7,
        scratch,
        11 * nside,
        moved=1_000_000,
        limit=PACK_LIMIT,
    )(*raw, medium)


def pack_faces_kernel(plan, *refs):
    raw, medium = refs[:6], refs[6]
    z_same, z_cross, swap = refs[8:11]
    face_code, face_float, sems = refs[11:]
    copies = Copies(sems)
    k = lax.axis_index("af")
    last = plan.planes - DEEP
    to_same, to_cross = last * (1 - k), last * k
    early = copies.start(medium.at[pl.ds(to_same, DEEP)], face_code)
    late = []
    for c in range(6):
        late.append(copies.start(raw[c].at[0, pl.ds(to_same, DEEP)], z_same.at[c]))
        late.append(copies.start(raw[c].at[0, pl.ds(to_cross, DEEP)], z_cross.at[c]))
        part = pl.ds((plan.own - DEEP) * (1 - k), plan.part)
        late.append(copies.start(raw[c].at[0, part], swap.at[c]))
    early.wait()
    face_float[...] = face_code[...].astype(F32)
    late.append(copies.start(face_float, z_same.at[6]))
    wait(late)


def pack_faces(plan, raw, medium, after):
    wide = (plan.cols, plan.lanes)
    shapes = [(7, DEEP) + wide, (6, DEEP) + wide, (6, plan.part) + wide]
    scratch = [pltpu.VMEM((DEEP,) + wide, jnp.int32), pltpu.VMEM((DEEP,) + wide, F32)]
    return call(
        plan,
        pack_faces_kernel,
        "pack_faces",
        shapes,
        [HBM] * 8,
        scratch,
        20,
        moved=4_000_000,
        limit=PACK_LIMIT,
    )(*raw, medium, after)


def clear(plan, old, new, code):
    zero = jnp.zeros((8, plan.lanes), F32)

    def halo(slot, side):
        tile = plan.tiles - 1 if side == "high" else 0

        def one(p, _):
            for ref in list(old) + code:
                ref[p, 8 * tile : 8 * tile + 8, :] = zero
            return 0

        lax.fori_loop(0, plan.ext, one, 0)

    each_side(plan, halo)

    def above(p, _):
        for c in (1, 2, 7, 8):
            for ref in (old[c], new[c]):
                ref[p, plan.width : plan.width + 8, :] = zero
        return 0

    lax.fori_loop(0, plan.ext, above, 0)
    for c, ref in enumerate(new):
        plane = DEEP + plan.own if c % 6 < 3 else DEEP - 1
        for t in range(plan.tiles):
            ref[plane, 8 * t : 8 * t + 8, :] = zero


def strip_row(plan, side):
    if side == "low":
        return 4
    return plan.cols if plan.paired else 8 + plan.cols


def spread_strip(refs, strip, at, plane, pairs):
    def one(q, _):
        for c, ref in refs:
            for h in range(2):
                ref[plane + 2 * q + h, at : at + 4, :] = strip[c, q, 4 * h : 4 * h + 4, :]
        return 0

    lax.fori_loop(0, pairs, one, 0)


def substeps(plan, first, second, base, silicon, charge, gen, coef):
    lanes = plan.lanes
    tile = (8, lanes)
    lane = lax.broadcasted_iota(jnp.int32, tile, 1)
    row = lax.broadcasted_iota(jnp.int32, tile, 0)
    keep_up, keep_down, at_top = lane < lanes - 1, lane > 0, row == 0
    z, x, k = (lax.axis_index(a) for a in LINE)
    at_low = jnp.logical_and(z == 0, k == 0)
    at_high = jnp.logical_and(z == plan.gz - 1, k == 1)

    def up(v):
        return jnp.where(keep_up, pltpu.roll(v, lanes - 1, 1), 0.0)

    def down(v):
        return jnp.where(keep_down, pltpu.roll(v, 1, 1), 0.0)

    def edge_mask(t):
        if plan.paired or t not in (0, plan.tiles - 1):
            return None
        off = (x == 0) if t == 0 else (x == plan.gx - 1)
        return jnp.where(off, 0.0, 1.0)

    kerr, half_two, half_free, two = [], [], [], []
    for s in range(2):
        which = k if s == 0 else 1 - k
        kerr.append(coef[which, 0])
        two.append(coef[which, 1])
        half_two.append(0.5 * coef[which, 1])
        half_free.append(0.5 * coef[which, 2])

    def new_magnetic(old, new, s, p, t):
        ex, ey, ez, hx, hy, hz = old[6 * s : 6 * s + 6]
        here, beside = slice(8 * t, 8 * t + 8), slice(8 * t + 1, 8 * t + 9)
        vx, vy, vz = ex[p, here, :], ey[p, here, :], ez[p, here, :]
        nx = hx[p, here, :] - COURANT * ((up(vz) - vz) - (ey[p + 1, here, :] - vy))
        ny = hy[p, here, :] - COURANT * ((ex[p + 1, here, :] - vx) - (ez[p, beside, :] - vz))
        nz = hz[p, here, :] - COURANT * ((ey[p, beside, :] - vy) - (up(vx) - vx))
        mask = edge_mask(t)
        if mask is not None:
            nx, ny, nz = nx * mask, ny * mask, nz * mask
        new[6 * s + 3][p, here, :] = nx
        new[6 * s + 4][p, here, :] = ny
        new[6 * s + 5][p, here, :] = nz
        return vx, vy, vz, nx, ny, nz

    def full_plane(old, new, p):
        coarse = p // BLOCK_FACTOR
        zero = jnp.zeros(tile, F32)
        rolled = [[zero, zero], [zero, zero]]
        for t in range(plan.tiles):
            here = slice(8 * t, 8 * t + 8)
            back = [[new[6 * s + c][p - 1, here, :] for c in (3, 4)] for s in range(2)]
            vals = [new_magnetic(old, new, s, p, t) for s in range(2)]
            strength = [v[0] * v[0] + v[1] * v[1] + v[2] * v[2] for v in vals]
            is_silicon = silicon[p, here, :]
            total = (strength[0] + strength[1]) * is_silicon
            carriers = charge[coarse, here, :] * is_silicon
            ground = base[p, here, :]
            gen[p, here, :] += (two[0] * strength[0] + two[1] * strength[1]) * total
            mask = edge_mask(t)
            for s in range(2):
                vx, vy, vz, nx, ny, nz = vals[s]
                loss = half_two[s] * total + half_free[s] * carriers
                perm = ground + kerr[s] * total
                divisor = perm + loss
                inv = pl.reciprocal(divisor, approx=True)
                inv = inv * (2.0 - divisor * inv)
                keep = (perm - loss) * inv
                push = COURANT * inv
                if mask is not None:
                    push = push * mask
                turn_y, turn_z = pltpu.roll(ny, 1, 0), pltpu.roll(nz, 1, 0)
                left_y = jnp.where(at_top, rolled[s][0], turn_y)
                left_z = jnp.where(at_top, rolled[s][1], turn_z)
                rolled[s] = [turn_y, turn_z]
                curl_x = (nz - down(nz)) - (ny - back[s][1])
                curl_y = (nx - back[s][0]) - (nz - left_z)
                curl_z = (ny - left_y) - (nx - down(nx))
                new[6 * s][p, here, :] = keep * vx + push * curl_x
                new[6 * s + 1][p, here, :] = keep * vy + push * curl_y
                new[6 * s + 2][p, here, :] = keep * vz + push * curl_z

    def substep(old, new, n):
        @pl.when(jnp.logical_not(at_low))
        def _():
            for t in range(plan.tiles):
                for s in range(2):
                    new_magnetic(old, new, s, n, t)

        begin = jnp.where(at_low, DEEP, n + 1)
        end = jnp.where(at_high, DEEP + plan.own, plan.ext - 1 - n)

        def step(p, _):
            full_plane(old, new, p)
            return 0

        lax.fori_loop(begin, end, step, 0)

    def pair(m, _):
        substep(first, second, 2 * m)
        substep(second, first, 2 * m + 1)
        return 0

    lax.fori_loop(0, SUBSTEPS // 2, pair, 0)


def set_media(plan, code, base, silicon):
    def one(p, _):
        for t in range(plan.tiles):
            here = slice(8 * t, 8 * t + 8)
            v = code[p, here, :]
            base[p, here, :] = jnp.where(v == 0.0, SILICON_PERM, jnp.where(v == 1.0, OXIDE_PERM, 1.0))
            silicon[p, here, :] = jnp.where(v == 0.0, 1.0, 0.0)
        return 0

    lax.fori_loop(0, plan.ext, one, 0)


def clear_generation(plan, gen):
    def one(p, _):
        gen[p] = jnp.zeros((plan.rows, plan.lanes), F32)
        return 0

    lax.fori_loop(DEEP, DEEP + plan.own, one, 0)


def sum_generation(plan, gen, message):
    blocks = plan.cols // BLOCK_FACTOR
    lane = lax.broadcasted_iota(jnp.int32, (blocks, plan.lanes), 1)
    across = plan.own_rows()
    out = jnp.zeros((blocks, plan.lanes), F32)
    for a in range(plan.own // BLOCK_FACTOR):
        p = DEEP + BLOCK_FACTOR * a
        rows = (gen[p, across, :] + gen[p + 1, across, :]) + (
            gen[p + 2, across, :] + gen[p + 3, across, :]
        )
        cells = rows.reshape(blocks, BLOCK_FACTOR, plan.lanes).sum(1)
        mean = cells.sum(1, keepdims=True) * (1.0 / (BLOCK_FACTOR * BLOCK_FACTOR * plan.lanes))
        out = jnp.where(lane == a, mean, out)
    z, x, k = (lax.axis_index(axis) for axis in LINE)
    message[...] = jnp.zeros(message.shape, F32)
    message[(z * plan.gx + x) * 2 + k] = out


def round_scratch(plan):
    wide = (plan.ext, plan.rows, plan.lanes)
    return [pltpu.VMEM(wide, F32)] * 27 + [
        pltpu.VMEM((plan.ext // BLOCK_FACTOR, plan.width, plan.lanes), F32),
        pltpu.VMEM(generation_shape(plan), F32),
    ]


def round_flops(plan):
    return SUBSTEPS * plan.ext * plan.width * plan.lanes * 150


def generation_shape(plan):
    return (plan.devices, plan.cols // BLOCK_FACTOR, plan.lanes)


def first_kernel(plan, *refs):
    nside = len(plan.sides)
    coef, density = refs[:2]
    x_in, d_in = refs[2 : 2 + 2 * nside], refs[5 + 2 * nside : 5 + 4 * nside]
    z_same, z_cross, swap = refs[2 + 2 * nside : 5 + 2 * nside]
    raw, medium = refs[5 + 4 * nside : 11 + 4 * nside], refs[11 + 4 * nside]
    strips_in = []
    for n in range(nside):
        strips_in += [*x_in[2 * n : 2 * n + 2], *d_in[2 * n : 2 * n + 2]]
    outs = refs[12 + 4 * nside : 17 + 7 * nside]
    own_out, z_out, core_out, gen_out, code_out = outs[:5]
    strip_out = outs[5:]
    rest = refs[17 + 7 * nside :]
    old, new, (base, silicon, gen, charge, message) = rest[:12], rest[12:24], rest[24:29]
    code, codes = rest[29:31]
    strips, strip_mine, sems = rest[31 : 31 + 4 * nside], rest[31 + 4 * nside : -1], rest[-1]
    copies = Copies(sems)
    z, x, k = (lax.axis_index(a) for a in LINE)
    near = DEEP * (1 - k)
    far = plan.part * k
    begin = (plan.own - DEEP) * k
    across = plan.own_rows()
    here, there = pl.ds(near, plan.part), pl.ds(far, DEEP)
    mine = pl.ds(begin, plan.part)
    early = [copies.start(medium.at[mine], codes)]
    early.append(copies.start(z_same.at[6], code.at[there, across]))
    for source, target in zip(strips_in, strips):
        early.append(copies.start(source, target))
    late = []
    for c in range(6):
        late.append(copies.start(raw[c].at[0, mine], old[c].at[here, across]))
        late.append(copies.start(swap.at[c], old[6 + c].at[here, across]))
        late.append(copies.start(z_same.at[c], old[c].at[there, across]))
        late.append(copies.start(z_cross.at[c], old[6 + c].at[there, across]))
    clear(plan, old, new, [code])
    clear_generation(plan, gen)
    for a in range(plan.ext // BLOCK_FACTOR):
        top = (plan.planes * z + plan.own * k - DEEP) // BLOCK_FACTOR + a
        top = jnp.clip(top, 0, plan.grid_rows - 1)
        for c in range(plan.width // BLOCK_FACTOR):
            left = (plan.cols * x - plan.first_row()) // BLOCK_FACTOR + c
            left = jnp.clip(left, 0, plan.grid_cols - 1)
            value = density[2 * (top // plan.slab), top % plan.slab, left]
            charge[a, 4 * c : 4 * c + 4, :] = jnp.full((4, plan.lanes), value)
    wait(early)

    def settle(p, _):
        code[near + p, across, :] = codes[p].astype(F32)
        return 0

    lax.fori_loop(0, plan.part, settle, 0)

    def place(slot, side):
        x_same, x_cross, d_same, d_cross = strips[4 * slot : 4 * slot + 4]
        at = strip_row(plan, side)
        same = list(enumerate(list(old[:6]) + [code]))
        cross = list(enumerate(old[6:]))
        spread_strip(same, x_same, at, near, plan.part // 2)
        spread_strip(cross, x_cross, at, near, plan.part // 2)
        spread_strip(same, d_same, at, far, DEEP // 2)
        spread_strip(cross, d_cross, at, far, DEEP // 2)

    each_side(plan, place)
    set_media(plan, code, base, silicon)
    wait(late)
    substeps(plan, old, new, base, silicon, charge, gen, coef)
    toward = DEEP + (plan.own - DEEP) * k
    inward = DEEP + (plan.own - DEEP) * (1 - k)
    copies = Copies(sems)
    late = []
    for c in range(12):
        late.append(copies.start(old[c].at[pl.ds(toward, DEEP), across], z_out.at[c]))
        late.append(copies.start(old[c].at[pl.ds(inward, DEEP), across], core_out.at[c]))
        late.append(copies.start(old[c].at[pl.ds(DEEP, plan.own), across], own_out.at[c]))
    late.append(copies.start(code, code_out))

    def gather(slot, side):
        high_end = (side == "high") if plan.paired else (side == "low")
        low = 0 if plan.paired and side == "high" else 8
        at = low + plan.cols - 4 if high_end else low

        def one(q, _):
            for c in range(12):
                for h in range(2):
                    strip_mine[slot][c, q, 4 * h : 4 * h + 4, :] = old[c][
                        DEEP + 2 * q + h, at : at + 4, :
                    ]
            return 0

        lax.fori_loop(0, plan.own // 2, one, 0)

    each_side(plan, gather)
    half, top = DEEP // 2, (plan.own - DEEP) // 2
    for n in range(nside):
        whole, inner, corner = strip_out[3 * n : 3 * n + 3]
        late.append(copies.start(strip_mine[n], whole))
        late.append(copies.start(strip_mine[n].at[:, pl.ds(top * (1 - k), half)], inner))
        late.append(copies.start(strip_mine[n].at[:, pl.ds(top * k, half)], corner))
    sum_generation(plan, gen, message)
    late.append(copies.start(message, gen_out))
    wait(late)


def first_round(plan, coef, density, raw, medium, swap, z_same, z_cross, strips):
    wide = (plan.cols, plan.lanes)
    nside = len(plan.sides)
    shapes = [
        (12, plan.own) + wide,
        (12, DEEP) + wide,
        (12, DEEP) + wide,
        generation_shape(plan),
        (plan.ext, plan.rows, plan.lanes),
    ]
    for _ in plan.sides:
        for rows in (plan.own, DEEP, DEEP):
            shapes.append((12, rows // 2, 8, plan.lanes))
    scratch = round_scratch(plan) + [
        pltpu.VMEM((plan.ext, plan.rows, plan.lanes), F32),
        pltpu.VMEM((plan.part,) + wide, jnp.int32),
    ]
    scratch += [pltpu.VMEM(s.shape, F32) for s in strips]
    scratch += [pltpu.VMEM((12, plan.own // 2, 8, plan.lanes), F32)] * nside
    x_in, d_in = [], []
    for n in range(nside):
        x_in += strips[4 * n : 4 * n + 2]
        d_in += strips[4 * n + 2 : 4 * n + 4]
    return call(
        plan,
        first_kernel,
        "first_round",
        shapes,
        [SMEM, SMEM] + [HBM] * (10 + 4 * nside),
        scratch,
        38 + 3 * nside,
        round_flops(plan),
        10_000_000,
    )(coef, density, *x_in, z_same, z_cross, swap, *d_in, *raw, medium)


def second_kernel(plan, *refs):
    nside = len(plan.sides)
    strips_in = refs[: 3 * nside]
    z_in, core_in, own_in, code_in, charge_in, coef = refs[3 * nside : 6 + 3 * nside]
    outs = refs[6 + 3 * nside : 14 + 3 * nside]
    kept, sent, gen_out = outs[:6], outs[6], outs[7]
    rest = refs[14 + 3 * nside :]
    old, new, (base, silicon, gen, charge, message) = rest[:12], rest[12:24], rest[24:29]
    code, strips, sems = rest[29], rest[30:-1], rest[-1]
    copies = Copies(sems)
    k = lax.axis_index("af")
    across = plan.own_rows()
    outward = plan.part * k
    inner = plan.part * (1 - k)
    early = [copies.start(code_in, code), copies.start(charge_in, charge)]
    for source, target in zip(strips_in, strips):
        early.append(copies.start(source, target))
    late = []
    for c in range(12):
        flip = (c + 6) % 12
        late.append(copies.start(own_in.at[c], old[c].at[pl.ds(DEEP, plan.own), across]))
        late.append(copies.start(z_in.at[flip], old[c].at[pl.ds(outward, DEEP), across]))
        late.append(copies.start(core_in.at[flip], old[c].at[pl.ds(inner, DEEP), across]))
    clear(plan, old, new, [])
    clear_generation(plan, gen)
    wait(early)

    def place(slot, side):
        x_same, x_cross, diag = strips[3 * slot : 3 * slot + 3]
        at = strip_row(plan, side)
        same = list(enumerate(old))
        flipped = list(enumerate(list(old[6:]) + list(old[:6])))
        spread_strip(same, x_same, at, DEEP, plan.own // 2)
        spread_strip(flipped, x_cross, at, inner, DEEP // 2)
        spread_strip(flipped, diag, at, outward, DEEP // 2)

    each_side(plan, place)
    set_media(plan, code, base, silicon)
    wait(late)
    substeps(plan, old, new, base, silicon, charge, gen, coef)
    copies = Copies(sems)
    late = []
    for c in range(6):
        late.append(copies.start(old[6 + c].at[pl.ds(DEEP, plan.own), across], sent.at[c]))
    sum_generation(plan, gen, message)
    late.append(copies.start(message, gen_out))
    for c in range(6):
        target = kept[c].at[0, pl.ds(plan.own * k, plan.own)]
        late.append(copies.start(old[c].at[pl.ds(DEEP, plan.own), across], target))
    wait(late)


def second_round(plan, coef, charge, code, own_in, z_in, core_in, strips):
    wide = (plan.cols, plan.lanes)
    nside = len(plan.sides)
    shapes = [(1, plan.planes) + wide] * 6 + [(6, plan.own) + wide, generation_shape(plan)]
    scratch = round_scratch(plan) + [pltpu.VMEM((plan.ext, plan.rows, plan.lanes), F32)]
    scratch += [pltpu.VMEM(s.shape, F32) for s in strips]
    return call(
        plan,
        second_kernel,
        "second_round",
        shapes,
        [HBM] * (5 + 3 * nside) + [SMEM],
        scratch,
        38 + 3 * nside,
        round_flops(plan),
        10_000_000,
    )(*strips, z_in, core_in, own_in, code, charge, coef)


def join_kernel(plan, *refs):
    got, outs, sems = refs[6], refs[7:13], refs[13]
    copies = Copies(sems)
    k = lax.axis_index("af")
    rows = pl.ds(plan.own * (1 - k), plan.own)
    wait([copies.start(got.at[c], outs[c].at[0, rows]) for c in range(6)])


def join(plan, halves, got):
    shapes = [h.shape for h in halves]
    aliases = {c: c for c in range(6)}
    return call(
        plan, join_kernel, "join", shapes, [HBM] * 7, [], 6, moved=3_000_000, aliases=aliases
    )(*halves, got)


def carrier_kernel(plan, last, *refs):
    density_in, gens_in = refs[:2]
    outs = refs[2:3] if last else refs[2:4]
    gens, one, two, source, charge, sems = refs[2 + len(outs) :]
    copies = Copies(sems)
    rows, cols, lanes = plan.grid_rows, plan.grid_cols, plan.lanes
    z, x, k = (lax.axis_index(a) for a in LINE)
    blocks, own = plan.cols // BLOCK_FACTOR, plan.own // BLOCK_FACTOR
    early = [copies.start(gens_in, gens)]
    if last:
        early.append(copies.start(density_in, one.at[pl.ds(1, rows), pl.ds(8, cols)]))
    zero = jnp.zeros((8, lanes), F32)

    def clean(i, _):
        for ref in (one, two):
            ref[i, 0:8, :] = zero
            ref[i, 8 + cols : 16 + cols, :] = zero
        return 0

    lax.fori_loop(0, rows + 2, clean, 0)
    for ref in (one, two):
        for i in (0, rows + 1):
            for c in range(8, 8 + cols, 8):
                ref[i, c : c + 8, :] = zero
    if not last:

        def read(i, _):
            for c in range(cols):
                value = density_in[2 * (i // plan.slab), i % plan.slab, c]
                one[i + 1, 8 + c : 9 + c, :] = jnp.full((1, lanes), value)
            return 0

        lax.fori_loop(0, rows, read, 0)
    wait(early)

    def unpack(line, _):
        for dx in range(plan.gx):
            for dk in range(2):
                tile = gens[(line * plan.gx + dx) * 2 + dk]
                for a in range(own):
                    source[(line * 2 + dk) * own + a, blocks * dx : blocks * dx + blocks, :] = (
                        jnp.broadcast_to(tile[:, a : a + 1], (blocks, lanes))
                    )
        return 0

    lax.fori_loop(0, plan.gz, unpack, 0)

    def step(old, new):
        def row(i, _):
            for c in range(8, 8 + cols, 8):
                now, before = old[i + 1, c : c + 8, :], old[i, c : c + 8, :]
                around = (
                    old[i + 2, c : c + 8, :]
                    + before
                    + old[i + 1, c + 1 : c + 9, :]
                    + old[i + 1, c - 1 : c + 7, :]
                    - 4.0 * now
                )
                new[i + 1, c : c + 8, :] = (
                    now
                    + SPREAD_COEFF * around
                    - MOBILITY_TERM * (now - before)
                    - LIFETIME_DECAY * now
                    + SOURCE_FACTOR * source[i, c - 8 : c, :]
                )
            return 0

        lax.fori_loop(0, rows, row, 0, unroll=4)

    def pair(_, carry):
        step(one, two)
        step(two, one)
        return carry

    lax.fori_loop(0, CSTEPS // 2, pair, 0)
    if last:
        rows_out = pl.ds(1 + (z * plan.gx + x) * plan.slab, plan.slab)
        wait([copies.start(one.at[rows_out, pl.ds(8, cols)], outs[0])])
        return
    late = [copies.start(one.at[pl.ds(1, rows), pl.ds(8, cols)], outs[0])]
    for a in range(plan.ext // BLOCK_FACTOR):
        top = (plan.planes * z + plan.own * k - DEEP) // BLOCK_FACTOR + a
        top = 1 + jnp.clip(top, 0, rows - 1)
        for c in range(plan.width // BLOCK_FACTOR):
            left = (plan.cols * x - plan.first_row()) // BLOCK_FACTOR + c
            left = 8 + jnp.clip(left, 0, cols - 1)
            value = one[top, pl.ds(left, 1), :]
            charge[a, 4 * c : 4 * c + 4, :] = jnp.broadcast_to(value, (4, lanes))
    late.append(copies.start(charge, outs[1]))
    wait(late)


def carriers(plan, last, density, gens):
    rows, cols, lanes = plan.grid_rows, plan.grid_cols, plan.lanes
    charge = (plan.ext // BLOCK_FACTOR, plan.width, lanes)
    shapes = [(plan.slab, cols, lanes)] if last else [(rows, cols, lanes), charge]
    scratch = [
        pltpu.VMEM(gens.shape, F32),
        pltpu.VMEM((rows + 2, cols + 16, lanes), F32),
        pltpu.VMEM((rows + 2, cols + 16, lanes), F32),
        pltpu.VMEM((rows, cols, lanes), F32),
        pltpu.VMEM(charge, F32),
    ]
    return call(
        plan,
        lambda plan, *refs: carrier_kernel(plan, last, *refs),
        "carriers",
        shapes,
        [HBM if last else SMEM, HBM],
        scratch,
        4,
        2_000_000,
        1_000_000,
    )(density, gens)


def local(ex, ey, ez, hx, hy, hz, medium, coef, density):
    raw = (ex, ey, ez, hx, hy, hz)
    plan = Plan(*medium.shape, density.shape[0])

    def send(message, target):
        return lax.ppermute(message, LINE, line_pairs(plan, target))

    toward = lambda z, goal: z + 1 if goal == 0 else z - 1
    core = lambda z, x, k: (z, x, 1 - k)

    z, x, k = (lax.axis_index(axis) for axis in LINE)
    slabs = jnp.zeros(generation_shape(plan), F32)
    slabs = lax.dynamic_update_slice(slabs, density[None], ((z * plan.gx + x) * 2 + k, 0, 0))
    density = lax.psum(slabs, LINE)[:, : plan.slab, : plan.grid_cols]

    packed = pack_strips(plan, raw, medium)
    strips = []
    for n, side in enumerate(plan.sides):
        to = functools.partial(across_step, side)
        x_same, x_cross, d_same, d_cross = packed[4 * n : 4 * n + 4]
        strips.append(send(x_same, lambda z, x, k: (z, to(x), k)))
        strips.append(send(x_cross, lambda z, x, k: (z, to(x), 1 - k)))
        strips.append(send(d_same, lambda z, x, k: (toward(z, k), to(x), k)))
        strips.append(send(d_cross, lambda z, x, k: (toward(z, 1 - k), to(x), 1 - k)))
    z_same, z_cross, swap = pack_faces(plan, raw, medium, packed[3])
    z_same = send(z_same, lambda z, x, k: (toward(z, k), x, k))
    z_cross = send(z_cross, lambda z, x, k: (toward(z, 1 - k), x, 1 - k))
    swap = send(swap, core)
    outs = first_round(plan, coef, density, raw, medium, swap, z_same, z_cross, strips)
    own, z_msg, core_msg, gens, code = outs[:5]
    gens = lax.psum(gens, LINE)
    strips = []
    for n, side in enumerate(plan.sides):
        to = functools.partial(across_step, side)
        whole, inner, corner = outs[5 + 3 * n : 8 + 3 * n]
        strips.append(send(whole, lambda z, x, k: (z, to(x), k)))
        strips.append(send(inner, lambda z, x, k: (z, to(x), 1 - k)))
        strips.append(send(corner, lambda z, x, k: (toward(z, 1 - k), to(x), 1 - k)))
    z_msg = send(z_msg, lambda z, x, k: (toward(z, 1 - k), x, 1 - k))
    core_msg = send(core_msg, core)
    density, charge = carriers(plan, False, density, gens)
    outs = second_round(plan, coef, charge, code, own, z_msg, core_msg, strips)
    halves, sent, gens = outs[:6], outs[6], outs[7]
    gens = lax.psum(gens, LINE)
    got = send(sent, core)
    (slab,) = carriers(plan, True, density, gens)
    return tuple(join(plan, halves, got)) + (slab[:, :, 0],)


def solution(mesh):
    field = P("af", ("group", "gz"), "gx", None)
    slabs = P(("group", "gz", "gx"), None)
    in_specs = (field,) * 6 + (P(("group", "gz"), "gx", None), P(), slabs)
    out_specs = (field,) * 6 + (slabs,)
    return jax.shard_map(local, mesh=mesh, in_specs=in_specs, out_specs=out_specs, check_vma=False)
```

```python
import functools

import jax
import jax.numpy as jnp
from jax import lax
from jax.experimental import pallas as pl
from jax.experimental.pallas import tpu as pltpu
from jax.sharding import PartitionSpec as P

BLOCK_FACTOR = 4
SUBSTEPS = 4
ROUNDS = 2
CSTEPS = 8

COURANT = 0.5
SILICON_PERM = 12.1
OXIDE_PERM = 2.1
SPREAD_COEFF = 0.2
MOBILITY_TERM = 0.1
LIFETIME_DECAY = 0.05
SOURCE_FACTOR = 0.02

DEEP = SUBSTEPS
LINE = ("gz", "gx", "af")
HBM = pl.BlockSpec(memory_space=pltpu.HBM)
SMEM = pl.BlockSpec(memory_space=pltpu.SMEM)
VMEM_LIMIT = 24 * 1024 * 1024
PACK_LIMIT = 60 * 1024 * 1024
F32 = jnp.float32


class Plan:
    def __init__(self, planes, cols, lanes, slab):
        self.gz = lax.axis_size("gz")
        self.gx = lax.axis_size("gx")
        self.planes, self.cols, self.lanes, self.slab = planes, cols, lanes, slab
        self.own = planes // 2
        self.part = self.own + DEEP
        self.ext = self.own + 2 * DEEP
        self.paired = self.gx == 2
        self.sides = ("face",) if self.paired else ("low", "high")
        self.width = cols + (8 if self.paired else 16)
        self.rows = self.width + 8
        self.tiles = self.width // 8
        self.grid_rows = planes * self.gz // BLOCK_FACTOR
        self.grid_cols = cols * self.gx // BLOCK_FACTOR
        self.devices = self.gz * self.gx * 2

    def first_row(self):
        return 8 * lax.axis_index("gx") if self.paired else 8

    def own_rows(self):
        return pl.ds(pl.multiple_of(self.first_row(), 8), self.cols)


def each_side(plan, act):
    if plan.paired:
        across = lax.axis_index("gx")

        @pl.when(across == 0)
        def _():
            act(0, "high")

        @pl.when(across == 1)
        def _():
            act(0, "low")
    else:
        act(0, "low")
        act(1, "high")


def line_pairs(plan, target):
    pairs = []
    for z in range(plan.gz):
        for x in range(plan.gx):
            for k in range(2):
                tz, tx, tk = target(z, x, k)
                if 0 <= tz < plan.gz and 0 <= tx < plan.gx:
                    pairs.append(((z * plan.gx + x) * 2 + k, (tz * plan.gx + tx) * 2 + tk))
    return pairs


def across_step(side, x):
    if side == "face":
        return 1 - x
    return x + 1 if side == "low" else x - 1


class Copies:
    def __init__(self, sems):
        self.sems, self.made = sems, 0

    def start(self, source, target):
        copy = pltpu.make_async_copy(source, target, self.sems.at[self.made])
        self.made += 1
        copy.start()
        return copy


def wait(copies):
    for copy in copies:
        copy.wait()


def call(plan, body, name, shapes, in_specs, scratch, copies, flops=0, moved=0, aliases=None, limit=VMEM_LIMIT):
    return pl.pallas_call(
        functools.partial(body, plan),
        out_shape=[jax.ShapeDtypeStruct(s, F32) for s in shapes],
        in_specs=in_specs,
        out_specs=[HBM] * len(shapes),
        scratch_shapes=scratch + [pltpu.SemaphoreType.DMA((copies,))],
        input_output_aliases=aliases or {},
        compiler_params=pltpu.CompilerParams(vmem_limit_bytes=limit),
        cost_estimate=pl.CostEstimate(flops=flops, bytes_accessed=moved, transcendentals=0),
        name=name,
    )


def pack_kernel(plan, *refs):
    raw, other, medium, nside = refs[:6], refs[6:12], refs[12], len(plan.sides)
    outs = refs[14 : 15 + 3 * nside]
    edge, edge_code, face, face_code, strips, sems = refs[15 + 3 * nside :]
    copies = Copies(sems)
    k = lax.axis_index("af")
    mine = pl.ds(plan.own * k, plan.own)
    outer = pl.ds((plan.planes - DEEP) * k, DEEP)
    if plan.paired:
        tile_rows = [pl.multiple_of((plan.cols - 8) * (1 - lax.axis_index("gx")), 8)]
    else:
        tile_rows = [plan.cols - 8, 0]
    early, late, last = [], [], []
    for n, row in enumerate(tile_rows):
        for c in range(6):
            side = pl.ds(row, 8)
            early.append(copies.start(raw[c].at[0, mine, side, :], edge.at[n, c]))
            early.append(copies.start(other[c].at[0, mine, side, :], edge.at[n, 6 + c]))
        early.append(copies.start(medium.at[mine, pl.ds(row, 8), :], edge_code.at[n]))
    for c in range(6):
        late.append(copies.start(raw[c].at[0, outer], face.at[c]))
        late.append(copies.start(other[c].at[0, outer], face.at[6 + c]))
    late.append(copies.start(medium.at[outer], face_code))
    wait(early)

    def fill(slot, low):
        def rows(q, _):
            for h in range(2):
                half = slice(4 * h, 4 * h + 4)
                for c in range(12):
                    strips[slot, c, q, half, :] = edge[slot, c, 2 * q + h, low : low + 4, :]
                code = edge_code[slot, 2 * q + h, low : low + 4, :]
                strips[slot, 12, q, half, :] = code.astype(F32)
            return 0

        lax.fori_loop(0, plan.own // 2, rows, 0)

    each_side(plan, lambda slot, side: fill(slot, 4 if plan.paired == (side == "high") else 0))
    send_strips(plan, copies, last, strips, outs[1:])
    wait(late)
    face[12] = face_code[...].astype(F32)
    last.append(copies.start(face, outs[0]))
    wait(last)


def send_strips(plan, copies, started, strips, outs):
    k = lax.axis_index("af")
    half, top = DEEP // 2, (plan.own - DEEP) // 2
    for n in range(len(plan.sides)):
        whole, inner, corner = outs[3 * n : 3 * n + 3]
        started.append(copies.start(strips.at[n], whole))
        started.append(copies.start(strips.at[n, :, pl.ds(top * (1 - k), half)], inner))
        started.append(copies.start(strips.at[n, :, pl.ds(top * k, half)], corner))


def strip_shapes(plan, comps):
    shapes = []
    for _ in plan.sides:
        for rows in (plan.own, DEEP, DEEP):
            shapes.append((comps, rows // 2, 8, plan.lanes))
    return shapes


def pack(plan, raw, other, medium, after):
    wide = (plan.cols, plan.lanes)
    nside = len(plan.sides)
    scratch = [
        pltpu.VMEM((nside, 12, plan.own, 8, plan.lanes), F32),
        pltpu.VMEM((nside, plan.own, 8, plan.lanes), jnp.int32),
        pltpu.VMEM((13, DEEP) + wide, F32),
        pltpu.VMEM((DEEP,) + wide, jnp.int32),
        pltpu.VMEM((nside, 13, plan.own // 2, 8, plan.lanes), F32),
    ]
    return call(
        plan,
        pack_kernel,
        "pack",
        [(13, DEEP) + wide] + strip_shapes(plan, 13),
        [HBM] * 14,
        scratch,
        16 * nside + 14,
        moved=4_000_000,
        limit=PACK_LIMIT,
    )(*raw, *other, medium, after)


def clear(plan, old, new, code):
    zero = jnp.zeros((8, plan.lanes), F32)

    def halo(slot, side):
        tile = plan.tiles - 1 if side == "high" else 0

        def one(p, _):
            for ref in list(old) + code:
                ref[p, 8 * tile : 8 * tile + 8, :] = zero
            return 0

        lax.fori_loop(0, plan.ext, one, 0)

    each_side(plan, halo)

    def above(p, _):
        for c in (1, 2, 7, 8):
            for ref in (old[c], new[c]):
                ref[p, plan.width : plan.width + 8, :] = zero
        return 0

    lax.fori_loop(0, plan.ext, above, 0)
    for c, ref in enumerate(new):
        plane = DEEP + plan.own if c % 6 < 3 else DEEP - 1
        for t in range(plan.tiles):
            ref[plane, 8 * t : 8 * t + 8, :] = zero


def strip_row(plan, side):
    if side == "low":
        return 4
    return plan.cols if plan.paired else 8 + plan.cols


def spread_strip(refs, strip, at, plane, pairs):
    def one(q, _):
        for c, ref in refs:
            for h in range(2):
                ref[plane + 2 * q + h, at : at + 4, :] = strip[c, q, 4 * h : 4 * h + 4, :]
        return 0

    lax.fori_loop(0, pairs, one, 0)


def substeps(plan, first, second, base, silicon, charge, gen, coef):
    lanes = plan.lanes
    tile = (8, lanes)
    lane = lax.broadcasted_iota(jnp.int32, tile, 1)
    row = lax.broadcasted_iota(jnp.int32, tile, 0)
    keep_up, keep_down, at_top = lane < lanes - 1, lane > 0, row == 0
    z, x, k = (lax.axis_index(a) for a in LINE)
    at_low = jnp.logical_and(z == 0, k == 0)
    at_high = jnp.logical_and(z == plan.gz - 1, k == 1)

    def up(v):
        return jnp.where(keep_up, pltpu.roll(v, lanes - 1, 1), 0.0)

    def down(v):
        return jnp.where(keep_down, pltpu.roll(v, 1, 1), 0.0)

    def edge_mask(t):
        if plan.paired or t not in (0, plan.tiles - 1):
            return None
        off = (x == 0) if t == 0 else (x == plan.gx - 1)
        return jnp.where(off, 0.0, 1.0)

    def new_magnetic(old, new, s, p, t):
        ex, ey, ez, hx, hy, hz = old[6 * s : 6 * s + 6]
        here, beside = slice(8 * t, 8 * t + 8), slice(8 * t + 1, 8 * t + 9)
        vx, vy, vz = ex[p, here, :], ey[p, here, :], ez[p, here, :]
        nx = hx[p, here, :] - COURANT * ((up(vz) - vz) - (ey[p + 1, here, :] - vy))
        ny = hy[p, here, :] - COURANT * ((ex[p + 1, here, :] - vx) - (ez[p, beside, :] - vz))
        nz = hz[p, here, :] - COURANT * ((ey[p, beside, :] - vy) - (up(vx) - vx))
        mask = edge_mask(t)
        if mask is not None:
            nx, ny, nz = nx * mask, ny * mask, nz * mask
        new[6 * s + 3][p, here, :] = nx
        new[6 * s + 4][p, here, :] = ny
        new[6 * s + 5][p, here, :] = nz
        return vx, vy, vz, nx, ny, nz

    def full_plane(old, new, p):
        coarse = p // BLOCK_FACTOR
        kerr, two = (coef[0], coef[4]), (coef[1], coef[5])
        half_two, half_free = (coef[2], coef[6]), (coef[3], coef[7])
        zero = jnp.zeros(tile, F32)
        rolled = [[zero, zero], [zero, zero]]
        for t in range(plan.tiles):
            here = slice(8 * t, 8 * t + 8)
            back = [[new[6 * s + c][p - 1, here, :] for c in (3, 4)] for s in range(2)]
            vals = [new_magnetic(old, new, s, p, t) for s in range(2)]
            strength = [v[0] * v[0] + v[1] * v[1] + v[2] * v[2] for v in vals]
            is_silicon = silicon[p, here, :]
            total = (strength[0] + strength[1]) * is_silicon
            carriers = charge[coarse, here, :] * is_silicon
            ground = base[p, here, :]
            gen[p, here, :] += (two[0] * strength[0] + two[1] * strength[1]) * total
            mask = edge_mask(t)
            for s in range(2):
                vx, vy, vz, nx, ny, nz = vals[s]
                loss = half_two[s] * total + half_free[s] * carriers
                perm = ground + kerr[s] * total
                divisor = perm + loss
                inv = pl.reciprocal(divisor, approx=True)
                inv = inv * (2.0 - divisor * inv)
                keep = (perm - loss) * inv
                push = COURANT * inv
                if mask is not None:
                    push = push * mask
                turn_y, turn_z = pltpu.roll(ny, 1, 0), pltpu.roll(nz, 1, 0)
                left_y = jnp.where(at_top, rolled[s][0], turn_y)
                left_z = jnp.where(at_top, rolled[s][1], turn_z)
                rolled[s] = [turn_y, turn_z]
                curl_x = (nz - down(nz)) - (ny - back[s][1])
                curl_y = (nx - back[s][0]) - (nz - left_z)
                curl_z = (ny - left_y) - (nx - down(nx))
                new[6 * s][p, here, :] = keep * vx + push * curl_x
                new[6 * s + 1][p, here, :] = keep * vy + push * curl_y
                new[6 * s + 2][p, here, :] = keep * vz + push * curl_z

    def substep(old, new, n):
        @pl.when(jnp.logical_not(at_low))
        def _():
            for t in range(plan.tiles):
                for s in range(2):
                    new_magnetic(old, new, s, n, t)

        begin = jnp.where(at_low, DEEP, n + 1)
        end = jnp.where(at_high, DEEP + plan.own, plan.ext - 1 - n)

        def step(p, _):
            full_plane(old, new, p)
            return 0

        lax.fori_loop(begin, end, step, 0)

    def pair(m, _):
        substep(first, second, 2 * m)
        substep(second, first, 2 * m + 1)
        return 0

    lax.fori_loop(0, SUBSTEPS // 2, pair, 0)


def set_media(plan, code, base, silicon):
    def one(p, _):
        for t in range(plan.tiles):
            here = slice(8 * t, 8 * t + 8)
            v = code[p, here, :]
            base[p, here, :] = jnp.where(v == 0.0, SILICON_PERM, jnp.where(v == 1.0, OXIDE_PERM, 1.0))
            silicon[p, here, :] = jnp.where(v == 0.0, 1.0, 0.0)
        return 0

    lax.fori_loop(0, plan.ext, one, 0)


def clear_generation(plan, gen):
    def one(p, _):
        gen[p] = jnp.zeros((plan.rows, plan.lanes), F32)
        return 0

    lax.fori_loop(DEEP, DEEP + plan.own, one, 0)


def sum_generation(plan, gen, message):
    blocks = plan.cols // BLOCK_FACTOR
    lane = lax.broadcasted_iota(jnp.int32, (blocks, plan.lanes), 1)
    across = plan.own_rows()
    out = jnp.zeros((blocks, plan.lanes), F32)
    for a in range(plan.own // BLOCK_FACTOR):
        p = DEEP + BLOCK_FACTOR * a
        rows = (gen[p, across, :] + gen[p + 1, across, :]) + (
            gen[p + 2, across, :] + gen[p + 3, across, :]
        )
        cells = rows.reshape(blocks, BLOCK_FACTOR, plan.lanes).sum(1)
        mean = cells.sum(1, keepdims=True) * (1.0 / (BLOCK_FACTOR * BLOCK_FACTOR * plan.lanes))
        out = jnp.where(lane == a, mean, out)
    message[...] = out


def round_scratch(plan):
    wide = (plan.ext, plan.rows, plan.lanes)
    return [pltpu.VMEM(wide, F32)] * 27 + [
        pltpu.VMEM((plan.ext // BLOCK_FACTOR, plan.width, plan.lanes), F32),
        pltpu.VMEM(generation_shape(plan)[1:], F32),
        pltpu.VMEM((8, 8, plan.lanes), F32),
        pltpu.VMEM(wide, F32),
    ]


def round_flops(plan):
    return SUBSTEPS * plan.ext * plan.width * plan.lanes * 150


def generation_shape(plan):
    return (plan.devices, plan.cols // BLOCK_FACTOR, plan.lanes)


def place_strips(plan, old, code, strips):
    k = lax.axis_index("af")
    outward, inner = plan.part * k, plan.part * (1 - k)

    def place(slot, side):
        whole, beside, corner = strips[3 * slot : 3 * slot + 3]
        at = strip_row(plan, side)
        same = list(enumerate(list(old) + code))
        flipped = list(enumerate(list(old[6:]) + list(old[:6]) + code))
        spread_strip(same, whole, at, DEEP, plan.own // 2)
        spread_strip(flipped, beside, at, inner, DEEP // 2)
        spread_strip(flipped, corner, at, outward, DEEP // 2)

    each_side(plan, place)


def send_generation(plan, copies, started, gen, message, gen_out):
    sum_generation(plan, gen, message)
    for d in range(plan.devices):
        started.append(copies.start(message, gen_out.at[d]))


def first_kernel(plan, *refs):
    nside = len(plan.sides)
    strips_in = refs[: 3 * nside]
    z_in, raw, other = refs[3 * nside], refs[1 + 3 * nside : 7 + 3 * nside], refs[7 + 3 * nside : 13 + 3 * nside]
    medium, charge_in, coef_in = refs[13 + 3 * nside : 16 + 3 * nside]
    outs = refs[16 + 3 * nside : 21 + 6 * nside]
    own_out, z_out, core_out, gen_out, code_out = outs[:5]
    rest = refs[21 + 6 * nside :]
    old, new, (base, silicon, gen, charge, message, coef, code) = rest[:12], rest[12:24], rest[24:31]
    codes, strips, strip_mine, sems = rest[31], rest[32 : 32 + 3 * nside], rest[-2], rest[-1]
    copies = Copies(sems)
    k = lax.axis_index("af")
    near = DEEP * (1 - k)
    far = plan.part * k
    across = plan.own_rows()
    here, there = pl.ds(near, plan.part), pl.ds(far, DEEP)
    mine = pl.ds((plan.own - DEEP) * k, plan.part)
    early = [copies.start(medium.at[mine], codes)]
    early.append(copies.start(z_in.at[12], code.at[there, across]))
    early.append(copies.start(charge_in, charge))
    early.append(copies.start(coef_in, coef))
    for source, target in zip(strips_in, strips):
        early.append(copies.start(source, target))
    late = []
    for c in range(6):
        late.append(copies.start(raw[c].at[0, mine], old[c].at[here, across]))
        late.append(copies.start(other[c].at[0, mine], old[6 + c].at[here, across]))
    for c in range(12):
        late.append(copies.start(z_in.at[(c + 6) % 12], old[c].at[there, across]))
    clear(plan, old, new, [code])
    clear_generation(plan, gen)
    wait(early)

    def settle(p, _):
        code[near + p, across, :] = codes[p].astype(F32)
        return 0

    lax.fori_loop(0, plan.part, settle, 0)
    place_strips(plan, old, [code], strips)
    set_media(plan, code, base, silicon)
    wait(late)
    substeps(plan, old, new, base, silicon, charge, gen, coef)
    copies = Copies(sems)
    late = []

    def gather(slot, side):
        high_end = (side == "high") if plan.paired else (side == "low")
        low = 0 if plan.paired and side == "high" else 8
        at = low + plan.cols - 4 if high_end else low

        def one(q, _):
            for c in range(12):
                for h in range(2):
                    strip_mine[slot, c, q, 4 * h : 4 * h + 4, :] = old[c][
                        DEEP + 2 * q + h, at : at + 4, :
                    ]
            return 0

        lax.fori_loop(0, plan.own // 2, one, 0)

    toward = DEEP + (plan.own - DEEP) * k
    inward = DEEP + (plan.own - DEEP) * (1 - k)
    for c in range(12):
        late.append(copies.start(old[c].at[pl.ds(toward, DEEP), across], z_out.at[c]))
        late.append(copies.start(old[c].at[pl.ds(inward, DEEP), across], core_out.at[c]))
        late.append(copies.start(old[c].at[pl.ds(DEEP, plan.own), across], own_out.at[c]))
    late.append(copies.start(code, code_out))
    each_side(plan, gather)
    send_strips(plan, copies, late, strip_mine, outs[5:])
    send_generation(plan, copies, late, gen, message, gen_out)
    wait(late)


def first_round(plan, strips, z_in, raw, other, medium, charge, coef):
    wide = (plan.cols, plan.lanes)
    nside = len(plan.sides)
    shapes = [
        (12, plan.own) + wide,
        (12, DEEP) + wide,
        (12, DEEP) + wide,
        generation_shape(plan),
        (plan.ext, plan.rows, plan.lanes),
    ] + strip_shapes(plan, 12)
    scratch = round_scratch(plan) + [pltpu.VMEM((plan.part,) + wide, jnp.int32)]
    scratch += [pltpu.VMEM(s.shape, F32) for s in strips]
    scratch += [pltpu.VMEM((nside, 12, plan.own // 2, 8, plan.lanes), F32)]
    return call(
        plan,
        first_kernel,
        "first_round",
        shapes,
        [HBM] * (16 + 3 * nside),
        scratch,
        37 + 3 * nside + plan.devices,
        round_flops(plan),
        10_000_000,
    )(*strips, z_in, *raw, *other, medium, charge, coef)


def second_kernel(plan, *refs):
    nside = len(plan.sides)
    strips_in = refs[: 3 * nside]
    z_in, core_in, own_in, code_in, charge_in, coef_in = refs[3 * nside : 6 + 3 * nside]
    outs = refs[6 + 3 * nside : 14 + 3 * nside]
    kept, sent, gen_out = outs[:6], outs[6], outs[7]
    rest = refs[14 + 3 * nside :]
    old, new, (base, silicon, gen, charge, message, coef, code) = rest[:12], rest[12:24], rest[24:31]
    strips, sems = rest[31:-1], rest[-1]
    copies = Copies(sems)
    k = lax.axis_index("af")
    across = plan.own_rows()
    outward = plan.part * k
    inner = plan.part * (1 - k)
    early = [copies.start(code_in, code), copies.start(charge_in, charge)]
    early.append(copies.start(coef_in, coef))
    for source, target in zip(strips_in, strips):
        early.append(copies.start(source, target))
    late = []
    for c in range(12):
        flip = (c + 6) % 12
        late.append(copies.start(own_in.at[c], old[c].at[pl.ds(DEEP, plan.own), across]))
        late.append(copies.start(z_in.at[flip], old[c].at[pl.ds(outward, DEEP), across]))
        late.append(copies.start(core_in.at[flip], old[c].at[pl.ds(inner, DEEP), across]))
    clear(plan, old, new, [])
    clear_generation(plan, gen)
    wait(early)
    place_strips(plan, old, [], strips)
    set_media(plan, code, base, silicon)
    wait(late)
    substeps(plan, old, new, base, silicon, charge, gen, coef)
    copies = Copies(sems)
    late = []
    for c in range(6):
        late.append(copies.start(old[6 + c].at[pl.ds(DEEP, plan.own), across], sent.at[c]))
    for c in range(6):
        target = kept[c].at[0, pl.ds(plan.own * k, plan.own)]
        late.append(copies.start(old[c].at[pl.ds(DEEP, plan.own), across], target))
    send_generation(plan, copies, late, gen, message, gen_out)
    wait(late)


def second_round(plan, strips, z_in, core_in, own_in, code, charge, coef):
    wide = (plan.cols, plan.lanes)
    nside = len(plan.sides)
    shapes = [(1, plan.planes) + wide] * 6 + [(6, plan.own) + wide, generation_shape(plan)]
    scratch = round_scratch(plan) + [pltpu.VMEM(s.shape, F32) for s in strips]
    return call(
        plan,
        second_kernel,
        "second_round",
        shapes,
        [HBM] * (6 + 3 * nside),
        scratch,
        39 + 3 * nside + plan.devices,
        round_flops(plan),
        10_000_000,
    )(*strips, z_in, core_in, own_in, code, charge, coef)


def join_kernel(plan, *refs):
    got, outs, sems = refs[6], refs[7:13], refs[13]
    copies = Copies(sems)
    k = lax.axis_index("af")
    rows = pl.ds(plan.own * (1 - k), plan.own)
    wait([copies.start(got.at[c], outs[c].at[0, rows]) for c in range(6)])


def join(plan, halves, got):
    shapes = [h.shape for h in halves]
    aliases = {c: c for c in range(6)}
    return call(
        plan, join_kernel, "join", shapes, [HBM] * 7, [], 6, moved=3_000_000, aliases=aliases
    )(*halves, got)


def under_cells(plan, grid, charge):
    z, x, k = (lax.axis_index(a) for a in LINE)
    for a in range(plan.ext // BLOCK_FACTOR):
        top = (plan.planes * z + plan.own * k - DEEP) // BLOCK_FACTOR + a
        top = 1 + jnp.clip(top, 0, plan.grid_rows - 1)
        for c in range(plan.width // BLOCK_FACTOR):
            left = (plan.cols * x - plan.first_row()) // BLOCK_FACTOR + c
            left = 8 + jnp.clip(left, 0, plan.grid_cols - 1)
            value = grid[top, pl.ds(left, 1), :]
            charge[a, 4 * c : 4 * c + 4, :] = jnp.broadcast_to(value, (4, plan.lanes))


def grid_shape(plan):
    return (plan.grid_rows + 2, plan.grid_cols + 16, plan.lanes)


def charge_shape(plan):
    return (plan.ext // BLOCK_FACTOR, plan.width, plan.lanes)


def spread_kernel(plan, density, table, grid_out, charge_out, coef_out, grid, charge, coef, sems):
    copies = Copies(sems)
    k = lax.axis_index("af")
    rows, cols, lanes = plan.grid_rows, plan.grid_cols, plan.lanes

    def clean(i, _):
        for c in range(0, cols + 16, 8):
            grid[i, c : c + 8, :] = jnp.zeros((8, lanes), F32)
        return 0

    lax.fori_loop(0, rows + 2, clean, 0)

    def read(i, _):
        for c in range(cols):
            value = density[i // plan.slab, i % plan.slab, c]
            grid[i + 1, 8 + c : 9 + c, :] = jnp.full((1, lanes), value)
        return 0

    lax.fori_loop(0, rows, read, 0)
    under_cells(plan, grid, charge)
    for s in range(2):
        which = k if s == 0 else 1 - k
        kerr, two, free = table[which, 0], table[which, 1], table[which, 2]
        for n, value in enumerate((kerr, two, 0.5 * two, 0.5 * free)):
            coef[4 * s + n] = jnp.full((8, lanes), value)
    pairs = ((grid, grid_out), (charge, charge_out), (coef, coef_out))
    wait([copies.start(source, target) for source, target in pairs])


def spread(plan, density, table):
    shapes = [grid_shape(plan), charge_shape(plan), (8, 8, plan.lanes)]
    scratch = [pltpu.VMEM(shape, F32) for shape in shapes]
    return call(
        plan, spread_kernel, "spread", shapes, [SMEM, SMEM], scratch, 3, 10_000, 1_000_000
    )(density, table)


def carrier_kernel(plan, last, density_in, gens_in, *refs):
    outs = refs[:1] if last else refs[:2]
    gens, one, two, source, charge, sems = refs[len(outs) :]
    copies = Copies(sems)
    rows, cols, lanes = plan.grid_rows, plan.grid_cols, plan.lanes
    z, x = lax.axis_index("gz"), lax.axis_index("gx")
    blocks, own = plan.cols // BLOCK_FACTOR, plan.own // BLOCK_FACTOR
    early = [copies.start(gens_in, gens), copies.start(density_in, one)]
    zero = jnp.zeros((8, lanes), F32)

    def clean(i, _):
        two[i, 0:8, :] = zero
        two[i, 8 + cols : 16 + cols, :] = zero
        return 0

    lax.fori_loop(0, rows + 2, clean, 0)
    for i in (0, rows + 1):
        for c in range(8, 8 + cols, 8):
            two[i, c : c + 8, :] = zero
    wait(early)

    def unpack(line, _):
        for dx in range(plan.gx):
            for dk in range(2):
                tile = gens[(line * plan.gx + dx) * 2 + dk]
                for a in range(own):
                    source[(line * 2 + dk) * own + a, blocks * dx : blocks * dx + blocks, :] = (
                        jnp.broadcast_to(SOURCE_FACTOR * tile[:, a : a + 1], (blocks, lanes))
                    )
        return 0

    lax.fori_loop(0, plan.gz, unpack, 0)

    def step(old, new):
        def row(m, _):
            for h in range(4):
                i = 4 * m + h
                for c in range(8, 8 + cols, 8):
                    now, before = old[i + 1, c : c + 8, :], old[i, c : c + 8, :]
                    around = (
                        old[i + 2, c : c + 8, :]
                        + before
                        + old[i + 1, c + 1 : c + 9, :]
                        + old[i + 1, c - 1 : c + 7, :]
                        - 4.0 * now
                    )
                    new[i + 1, c : c + 8, :] = (
                        now
                        + SPREAD_COEFF * around
                        - MOBILITY_TERM * (now - before)
                        - LIFETIME_DECAY * now
                        + source[i, c - 8 : c, :]
                    )
            return 0

        lax.fori_loop(0, rows // 4, row, 0)

    def pair(_, carry):
        step(one, two)
        step(two, one)
        return carry

    lax.fori_loop(0, CSTEPS // 2, pair, 0)
    if last:
        rows_out = pl.ds(1 + (z * plan.gx + x) * plan.slab, plan.slab)
        wait([copies.start(one.at[rows_out, pl.ds(8, cols)], outs[0])])
        return
    under_cells(plan, one, charge)
    wait([copies.start(one, outs[0]), copies.start(charge, outs[1])])


def carriers(plan, last, density, gens):
    grid, lanes = grid_shape(plan), plan.lanes
    shapes = [(plan.slab, plan.grid_cols, lanes)] if last else [grid, charge_shape(plan)]
    scratch = [
        pltpu.VMEM(gens.shape, F32),
        pltpu.VMEM(grid, F32),
        pltpu.VMEM(grid, F32),
        pltpu.VMEM((plan.grid_rows, plan.grid_cols, lanes), F32),
        pltpu.VMEM(charge_shape(plan), F32),
    ]
    return call(
        plan,
        lambda plan, *refs: carrier_kernel(plan, last, *refs),
        "carriers",
        shapes,
        [HBM, HBM],
        scratch,
        4,
        2_000_000,
        1_000_000,
    )(density, gens)


def local(ex, ey, ez, hx, hy, hz, medium, table, density):
    raw = (ex, ey, ez, hx, hy, hz)
    plan = Plan(*medium.shape, density.shape[0])

    def send(message, target):
        return lax.ppermute(message, LINE, line_pairs(plan, target))

    def everywhere(message, axes):
        return lax.all_to_all(message, axes, split_axis=0, concat_axis=0, tiled=True)

    core = lambda z, x, k: (z, x, 1 - k)
    beyond = lambda z, k: z - 1 if k == 0 else z + 1

    def exchange(z_msg, strips):
        got = []
        for n, side in enumerate(plan.sides):
            to = functools.partial(across_step, side)
            whole, inner, corner = strips[3 * n : 3 * n + 3]
            got.append(send(whole, lambda z, x, k: (z, to(x), k)))
            got.append(send(inner, lambda z, x, k: (z, to(x), 1 - k)))
            got.append(send(corner, lambda z, x, k: (beyond(z, k), to(x), 1 - k)))
        return send(z_msg, lambda z, x, k: (beyond(z, k), x, 1 - k)), got

    other = [send(r, core) for r in raw]
    tiles = plan.gz * plan.gx
    slabs = everywhere(jnp.broadcast_to(density, (tiles,) + density.shape), ("gz", "gx"))
    packed = pack(plan, raw, other, medium, slabs)
    grid, charge, coef = spread(plan, slabs, table)
    z_in, strips = exchange(packed[0], packed[1:])
    outs = first_round(plan, strips, z_in, raw, other, medium, charge, coef)
    own, z_msg, core_msg, gens, code = outs[:5]
    gens = everywhere(gens, LINE)
    z_in, strips = exchange(z_msg, outs[5:])
    core_in = send(core_msg, core)
    grid, charge = carriers(plan, False, grid, gens)
    outs = second_round(plan, strips, z_in, core_in, own, code, charge, coef)
    halves, sent, gens = outs[:6], outs[6], outs[7]
    gens = everywhere(gens, LINE)
    got = send(sent, core)
    (slab,) = carriers(plan, True, grid, gens)
    return tuple(join(plan, halves, got)) + (slab[:, :, 0],)


def solution(mesh):
    field = P("af", ("group", "gz"), "gx", None)
    slabs = P(("group", "gz", "gx"), None)
    in_specs = (field,) * 6 + (P(("group", "gz"), "gx", None), P(), slabs)
    out_specs = (field,) * 6 + (slabs,)
    return jax.shard_map(local, mesh=mesh, in_specs=in_specs, out_specs=out_specs, check_vma=False)
```

```python
import functools

import jax
import jax.numpy as jnp
from jax import lax
from jax.experimental import pallas as pl
from jax.experimental.pallas import tpu as pltpu
from jax.sharding import PartitionSpec as P

BLOCK_FACTOR = 4
SUBSTEPS = 4
ROUNDS = 2
CSTEPS = 8

COURANT = 0.5
SILICON_PERM = 12.1
OXIDE_PERM = 2.1
SPREAD_COEFF = 0.2
MOBILITY_TERM = 0.1
LIFETIME_DECAY = 0.05
SOURCE_FACTOR = 0.02

DEEP = SUBSTEPS
LINE = ("gz", "gx", "af")
HBM = pl.BlockSpec(memory_space=pltpu.HBM)
ANY = pl.BlockSpec(memory_space=pl.ANY)
SMEM = pl.BlockSpec(memory_space=pltpu.SMEM)
VMEM_LIMIT = 24 * 1024 * 1024
F32 = jnp.float32


class Plan:
    def __init__(self, planes, cols, lanes, slab):
        self.gz = lax.axis_size("gz")
        self.gx = lax.axis_size("gx")
        self.planes, self.cols, self.lanes, self.slab = planes, cols, lanes, slab
        self.own = planes // 2
        self.part = self.own + DEEP
        self.ext = self.own + 2 * DEEP
        self.paired = self.gx == 2
        self.sides = ("face",) if self.paired else ("low", "high")
        self.width = cols + (8 if self.paired else 16)
        self.rows = self.width + 8
        self.tiles = self.width // 8
        self.grid_rows = planes * self.gz // BLOCK_FACTOR
        self.grid_cols = cols * self.gx // BLOCK_FACTOR
        self.devices = self.gz * self.gx * 2

    def first_row(self):
        return 8 * lax.axis_index("gx") if self.paired else 8

    def own_rows(self):
        return pl.ds(pl.multiple_of(self.first_row(), 8), self.cols)


def each_side(plan, act):
    if plan.paired:
        across = lax.axis_index("gx")

        @pl.when(across == 0)
        def _():
            act(0, "high")

        @pl.when(across == 1)
        def _():
            act(0, "low")
    else:
        act(0, "low")
        act(1, "high")


def line_pairs(plan, target):
    pairs = []
    for z in range(plan.gz):
        for x in range(plan.gx):
            for k in range(2):
                tz, tx, tk = target(z, x, k)
                if 0 <= tz < plan.gz and 0 <= tx < plan.gx:
                    pairs.append(((z * plan.gx + x) * 2 + k, (tz * plan.gx + tx) * 2 + tk))
    return pairs


def across_step(side, x):
    if side == "face":
        return 1 - x
    return x + 1 if side == "low" else x - 1


class Copies:
    def __init__(self, sems):
        self.sems, self.made = sems, 0

    def start(self, source, target):
        copy = pltpu.make_async_copy(source, target, self.sems.at[self.made])
        self.made += 1
        copy.start()
        return copy


def wait(copies):
    for copy in copies:
        copy.wait()


def call(plan, body, name, shapes, in_specs, scratch, copies, flops=0, moved=0, aliases=None):
    kernel = pl.pallas_call(
        functools.partial(body, plan),
        out_shape=[pltpu.HBM(s, F32) for s in shapes],
        in_specs=in_specs,
        out_specs=[HBM] * len(shapes),
        scratch_shapes=scratch + [pltpu.SemaphoreType.DMA((copies,))],
        input_output_aliases=aliases or {},
        compiler_params=pltpu.CompilerParams(vmem_limit_bytes=VMEM_LIMIT),
        cost_estimate=pl.CostEstimate(flops=flops, bytes_accessed=moved, transcendentals=0),
        name=name,
    )

    def run(*args):
        placed = []
        for arg, spec in zip(args, in_specs):
            in_hbm = spec.memory_space is pltpu.HBM
            placed.append(pltpu.with_memory_space_constraint(arg, pltpu.HBM) if in_hbm else arg)
        return kernel(*placed)

    return run


def pack_kernel(plan, *refs):
    raw, other, medium, nside = refs[:6], refs[6:12], refs[12], len(plan.sides)
    slab_in, table = refs[13:15]
    outs = refs[15 : 17 + 3 * nside]
    edge, edge_code, face, face_code, strips, slab, coef, sems = refs[17 + 3 * nside :]
    copies = Copies(sems)
    k = lax.axis_index("af")
    mine = pl.ds(plan.own * k, plan.own)
    outer = pl.ds((plan.planes - DEEP) * k, DEEP)
    if plan.paired:
        tile_rows = [pl.multiple_of((plan.cols - 8) * (1 - lax.axis_index("gx")), 8)]
    else:
        tile_rows = [plan.cols - 8, 0]
    early, late, last = [], [], []
    for n, row in enumerate(tile_rows):
        for c in range(6):
            side = pl.ds(row, 8)
            early.append(copies.start(raw[c].at[0, mine, side, :], edge.at[n, c]))
            early.append(copies.start(other[c].at[0, mine, side, :], edge.at[n, 6 + c]))
        early.append(copies.start(medium.at[mine, pl.ds(row, 8), :], edge_code.at[n]))
    for c in range(6):
        late.append(copies.start(raw[c].at[0, outer], face.at[c]))
        late.append(copies.start(other[c].at[0, outer], face.at[6 + c]))
    late.append(copies.start(medium.at[outer], face_code))
    early.append(copies.start(slab_in, slab))
    for s in range(2):
        which = k if s == 0 else 1 - k
        kerr, two, free = table[which, 0], table[which, 1], table[which, 2]
        for n, value in enumerate((kerr, two, 0.5 * two, 0.5 * free)):
            coef[4 * s + n] = jnp.full((8, plan.lanes), value)
    last.append(copies.start(coef, outs[-1]))
    wait(early)
    page = slab[...]
    face[13] = jnp.broadcast_to(page[None, 0:1], (DEEP, plan.cols, plan.lanes))
    face[13, 0, 0:8, :] = page
    for n in range(nside):
        for q in range(plan.own // 2):
            strips[n, 13, q] = page

    def fill(slot, low):
        def rows(q, _):
            for h in range(2):
                half = slice(4 * h, 4 * h + 4)
                for c in range(12):
                    strips[slot, c, q, half, :] = edge[slot, c, 2 * q + h, low : low + 4, :]
                code = edge_code[slot, 2 * q + h, low : low + 4, :]
                strips[slot, 12, q, half, :] = code.astype(F32)
            return 0

        lax.fori_loop(0, plan.own // 2, rows, 0)

    each_side(plan, lambda slot, side: fill(slot, 4 if plan.paired == (side == "high") else 0))
    send_strips(plan, copies, last, strips, outs[1:-1])
    wait(late)
    face[12] = face_code[...].astype(F32)
    last.append(copies.start(face, outs[0]))
    wait(last)


def send_strips(plan, copies, started, strips, outs):
    k = lax.axis_index("af")
    half, top = DEEP // 2, (plan.own - DEEP) // 2
    for n in range(len(plan.sides)):
        whole, inner, corner = outs[3 * n : 3 * n + 3]
        started.append(copies.start(strips.at[n], whole))
        started.append(copies.start(strips.at[n, :, pl.ds(top * (1 - k), half)], inner))
        started.append(copies.start(strips.at[n, :, pl.ds(top * k, half)], corner))


def strip_shapes(plan, comps):
    shapes = []
    for _ in plan.sides:
        for rows in (plan.own, DEEP, DEEP):
            shapes.append((comps, rows // 2, 8, plan.lanes))
    return shapes


def pack(plan, raw, other, medium, slab, table):
    wide = (plan.cols, plan.lanes)
    nside = len(plan.sides)
    scratch = [
        pltpu.VMEM((nside, 12, plan.own, 8, plan.lanes), F32),
        pltpu.VMEM((nside, plan.own, 8, plan.lanes), jnp.int32),
        pltpu.VMEM((14, DEEP) + wide, F32),
        pltpu.VMEM((DEEP,) + wide, jnp.int32),
        pltpu.VMEM((nside, 14, plan.own // 2, 8, plan.lanes), F32),
        pltpu.VMEM((8, plan.lanes), F32),
        pltpu.VMEM((8, 8, plan.lanes), F32),
    ]
    return call(
        plan,
        pack_kernel,
        "pack",
        [(14, DEEP) + wide] + strip_shapes(plan, 14) + [(8, 8, plan.lanes)],
        [HBM] * 6 + [ANY] * 6 + [HBM, ANY, SMEM],
        scratch,
        16 * nside + 16,
        moved=4_000_000,
    )(*raw, *other, medium, slab, table)


def clear(plan, old, new, code):
    zero = jnp.zeros((8, plan.lanes), F32)

    def halo(slot, side):
        tile = plan.tiles - 1 if side == "high" else 0

        def one(p, _):
            for ref in list(old) + code:
                ref[p, 8 * tile : 8 * tile + 8, :] = zero
            return 0

        lax.fori_loop(0, plan.ext, one, 0)

    each_side(plan, halo)

    def above(p, _):
        for c in (1, 2, 7, 8):
            for ref in (old[c], new[c]):
                ref[p, plan.width : plan.width + 8, :] = zero
        return 0

    lax.fori_loop(0, plan.ext, above, 0)
    for c, ref in enumerate(new):
        plane = DEEP + plan.own if c % 6 < 3 else DEEP - 1
        for t in range(plan.tiles):
            ref[plane, 8 * t : 8 * t + 8, :] = zero


def strip_row(plan, side):
    if side == "low":
        return 4
    return plan.cols if plan.paired else 8 + plan.cols


def spread_strip(refs, strip, at, plane, pairs):
    def one(q, _):
        for c, ref in refs:
            for h in range(2):
                ref[plane + 2 * q + h, at : at + 4, :] = strip[c, q, 4 * h : 4 * h + 4, :]
        return 0

    lax.fori_loop(0, pairs, one, 0)


def substeps(plan, first, second, base, silicon, charge, gen, coef):
    lanes = plan.lanes
    tile = (8, lanes)
    lane = lax.broadcasted_iota(jnp.int32, tile, 1)
    row = lax.broadcasted_iota(jnp.int32, tile, 0)
    keep_up, keep_down, at_top = lane < lanes - 1, lane > 0, row == 0
    z, x, k = (lax.axis_index(a) for a in LINE)
    at_low = jnp.logical_and(z == 0, k == 0)
    at_high = jnp.logical_and(z == plan.gz - 1, k == 1)

    def up(v):
        return jnp.where(keep_up, pltpu.roll(v, lanes - 1, 1), 0.0)

    def down(v):
        return jnp.where(keep_down, pltpu.roll(v, 1, 1), 0.0)

    def edge_mask(t):
        if plan.paired or t not in (0, plan.tiles - 1):
            return None
        off = (x == 0) if t == 0 else (x == plan.gx - 1)
        return jnp.where(off, 0.0, 1.0)

    def new_magnetic(old, new, s, p, t):
        ex, ey, ez, hx, hy, hz = old[6 * s : 6 * s + 6]
        here, beside = slice(8 * t, 8 * t + 8), slice(8 * t + 1, 8 * t + 9)
        vx, vy, vz = ex[p, here, :], ey[p, here, :], ez[p, here, :]
        nx = hx[p, here, :] - COURANT * ((up(vz) - vz) - (ey[p + 1, here, :] - vy))
        ny = hy[p, here, :] - COURANT * ((ex[p + 1, here, :] - vx) - (ez[p, beside, :] - vz))
        nz = hz[p, here, :] - COURANT * ((ey[p, beside, :] - vy) - (up(vx) - vx))
        mask = edge_mask(t)
        if mask is not None:
            nx, ny, nz = nx * mask, ny * mask, nz * mask
        new[6 * s + 3][p, here, :] = nx
        new[6 * s + 4][p, here, :] = ny
        new[6 * s + 5][p, here, :] = nz
        return vx, vy, vz, nx, ny, nz

    def full_plane(old, new, p):
        coarse = p // BLOCK_FACTOR
        kerr, two = (coef[0], coef[4]), (coef[1], coef[5])
        half_two, half_free = (coef[2], coef[6]), (coef[3], coef[7])
        zero = jnp.zeros(tile, F32)
        rolled = [[zero, zero], [zero, zero]]
        for t in range(plan.tiles):
            here = slice(8 * t, 8 * t + 8)
            back = [[new[6 * s + c][p - 1, here, :] for c in (3, 4)] for s in range(2)]
            vals = [new_magnetic(old, new, s, p, t) for s in range(2)]
            strength = [v[0] * v[0] + v[1] * v[1] + v[2] * v[2] for v in vals]
            is_silicon = silicon[p, here, :]
            total = (strength[0] + strength[1]) * is_silicon
            carriers = charge[coarse, here, :] * is_silicon
            ground = base[p, here, :]
            gen[p, here, :] += (two[0] * strength[0] + two[1] * strength[1]) * total
            mask = edge_mask(t)
            for s in range(2):
                vx, vy, vz, nx, ny, nz = vals[s]
                loss = half_two[s] * total + half_free[s] * carriers
                perm = ground + kerr[s] * total
                divisor = perm + loss
                inv = pl.reciprocal(divisor, approx=True)
                inv = inv * (2.0 - divisor * inv)
                keep = (perm - loss) * inv
                push = COURANT * inv
                if mask is not None:
                    push = push * mask
                turn_y, turn_z = pltpu.roll(ny, 1, 0), pltpu.roll(nz, 1, 0)
                left_y = jnp.where(at_top, rolled[s][0], turn_y)
                left_z = jnp.where(at_top, rolled[s][1], turn_z)
                rolled[s] = [turn_y, turn_z]
                curl_x = (nz - down(nz)) - (ny - back[s][1])
                curl_y = (nx - back[s][0]) - (nz - left_z)
                curl_z = (ny - left_y) - (nx - down(nx))
                new[6 * s][p, here, :] = keep * vx + push * curl_x
                new[6 * s + 1][p, here, :] = keep * vy + push * curl_y
                new[6 * s + 2][p, here, :] = keep * vz + push * curl_z

    def substep(old, new, n):
        @pl.when(jnp.logical_not(at_low))
        def _():
            for t in range(plan.tiles):
                for s in range(2):
                    new_magnetic(old, new, s, n, t)

        begin = jnp.where(at_low, DEEP, n + 1)
        end = jnp.where(at_high, DEEP + plan.own, plan.ext - 1 - n)

        def step(p, _):
            full_plane(old, new, p)
            return 0

        lax.fori_loop(begin, end, step, 0)

    def pair(m, _):
        substep(first, second, 2 * m)
        substep(second, first, 2 * m + 1)
        return 0

    lax.fori_loop(0, SUBSTEPS // 2, pair, 0)


def set_media(plan, code, base, silicon):
    def one(p, _):
        for t in range(plan.tiles):
            here = slice(8 * t, 8 * t + 8)
            v = code[p, here, :]
            base[p, here, :] = jnp.where(v == 0.0, SILICON_PERM, jnp.where(v == 1.0, OXIDE_PERM, 1.0))
            silicon[p, here, :] = jnp.where(v == 0.0, 1.0, 0.0)
        return 0

    lax.fori_loop(0, plan.ext, one, 0)


def clear_generation(plan, gen):
    def one(p, _):
        gen[p] = jnp.zeros((plan.rows, plan.lanes), F32)
        return 0

    lax.fori_loop(DEEP, DEEP + plan.own, one, 0)


def sum_generation(plan, gen, message):
    blocks = plan.cols // BLOCK_FACTOR
    lane = lax.broadcasted_iota(jnp.int32, (blocks, plan.lanes), 1)
    across = plan.own_rows()
    out = jnp.zeros((blocks, plan.lanes), F32)
    for a in range(plan.own // BLOCK_FACTOR):
        p = DEEP + BLOCK_FACTOR * a
        rows = (gen[p, across, :] + gen[p + 1, across, :]) + (
            gen[p + 2, across, :] + gen[p + 3, across, :]
        )
        cells = rows.reshape(blocks, BLOCK_FACTOR, plan.lanes).sum(1)
        mean = cells.sum(1, keepdims=True) * (1.0 / (BLOCK_FACTOR * BLOCK_FACTOR * plan.lanes))
        out = jnp.where(lane == a, mean, out)
    message[...] = out


def round_scratch(plan):
    wide = (plan.ext, plan.rows, plan.lanes)
    return [pltpu.VMEM(wide, F32)] * 27 + [
        pltpu.VMEM((plan.ext // BLOCK_FACTOR, plan.width, plan.lanes), F32),
        pltpu.VMEM(generation_shape(plan)[1:], F32),
        pltpu.VMEM((8, 8, plan.lanes), F32),
        pltpu.VMEM(wide, F32),
    ]


def round_flops(plan):
    return SUBSTEPS * plan.ext * plan.width * plan.lanes * 150


def generation_shape(plan, rows=0):
    return (plan.devices, plan.cols // BLOCK_FACTOR + rows, plan.lanes)


def place_strips(plan, old, code, strips):
    k = lax.axis_index("af")
    outward, inner = plan.part * k, plan.part * (1 - k)

    def place(slot, side):
        whole, beside, corner = strips[3 * slot : 3 * slot + 3]
        at = strip_row(plan, side)
        same = list(enumerate(list(old) + code))
        flipped = list(enumerate(list(old[6:]) + list(old[:6]) + code))
        spread_strip(same, whole, at, DEEP, plan.own // 2)
        spread_strip(flipped, beside, at, inner, DEEP // 2)
        spread_strip(flipped, corner, at, outward, DEEP // 2)

    each_side(plan, place)


def send_generation(plan, copies, started, gen, message, gen_out):
    sum_generation(plan, gen, message)
    for d in range(plan.devices):
        started.append(copies.start(message, gen_out.at[d, pl.ds(0, plan.cols // BLOCK_FACTOR)]))


def charge_from_slabs(plan, charge, mine, across, chip, corner):
    across, chip = chip, across
    x, k = lax.axis_index("gx"), lax.axis_index("af")
    slab = plan.slab
    left = jnp.where(x == 0, mine, across)
    right = jnp.where(x == 0, across, mine)
    beyond = jnp.where(x != k, chip, corner)
    body = jnp.where(k == 0, left, right)
    before = jnp.where(k == 0, beyond, left)[slab - 1 : slab]
    after = jnp.where(k == 0, right, beyond)[0:1]
    skip = (plan.cols - 8) // BLOCK_FACTOR
    for a in range(slab + 2):
        row = before if a == 0 else after if a == slab + 1 else body[a - 1 : a]
        row = jnp.broadcast_to(row, (8, plan.lanes))
        row = jnp.where(x == 0, row, pltpu.roll(row, plan.lanes - skip, 1))
        for c in range(plan.width // BLOCK_FACTOR):
            value = jnp.broadcast_to(row[0:4, c : c + 1], (4, plan.lanes))
            charge[a, 4 * c : 4 * c + 4, :] = value


def first_kernel(plan, *refs):
    nside = len(plan.sides)
    strips_in = refs[: 3 * nside]
    z_in, raw, other = refs[3 * nside], refs[1 + 3 * nside : 7 + 3 * nside], refs[7 + 3 * nside : 13 + 3 * nside]
    medium, slab_in, under_in, coef_in = refs[13 + 3 * nside : 17 + 3 * nside]
    outs = refs[17 + 3 * nside : 22 + 6 * nside]
    own_out, z_out, core_out, gen_out, code_out = outs[:5]
    rest = refs[22 + 6 * nside :]
    old, new, (base, silicon, gen, charge, message, coef, code) = rest[:12], rest[12:24], rest[24:31]
    codes, strips, (strip_mine, slabs, sems) = rest[31], rest[32 : 32 + 3 * nside], rest[-3:]
    copies = Copies(sems)
    k = lax.axis_index("af")
    near = DEEP * (1 - k)
    far = plan.part * k
    across = plan.own_rows()
    here, there = pl.ds(near, plan.part), pl.ds(far, DEEP)
    mine = pl.ds((plan.own - DEEP) * k, plan.part)
    early = [copies.start(medium.at[mine], codes)]
    early.append(copies.start(z_in.at[12], code.at[there, across]))
    early.append(copies.start(slab_in, slabs.at[0]))
    if plan.paired:
        early.append(copies.start(z_in.at[13, 0, pl.ds(0, 8)], slabs.at[1]))
    else:
        early.append(copies.start(under_in, charge))
    early.append(copies.start(coef_in, coef))
    for source, target in zip(strips_in, strips):
        early.append(copies.start(source, target))
    late = []
    for c in range(6):
        late.append(copies.start(raw[c].at[0, mine], old[c].at[here, across]))
        late.append(copies.start(other[c].at[0, mine], old[6 + c].at[here, across]))
    for c in range(12):
        late.append(copies.start(z_in.at[(c + 6) % 12], old[c].at[there, across]))
    clear(plan, old, new, [code])
    clear_generation(plan, gen)
    wait(early)

    def settle(p, _):
        code[near + p, across, :] = codes[p].astype(F32)
        return 0

    lax.fori_loop(0, plan.part, settle, 0)
    place_strips(plan, old, [code], strips)
    set_media(plan, code, base, silicon)
    if plan.paired:
        charge_from_slabs(plan, charge, slabs[0], slabs[1], strips[0][13, 0], strips[2][13, 0])
    wait(late)
    substeps(plan, old, new, base, silicon, charge, gen, coef)
    copies = Copies(sems)
    late = []

    def gather(slot, side):
        high_end = (side == "high") if plan.paired else (side == "low")
        low = 0 if plan.paired and side == "high" else 8
        at = low + plan.cols - 4 if high_end else low

        def one(q, _):
            for c in range(12):
                for h in range(2):
                    strip_mine[slot, c, q, 4 * h : 4 * h + 4, :] = old[c][
                        DEEP + 2 * q + h, at : at + 4, :
                    ]
            return 0

        lax.fori_loop(0, plan.own // 2, one, 0)

    toward = DEEP + (plan.own - DEEP) * k
    inward = DEEP + (plan.own - DEEP) * (1 - k)
    for c in range(12):
        late.append(copies.start(old[c].at[pl.ds(toward, DEEP), across], z_out.at[c]))
        late.append(copies.start(old[c].at[pl.ds(inward, DEEP), across], core_out.at[c]))
        late.append(copies.start(old[c].at[pl.ds(DEEP, plan.own), across], own_out.at[c]))
    late.append(copies.start(code, code_out))
    slab_rows = pl.ds(plan.cols // BLOCK_FACTOR, 8)
    for d in range(plan.devices):
        late.append(copies.start(slabs.at[0], gen_out.at[d, slab_rows]))
    each_side(plan, gather)
    send_strips(plan, copies, late, strip_mine, outs[5:])
    send_generation(plan, copies, late, gen, message, gen_out)
    wait(late)


def first_round(plan, strips, z_in, raw, other, medium, slab, under, coef):
    wide = (plan.cols, plan.lanes)
    nside = len(plan.sides)
    shapes = [
        (12, plan.own) + wide,
        (12, DEEP) + wide,
        (12, DEEP) + wide,
        generation_shape(plan, 8),
        (plan.ext, plan.rows, plan.lanes),
    ] + strip_shapes(plan, 12)
    scratch = round_scratch(plan) + [pltpu.VMEM((plan.part,) + wide, jnp.int32)]
    scratch += [pltpu.VMEM(s.shape, F32) for s in strips]
    scratch += [
        pltpu.VMEM((nside, 12, plan.own // 2, 8, plan.lanes), F32),
        pltpu.VMEM((2, 8, plan.lanes), F32),
    ]
    return call(
        plan,
        first_kernel,
        "first_round",
        shapes,
        [ANY] * (1 + 3 * nside) + [HBM] * 6 + [ANY] * 6 + [HBM, ANY, ANY, HBM],
        scratch,
        40 + 3 * nside + 2 * plan.devices,
        round_flops(plan),
        10_000_000,
    )(*strips, z_in, *raw, *other, medium, slab, under, coef)


def second_kernel(plan, *refs):
    nside = len(plan.sides)
    strips_in = refs[: 3 * nside]
    z_in, core_in, own_in, code_in, charge_in, coef_in = refs[3 * nside : 6 + 3 * nside]
    outs = refs[6 + 3 * nside : 14 + 3 * nside]
    kept, sent, gen_out = outs[:6], outs[6], outs[7]
    rest = refs[14 + 3 * nside :]
    old, new, (base, silicon, gen, charge, message, coef, code) = rest[:12], rest[12:24], rest[24:31]
    strips, sems = rest[31:-1], rest[-1]
    copies = Copies(sems)
    k = lax.axis_index("af")
    across = plan.own_rows()
    outward = plan.part * k
    inner = plan.part * (1 - k)
    early = [copies.start(code_in, code), copies.start(charge_in, charge)]
    early.append(copies.start(coef_in, coef))
    for source, target in zip(strips_in, strips):
        early.append(copies.start(source, target))
    late = []
    for c in range(12):
        flip = (c + 6) % 12
        late.append(copies.start(own_in.at[c], old[c].at[pl.ds(DEEP, plan.own), across]))
        late.append(copies.start(z_in.at[flip], old[c].at[pl.ds(outward, DEEP), across]))
        late.append(copies.start(core_in.at[flip], old[c].at[pl.ds(inner, DEEP), across]))
    clear(plan, old, new, [])
    clear_generation(plan, gen)
    wait(early)
    place_strips(plan, old, [], strips)
    set_media(plan, code, base, silicon)
    wait(late)
    substeps(plan, old, new, base, silicon, charge, gen, coef)
    copies = Copies(sems)
    late = []
    for c in range(6):
        late.append(copies.start(old[6 + c].at[pl.ds(DEEP, plan.own), across], sent.at[c]))
    for c in range(6):
        target = kept[c].at[0, pl.ds(plan.own * k, plan.own)]
        late.append(copies.start(old[c].at[pl.ds(DEEP, plan.own), across], target))
    send_generation(plan, copies, late, gen, message, gen_out)
    wait(late)


def second_round(plan, strips, z_in, core_in, own_in, code, charge, coef):
    wide = (plan.cols, plan.lanes)
    nside = len(plan.sides)
    shapes = [(1, plan.planes) + wide] * 6 + [(6, plan.own) + wide, generation_shape(plan)]
    scratch = round_scratch(plan) + [pltpu.VMEM(s.shape, F32) for s in strips]
    return call(
        plan,
        second_kernel,
        "second_round",
        shapes,
        [ANY] * (2 + 3 * nside) + [HBM] * 4,
        scratch,
        39 + 3 * nside + plan.devices,
        round_flops(plan),
        10_000_000,
    )(*strips, z_in, core_in, own_in, code, charge, coef)


def join_kernel(plan, *refs):
    got, outs, (half, sems) = refs[6], refs[7:13], refs[13:]
    copies = Copies(sems)
    rows = pl.ds(plan.own * (1 - lax.axis_index("af")), plan.own)
    early = [copies.start(got.at[c], half.at[c]) for c in range(6)]
    late = []
    for c in range(6):
        early[c].wait()
        late.append(copies.start(half.at[c], outs[c].at[0, rows]))
    wait(late)


def join(plan, halves, got):
    shapes = [h.shape for h in halves]
    aliases = {c: c for c in range(6)}
    scratch = [pltpu.VMEM(got.shape, F32)]
    return call(
        plan, join_kernel, "join", shapes, [HBM] * 6 + [ANY], scratch, 12, moved=3_000_000, aliases=aliases
    )(*halves, got)


def under_cells(plan, grid, charge):
    z, x, k = (lax.axis_index(a) for a in LINE)
    for a in range(plan.ext // BLOCK_FACTOR):
        top = (plan.planes * z + plan.own * k - DEEP) // BLOCK_FACTOR + a
        top = 1 + jnp.clip(top, 0, plan.grid_rows - 1)
        for c in range(plan.width // BLOCK_FACTOR):
            left = (plan.cols * x - plan.first_row()) // BLOCK_FACTOR + c
            left = 8 + jnp.clip(left, 0, plan.grid_cols - 1)
            value = grid[top, pl.ds(left, 1), :]
            charge[a, 4 * c : 4 * c + 4, :] = jnp.broadcast_to(value, (4, plan.lanes))


def grid_shape(plan):
    return (plan.grid_rows + 2, plan.grid_cols + 16, plan.lanes)


def charge_shape(plan):
    return (plan.ext // BLOCK_FACTOR, plan.width, plan.lanes)


def spread_kernel(plan, density, charge_out, grid, charge, sems):
    copies = Copies(sems)
    rows, cols, lanes = plan.grid_rows, plan.grid_cols, plan.lanes

    def clean(i, _):
        for c in range(0, cols + 16, 8):
            grid[i, c : c + 8, :] = jnp.zeros((8, lanes), F32)
        return 0

    lax.fori_loop(0, rows + 2, clean, 0)

    def read(i, _):
        for c in range(cols):
            value = density[i // plan.slab, i % plan.slab, c]
            grid[i + 1, 8 + c : 9 + c, :] = jnp.full((1, lanes), value)
        return 0

    lax.fori_loop(0, rows, read, 0)
    under_cells(plan, grid, charge)
    copies.start(charge, charge_out).wait()


def spread(plan, density):
    scratch = [pltpu.VMEM(grid_shape(plan), F32), pltpu.VMEM(charge_shape(plan), F32)]
    shapes = [charge_shape(plan)]
    return call(plan, spread_kernel, "spread", shapes, [SMEM], scratch, 1, 10_000, 1_000_000)(density)


def carrier_kernel(plan, last, *refs):
    gens_in, refs = refs[0], refs[1:]
    if last:
        density_in, refs = refs[0], refs[1:]
    outs = refs[:1] if last else refs[:2]
    gens, one, two, source, charge, slab_out, sems = refs[len(outs) :]
    copies = Copies(sems)
    rows, cols, lanes = plan.grid_rows, plan.grid_cols, plan.lanes
    z, x = lax.axis_index("gz"), lax.axis_index("gx")
    blocks, own = plan.cols // BLOCK_FACTOR, plan.own // BLOCK_FACTOR
    early = [copies.start(gens_in, gens)]
    if last:
        early.append(copies.start(density_in, one))
    zero = jnp.zeros((8, lanes), F32)
    both = (two,) if last else (one, two)

    def clean(i, _):
        for ref in both:
            ref[i, 0:8, :] = zero
            ref[i, 8 + cols : 16 + cols, :] = zero
        return 0

    lax.fori_loop(0, rows + 2, clean, 0)
    for ref in both:
        for i in (0, rows + 1):
            for c in range(8, 8 + cols, 8):
                ref[i, c : c + 8, :] = zero
    wait(early)
    diagonal = lax.broadcasted_iota(jnp.int32, (cols, lanes), 0) == lax.broadcasted_iota(
        jnp.int32, (cols, lanes), 1
    )
    if not last:

        def turn(d, _):
            for r in range(plan.slab):
                row = jnp.broadcast_to(gens[2 * d, blocks + r : blocks + r + 1, :], (cols, lanes))
                upright = jnp.where(diagonal, row, 0.0).sum(1, keepdims=True)
                one[1 + d * plan.slab + r, 8 : 8 + cols, :] = jnp.broadcast_to(upright, (cols, lanes))
            return 0

        lax.fori_loop(0, plan.gz * plan.gx, turn, 0)

    def unpack(line, _):
        for dx in range(plan.gx):
            for dk in range(2):
                tile = gens[(line * plan.gx + dx) * 2 + dk, 0:blocks, :]
                for a in range(own):
                    source[(line * 2 + dk) * own + a, blocks * dx : blocks * dx + blocks, :] = (
                        jnp.broadcast_to(SOURCE_FACTOR * tile[:, a : a + 1], (blocks, lanes))
                    )
        return 0

    lax.fori_loop(0, plan.gz, unpack, 0)

    def step(old, new):
        def row(m, _):
            for h in range(4):
                i = 4 * m + h
                for c in range(8, 8 + cols, 8):
                    now, before = old[i + 1, c : c + 8, :], old[i, c : c + 8, :]
                    around = (
                        old[i + 2, c : c + 8, :]
                        + before
                        + old[i + 1, c + 1 : c + 9, :]
                        + old[i + 1, c - 1 : c + 7, :]
                        - 4.0 * now
                    )
                    new[i + 1, c : c + 8, :] = (
                        now
                        + SPREAD_COEFF * around
                        - MOBILITY_TERM * (now - before)
                        - LIFETIME_DECAY * now
                        + source[i, c - 8 : c, :]
                    )
            return 0

        lax.fori_loop(0, rows // 4, row, 0)

    def pair(_, carry):
        step(one, two)
        step(two, one)
        return carry

    lax.fori_loop(0, CSTEPS // 2, pair, 0)
    if last:
        for r in range(plan.slab):
            upright = one[1 + (z * plan.gx + x) * plan.slab + r, 8 : 8 + cols, :]
            flat = jnp.where(diagonal, upright, 0.0).sum(0, keepdims=True)
            slab_out[r : r + 1, :] = flat
        copies.start(slab_out, outs[0]).wait()
        return
    under_cells(plan, one, charge)
    wait([copies.start(one, outs[0]), copies.start(charge, outs[1])])


def carriers(plan, last, *arrays):
    grid, lanes = grid_shape(plan), plan.lanes
    shapes = [(8, lanes)] if last else [grid, charge_shape(plan)]
    scratch = [
        pltpu.VMEM(arrays[0].shape, F32),
        pltpu.VMEM(grid, F32),
        pltpu.VMEM(grid, F32),
        pltpu.VMEM((plan.grid_rows, plan.grid_cols, lanes), F32),
        pltpu.VMEM(charge_shape(plan), F32),
        pltpu.VMEM((8, lanes), F32),
    ]
    return call(
        plan,
        lambda plan, *refs: carrier_kernel(plan, last, *refs),
        "carriers",
        shapes,
        [ANY] + [HBM] * (len(arrays) - 1),
        scratch,
        4,
        2_000_000,
        1_000_000,
    )(*arrays)


def local(ex, ey, ez, hx, hy, hz, medium, table, density):
    raw = (ex, ey, ez, hx, hy, hz)
    plan = Plan(*medium.shape, density.shape[0])

    def send(message, target):
        return lax.ppermute(message, LINE, line_pairs(plan, target))

    def everywhere(message, axes):
        return lax.all_to_all(message, axes, split_axis=0, concat_axis=0, tiled=True)

    core = lambda z, x, k: (z, x, 1 - k)
    beyond = lambda z, k: z - 1 if k == 0 else z + 1

    def exchange(z_msg, strips):
        got = []
        for n, side in enumerate(plan.sides):
            to = functools.partial(across_step, side)
            whole, inner, corner = strips[3 * n : 3 * n + 3]
            got.append(send(whole, lambda z, x, k: (z, to(x), k)))
            got.append(send(inner, lambda z, x, k: (z, to(x), 1 - k)))
            got.append(send(corner, lambda z, x, k: (beyond(z, k), to(x), 1 - k)))
        return send(z_msg, lambda z, x, k: (beyond(z, k), x, 1 - k)), got

    other = [send(r, core) for r in raw]
    slab = jnp.pad(density, ((0, 8 - plan.slab), (0, plan.lanes - plan.grid_cols)))
    packed = pack(plan, raw, other, medium, slab, table)
    z_in, strips = exchange(packed[0], packed[1:-1])
    coef = packed[-1]
    under = slab
    if not plan.paired:
        tiles = plan.gz * plan.gx
        slabs = everywhere(jnp.broadcast_to(density, (tiles,) + density.shape), ("gz", "gx"))
        (under,) = spread(plan, slabs)
    outs = first_round(plan, strips, z_in, raw, other, medium, slab, under, coef)
    own, z_msg, core_msg, gens, code = outs[:5]
    gens = everywhere(gens, LINE)
    z_in, strips = exchange(z_msg, outs[5:])
    core_in = send(core_msg, core)
    grid, charge = carriers(plan, False, gens)
    outs = second_round(plan, strips, z_in, core_in, own, code, charge, coef)
    halves, sent, gens = outs[:6], outs[6], outs[7]
    gens = everywhere(gens, LINE)
    got = send(sent, core)
    (new_slab,) = carriers(plan, True, gens, grid)
    new_slab = new_slab[: plan.slab, : plan.grid_cols]
    return tuple(join(plan, halves, got)) + (new_slab,)


def solution(mesh):
    field = P("af", ("group", "gz"), "gx", None)
    slabs = P(("group", "gz", "gx"), None)
    in_specs = (field,) * 6 + (P(("group", "gz"), "gx", None), P(), slabs)
    out_specs = (field,) * 6 + (slabs,)
    return jax.shard_map(local, mesh=mesh, in_specs=in_specs, out_specs=out_specs, check_vma=False)
```

```python
import functools

import jax
import jax.numpy as jnp
from jax import lax
from jax.experimental import pallas as pl
from jax.experimental.pallas import tpu as pltpu
from jax.sharding import PartitionSpec as P

BLOCK_FACTOR = 4
SUBSTEPS = 4
ROUNDS = 2
CSTEPS = 8

COURANT = 0.5
SILICON_PERM = 12.1
OXIDE_PERM = 2.1
SPREAD_COEFF = 0.2
MOBILITY_TERM = 0.1
LIFETIME_DECAY = 0.05
SOURCE_FACTOR = 0.02

DEEP = SUBSTEPS
LINE = ("gz", "gx", "af")
HBM = pl.BlockSpec(memory_space=pltpu.HBM)
ANY = pl.BlockSpec(memory_space=pl.ANY)
SMEM = pl.BlockSpec(memory_space=pltpu.SMEM)
VMEM_LIMIT = 24 * 1024 * 1024
F32 = jnp.float32


class Plan:
    def __init__(self, planes, cols, lanes, slab):
        self.gz = lax.axis_size("gz")
        self.gx = lax.axis_size("gx")
        self.planes, self.cols, self.lanes, self.slab = planes, cols, lanes, slab
        self.own = planes // 2
        self.part = self.own + DEEP
        self.ext = self.own + 2 * DEEP
        self.paired = self.gx == 2
        self.sides = ("face",) if self.paired else ("low", "high")
        self.width = cols + (8 if self.paired else 16)
        self.rows = self.width + 8
        self.tiles = self.width // 8
        self.grid_rows = planes * self.gz // BLOCK_FACTOR
        self.grid_cols = cols * self.gx // BLOCK_FACTOR
        self.devices = self.gz * self.gx * 2

    def first_row(self):
        return 8 * lax.axis_index("gx") if self.paired else 8

    def own_rows(self):
        return pl.ds(pl.multiple_of(self.first_row(), 8), self.cols)


def each_side(plan, act):
    if plan.paired:
        across = lax.axis_index("gx")

        @pl.when(across == 0)
        def _():
            act(0, "high")

        @pl.when(across == 1)
        def _():
            act(0, "low")
    else:
        act(0, "low")
        act(1, "high")


def line_pairs(plan, target):
    pairs = []
    for z in range(plan.gz):
        for x in range(plan.gx):
            for k in range(2):
                tz, tx, tk = target(z, x, k)
                if 0 <= tz < plan.gz and 0 <= tx < plan.gx:
                    pairs.append(((z * plan.gx + x) * 2 + k, (tz * plan.gx + tx) * 2 + tk))
    return pairs


def across_step(side, x):
    if side == "face":
        return 1 - x
    return x + 1 if side == "low" else x - 1


class Copies:
    def __init__(self, sems):
        self.sems, self.made = sems, 0

    def start(self, source, target):
        copy = pltpu.make_async_copy(source, target, self.sems.at[self.made])
        self.made += 1
        copy.start()
        return copy


def wait(copies):
    for copy in copies:
        copy.wait()


def call(plan, body, name, shapes, in_specs, scratch, copies, flops=0, moved=0, aliases=None):
    kernel = pl.pallas_call(
        functools.partial(body, plan),
        out_shape=[pltpu.HBM(s, F32) for s in shapes],
        in_specs=in_specs,
        out_specs=[HBM] * len(shapes),
        scratch_shapes=scratch + [pltpu.SemaphoreType.DMA((copies,))],
        input_output_aliases=aliases or {},
        compiler_params=pltpu.CompilerParams(vmem_limit_bytes=VMEM_LIMIT),
        cost_estimate=pl.CostEstimate(flops=flops, bytes_accessed=moved, transcendentals=0),
        name=name,
    )

    def run(*args):
        placed = []
        for arg, spec in zip(args, in_specs):
            in_hbm = spec.memory_space is pltpu.HBM
            placed.append(pltpu.with_memory_space_constraint(arg, pltpu.HBM) if in_hbm else arg)
        return kernel(*placed)

    return run


def pack_kernel(plan, *refs):
    raw, other, medium, nside = refs[:6], refs[6:12], refs[12], len(plan.sides)
    slab_in, table = refs[13:15]
    outs = refs[15 : 17 + 3 * nside]
    edge, edge_code, face, face_code, strips, slab, coef, sems = refs[17 + 3 * nside :]
    copies = Copies(sems)
    k = lax.axis_index("af")
    mine = pl.ds(plan.own * k, plan.own)
    outer = pl.ds((plan.planes - DEEP) * k, DEEP)
    if plan.paired:
        tile_rows = [pl.multiple_of((plan.cols - 8) * (1 - lax.axis_index("gx")), 8)]
    else:
        tile_rows = [plan.cols - 8, 0]
    early, late, last = [], [], []
    for n, row in enumerate(tile_rows):
        for c in range(6):
            side = pl.ds(row, 8)
            early.append(copies.start(raw[c].at[0, mine, side, :], edge.at[n, c]))
            early.append(copies.start(other[c].at[0, mine, side, :], edge.at[n, 6 + c]))
        early.append(copies.start(medium.at[mine, pl.ds(row, 8), :], edge_code.at[n]))
    for c in range(6):
        late.append(copies.start(raw[c].at[0, outer], face.at[c]))
        late.append(copies.start(other[c].at[0, outer], face.at[6 + c]))
    late.append(copies.start(medium.at[outer], face_code))
    early.append(copies.start(slab_in, slab))
    for s in range(2):
        which = k if s == 0 else 1 - k
        kerr, two, free = table[which, 0], table[which, 1], table[which, 2]
        for n, value in enumerate((kerr, two, 0.5 * two, 0.5 * free)):
            coef[4 * s + n] = jnp.full((8, plan.lanes), value)
    last.append(copies.start(coef, outs[-1]))
    wait(early)
    page = slab[...]
    face[13] = jnp.broadcast_to(page[None, 0:1], (DEEP, plan.cols, plan.lanes))
    face[13, 0, 0:8, :] = page
    for n in range(nside):
        for q in range(plan.own // 2):
            strips[n, 13, q] = page

    def fill(slot, low):
        def rows(q, _):
            for h in range(2):
                half = slice(4 * h, 4 * h + 4)
                for c in range(12):
                    strips[slot, c, q, half, :] = edge[slot, c, 2 * q + h, low : low + 4, :]
                code = edge_code[slot, 2 * q + h, low : low + 4, :]
                strips[slot, 12, q, half, :] = code.astype(F32)
            return 0

        lax.fori_loop(0, plan.own // 2, rows, 0)

    each_side(plan, lambda slot, side: fill(slot, 4 if plan.paired == (side == "high") else 0))
    send_strips(plan, copies, last, strips, outs[1:-1])
    wait(late)
    face[12] = face_code[...].astype(F32)
    last.append(copies.start(face, outs[0]))
    wait(last)


def send_strips(plan, copies, started, strips, outs):
    k = lax.axis_index("af")
    half, top = DEEP // 2, (plan.own - DEEP) // 2
    for n in range(len(plan.sides)):
        whole, inner, corner = outs[3 * n : 3 * n + 3]
        started.append(copies.start(strips.at[n], whole))
        started.append(copies.start(strips.at[n, :, pl.ds(top * (1 - k), half)], inner))
        started.append(copies.start(strips.at[n, :, pl.ds(top * k, half)], corner))


def strip_shapes(plan, comps):
    shapes = []
    for _ in plan.sides:
        for rows in (plan.own, DEEP, DEEP):
            shapes.append((comps, rows // 2, 8, plan.lanes))
    return shapes


def pack(plan, raw, other, medium, slab, table):
    wide = (plan.cols, plan.lanes)
    nside = len(plan.sides)
    scratch = [
        pltpu.VMEM((nside, 12, plan.own, 8, plan.lanes), F32),
        pltpu.VMEM((nside, plan.own, 8, plan.lanes), jnp.int32),
        pltpu.VMEM((14, DEEP) + wide, F32),
        pltpu.VMEM((DEEP,) + wide, jnp.int32),
        pltpu.VMEM((nside, 14, plan.own // 2, 8, plan.lanes), F32),
        pltpu.VMEM((8, plan.lanes), F32),
        pltpu.VMEM((8, 8, plan.lanes), F32),
    ]
    return call(
        plan,
        pack_kernel,
        "pack",
        [(14, DEEP) + wide] + strip_shapes(plan, 14) + [(8, 8, plan.lanes)],
        [HBM] * 6 + [ANY] * 6 + [HBM, ANY, SMEM],
        scratch,
        16 * nside + 16,
        moved=4_000_000,
    )(*raw, *other, medium, slab, table)


def clear(plan, old, new, code):
    zero = jnp.zeros((8, plan.lanes), F32)

    def halo(slot, side):
        tile = plan.tiles - 1 if side == "high" else 0

        def one(p, _):
            for ref in list(old) + code:
                ref[p, 8 * tile : 8 * tile + 8, :] = zero
            return 0

        lax.fori_loop(0, plan.ext, one, 0)

    each_side(plan, halo)

    def above(p, _):
        for c in (1, 2, 7, 8):
            for ref in (old[c], new[c]):
                ref[p, plan.width : plan.width + 8, :] = zero
        return 0

    lax.fori_loop(0, plan.ext, above, 0)
    for c, ref in enumerate(new):
        plane = DEEP + plan.own if c % 6 < 3 else DEEP - 1
        for t in range(plan.tiles):
            ref[plane, 8 * t : 8 * t + 8, :] = zero


def strip_row(plan, side):
    if side == "low":
        return 4
    return plan.cols if plan.paired else 8 + plan.cols


def spread_strip(refs, strip, at, plane, pairs):
    def one(q, _):
        for c, ref in refs:
            for h in range(2):
                ref[plane + 2 * q + h, at : at + 4, :] = strip[c, q, 4 * h : 4 * h + 4, :]
        return 0

    lax.fori_loop(0, pairs, one, 0)


def substeps(plan, first, second, base, silicon, charge, gen, coef):
    lanes = plan.lanes
    tile = (8, lanes)
    lane = lax.broadcasted_iota(jnp.int32, tile, 1)
    row = lax.broadcasted_iota(jnp.int32, tile, 0)
    keep_up, keep_down, at_top = lane < lanes - 1, lane > 0, row == 0
    z, x, k = (lax.axis_index(a) for a in LINE)
    at_low = jnp.logical_and(z == 0, k == 0)
    at_high = jnp.logical_and(z == plan.gz - 1, k == 1)

    def up(v):
        return jnp.where(keep_up, pltpu.roll(v, lanes - 1, 1), 0.0)

    def down(v):
        return jnp.where(keep_down, pltpu.roll(v, 1, 1), 0.0)

    def edge_mask(t):
        if plan.paired or t not in (0, plan.tiles - 1):
            return None
        off = (x == 0) if t == 0 else (x == plan.gx - 1)
        return jnp.where(off, 0.0, 1.0)

    def magnetic(old, new, s, p, t):
        ex, ey, ez, hx, hy, hz = old[6 * s : 6 * s + 6]
        here, beside = slice(8 * t, 8 * t + 8), slice(8 * t + 1, 8 * t + 9)
        vx, vy, vz = ex[p, here, :], ey[p, here, :], ez[p, here, :]
        nx = hx[p, here, :] - COURANT * ((up(vz) - vz) - (ey[p + 1, here, :] - vy))
        ny = hy[p, here, :] - COURANT * ((ex[p + 1, here, :] - vx) - (ez[p, beside, :] - vz))
        nz = hz[p, here, :] - COURANT * ((ey[p, beside, :] - vy) - (up(vx) - vx))
        mask = edge_mask(t)
        if mask is not None:
            nx, ny, nz = nx * mask, ny * mask, nz * mask
        new[6 * s + 3][p, here, :] = nx
        new[6 * s + 4][p, here, :] = ny
        new[6 * s + 5][p, here, :] = nz

    def electric(old, new, p, t):
        coarse = p // BLOCK_FACTOR
        here = slice(8 * t, 8 * t + 8)
        volts = [[old[6 * s + c][p, here, :] for c in range(3)] for s in range(2)]
        strength = [v[0] * v[0] + v[1] * v[1] + v[2] * v[2] for v in volts]
        is_silicon = silicon[p, here, :]
        total = (strength[0] + strength[1]) * is_silicon
        carriers = charge[coarse, here, :] * is_silicon
        ground = base[p, here, :]
        gen[p, here, :] += (coef[1] * strength[0] + coef[5] * strength[1]) * total
        mask = edge_mask(t)
        for s in range(2):
            vx, vy, vz = volts[s]
            hx, hy, hz = new[6 * s + 3 : 6 * s + 6]
            nx, ny, nz = hx[p, here, :], hy[p, here, :], hz[p, here, :]
            if t == 0:
                left_y = jnp.where(at_top, 0.0, pltpu.roll(ny, 1, 0))
                left_z = jnp.where(at_top, 0.0, pltpu.roll(nz, 1, 0))
            else:
                before = slice(8 * t - 1, 8 * t + 7)
                left_y, left_z = hy[p, before, :], hz[p, before, :]
            loss = coef[4 * s + 2] * total + coef[4 * s + 3] * carriers
            perm = ground + coef[4 * s] * total
            inv = pl.reciprocal(perm + loss, approx=True)
            keep = (perm - loss) * inv
            push = COURANT * inv
            if mask is not None:
                push = push * mask
            curl_x = (nz - down(nz)) - (ny - hy[p - 1, here, :])
            curl_y = (nx - hx[p - 1, here, :]) - (nz - left_z)
            curl_z = (ny - left_y) - (nx - down(nx))
            new[6 * s][p, here, :] = keep * vx + push * curl_x
            new[6 * s + 1][p, here, :] = keep * vy + push * curl_y
            new[6 * s + 2][p, here, :] = keep * vz + push * curl_z

    def magnetic_plane(old, new, p):
        for t in range(plan.tiles):
            for s in range(2):
                magnetic(old, new, s, p, t)

    def substep(old, new, n):
        begin = jnp.where(at_low, DEEP, n + 1)
        end = jnp.where(at_high, DEEP + plan.own, plan.ext - 1 - n)

        @pl.when(jnp.logical_not(at_low))
        def _():
            magnetic_plane(old, new, n)

        magnetic_plane(old, new, begin)

        def step(p, _):
            for t in range(plan.tiles):
                electric(old, new, p, t)
                for s in range(2):
                    magnetic(old, new, s, p + 1, t)
            return 0

        lax.fori_loop(begin, end, step, 0)

    def pair(m, _):
        substep(first, second, 2 * m)
        substep(second, first, 2 * m + 1)
        return 0

    lax.fori_loop(0, SUBSTEPS // 2, pair, 0)


def set_media(plan, code, base, silicon):
    def one(p, _):
        for t in range(plan.tiles):
            here = slice(8 * t, 8 * t + 8)
            v = code[p, here, :]
            base[p, here, :] = jnp.where(v == 0.0, SILICON_PERM, jnp.where(v == 1.0, OXIDE_PERM, 1.0))
            silicon[p, here, :] = jnp.where(v == 0.0, 1.0, 0.0)
        return 0

    lax.fori_loop(0, plan.ext, one, 0)


def clear_generation(plan, gen):
    def one(p, _):
        gen[p] = jnp.zeros((plan.rows, plan.lanes), F32)
        return 0

    lax.fori_loop(DEEP, DEEP + plan.own, one, 0)


def sum_generation(plan, gen, message):
    blocks = plan.cols // BLOCK_FACTOR
    shape = (blocks, plan.lanes)
    column = lax.broadcasted_iota(jnp.int32, shape, 0) + blocks * lax.axis_index("gx")
    upright = lax.broadcasted_iota(jnp.int32, shape, 1) == column
    across = plan.own_rows()
    for a in range(plan.own // BLOCK_FACTOR):
        p = DEEP + BLOCK_FACTOR * a
        rows = (gen[p, across, :] + gen[p + 1, across, :]) + (
            gen[p + 2, across, :] + gen[p + 3, across, :]
        )
        cells = rows.reshape(blocks, BLOCK_FACTOR, plan.lanes).sum(1)
        mean = cells.sum(1, keepdims=True) * (1.0 / (BLOCK_FACTOR * BLOCK_FACTOR * plan.lanes))
        message[a : a + 1, :] = jnp.where(upright, mean, 0.0).sum(0, keepdims=True)


def round_scratch(plan):
    wide = (plan.ext, plan.rows, plan.lanes)
    return [pltpu.VMEM((plan.ext + 1, plan.rows, plan.lanes), F32)] * 24 + [
        pltpu.VMEM(wide, F32)
    ] * 3 + [
        pltpu.VMEM((plan.ext // BLOCK_FACTOR, plan.width, plan.lanes), F32),
        pltpu.VMEM((8, plan.lanes), F32),
        pltpu.VMEM((8, 8, plan.lanes), F32),
        pltpu.VMEM(wide, F32),
    ]


def round_flops(plan):
    return SUBSTEPS * plan.ext * plan.width * plan.lanes * 150


def generation_shape(plan):
    return (plan.devices, 8, plan.lanes)


def place_strips(plan, old, code, strips):
    k = lax.axis_index("af")
    outward, inner = plan.part * k, plan.part * (1 - k)

    def place(slot, side):
        whole, beside, corner = strips[3 * slot : 3 * slot + 3]
        at = strip_row(plan, side)
        same = list(enumerate(list(old) + code))
        flipped = list(enumerate(list(old[6:]) + list(old[:6]) + code))
        spread_strip(same, whole, at, DEEP, plan.own // 2)
        spread_strip(flipped, beside, at, inner, DEEP // 2)
        spread_strip(flipped, corner, at, outward, DEEP // 2)

    each_side(plan, place)


def send_generation(plan, copies, started, gen, message, gen_out):
    sum_generation(plan, gen, message)
    for d in range(plan.devices):
        started.append(copies.start(message, gen_out.at[d]))


def charge_from_slabs(plan, charge, mine, across, chip, corner):
    across, chip = chip, across
    x, k = lax.axis_index("gx"), lax.axis_index("af")
    slab = plan.slab
    left = jnp.where(x == 0, mine, across)
    right = jnp.where(x == 0, across, mine)
    beyond = jnp.where(x != k, chip, corner)
    body = jnp.where(k == 0, left, right)
    before = jnp.where(k == 0, beyond, left)[slab - 1 : slab]
    after = jnp.where(k == 0, right, beyond)[0:1]
    for a in range(slab + 2):
        row = before if a == 0 else after if a == slab + 1 else body[a - 1 : a]
        spread_row(plan, row, charge, a)


def spread_row(plan, row, charge, a):
    left = (plan.cols * lax.axis_index("gx") - plan.first_row()) // BLOCK_FACTOR
    row = jnp.broadcast_to(row, (8, plan.lanes))
    row = pltpu.roll(row, lax.rem(plan.lanes - left, plan.lanes), 1)
    for c in range(plan.width // BLOCK_FACTOR):
        charge[a, 4 * c : 4 * c + 4, :] = jnp.broadcast_to(row[0:4, c : c + 1], (4, plan.lanes))


def first_kernel(plan, *refs):
    nside = len(plan.sides)
    strips_in = refs[: 3 * nside]
    z_in, raw, other = refs[3 * nside], refs[1 + 3 * nside : 7 + 3 * nside], refs[7 + 3 * nside : 13 + 3 * nside]
    medium, slab_in, under_in, coef_in = refs[13 + 3 * nside : 17 + 3 * nside]
    outs = refs[17 + 3 * nside : 22 + 6 * nside]
    own_out, z_out, core_out, gen_out, code_out = outs[:5]
    rest = refs[22 + 6 * nside :]
    old, new, (base, silicon, gen, charge, message, coef, code) = rest[:12], rest[12:24], rest[24:31]
    codes, strips, (strip_mine, slabs, sems) = rest[31], rest[32 : 32 + 3 * nside], rest[-3:]
    copies = Copies(sems)
    k = lax.axis_index("af")
    near = DEEP * (1 - k)
    far = plan.part * k
    across = plan.own_rows()
    here, there = pl.ds(near, plan.part), pl.ds(far, DEEP)
    mine = pl.ds((plan.own - DEEP) * k, plan.part)
    early = [copies.start(medium.at[mine], codes)]
    early.append(copies.start(z_in.at[12], code.at[there, across]))
    early.append(copies.start(slab_in, slabs.at[0]))
    if plan.paired:
        early.append(copies.start(z_in.at[13, 0, pl.ds(0, 8)], slabs.at[1]))
    else:
        early.append(copies.start(under_in, charge))
    early.append(copies.start(coef_in, coef))
    for source, target in zip(strips_in, strips):
        early.append(copies.start(source, target))
    late = []
    for c in range(6):
        late.append(copies.start(raw[c].at[0, mine], old[c].at[here, across]))
        late.append(copies.start(other[c].at[0, mine], old[6 + c].at[here, across]))
    for c in range(12):
        late.append(copies.start(z_in.at[(c + 6) % 12], old[c].at[there, across]))
    clear(plan, old, new, [code])
    clear_generation(plan, gen)
    wait(early)

    def settle(p, _):
        code[near + p, across, :] = codes[p].astype(F32)
        return 0

    lax.fori_loop(0, plan.part, settle, 0)
    place_strips(plan, old, [code], strips)
    set_media(plan, code, base, silicon)
    if plan.paired:
        charge_from_slabs(plan, charge, slabs[0], slabs[1], strips[0][13, 0], strips[2][13, 0])
    wait(late)
    substeps(plan, old, new, base, silicon, charge, gen, coef)
    copies = Copies(sems)
    late = []

    def gather(slot, side):
        high_end = (side == "high") if plan.paired else (side == "low")
        low = 0 if plan.paired and side == "high" else 8
        at = low + plan.cols - 4 if high_end else low

        def one(q, _):
            for c in range(12):
                for h in range(2):
                    strip_mine[slot, c, q, 4 * h : 4 * h + 4, :] = old[c][
                        DEEP + 2 * q + h, at : at + 4, :
                    ]
            return 0

        lax.fori_loop(0, plan.own // 2, one, 0)

    toward = DEEP + (plan.own - DEEP) * k
    inward = DEEP + (plan.own - DEEP) * (1 - k)
    for c in range(12):
        late.append(copies.start(old[c].at[pl.ds(toward, DEEP), across], z_out.at[c]))
        late.append(copies.start(old[c].at[pl.ds(inward, DEEP), across], core_out.at[c]))
        late.append(copies.start(old[c].at[pl.ds(DEEP, plan.own), across], own_out.at[c]))
    late.append(copies.start(code, code_out))
    message[4:8, :] = slabs[0, 0:4, :]
    each_side(plan, gather)
    send_strips(plan, copies, late, strip_mine, outs[5:])
    send_generation(plan, copies, late, gen, message, gen_out)
    wait(late)


def first_round(plan, strips, z_in, raw, other, medium, slab, under, coef):
    wide = (plan.cols, plan.lanes)
    nside = len(plan.sides)
    shapes = [
        (12, plan.own) + wide,
        (12, DEEP) + wide,
        (12, DEEP) + wide,
        generation_shape(plan),
        (plan.ext, plan.rows, plan.lanes),
    ] + strip_shapes(plan, 12)
    scratch = round_scratch(plan) + [pltpu.VMEM((plan.part,) + wide, jnp.int32)]
    scratch += [pltpu.VMEM(s.shape, F32) for s in strips]
    scratch += [
        pltpu.VMEM((nside, 12, plan.own // 2, 8, plan.lanes), F32),
        pltpu.VMEM((2, 8, plan.lanes), F32),
    ]
    return call(
        plan,
        first_kernel,
        "first_round",
        shapes,
        [ANY] * (1 + 3 * nside) + [HBM] * 6 + [ANY] * 6 + [HBM, ANY, ANY, HBM],
        scratch,
        40 + 3 * nside + plan.devices,
        round_flops(plan),
        10_000_000,
    )(*strips, z_in, *raw, *other, medium, slab, under, coef)


def second_kernel(plan, *refs):
    nside = len(plan.sides)
    strips_in = refs[: 3 * nside]
    z_in, core_in, own_in, code_in, charge_in, coef_in = refs[3 * nside : 6 + 3 * nside]
    outs = refs[6 + 3 * nside : 14 + 3 * nside]
    kept, sent, gen_out = outs[:6], outs[6], outs[7]
    rest = refs[14 + 3 * nside :]
    old, new, (base, silicon, gen, charge, message, coef, code) = rest[:12], rest[12:24], rest[24:31]
    strips, sems = rest[31:-1], rest[-1]
    copies = Copies(sems)
    k = lax.axis_index("af")
    across = plan.own_rows()
    outward = plan.part * k
    inner = plan.part * (1 - k)
    early = [copies.start(code_in, code), copies.start(charge_in, charge)]
    early.append(copies.start(coef_in, coef))
    for source, target in zip(strips_in, strips):
        early.append(copies.start(source, target))
    late = []
    for c in range(12):
        flip = (c + 6) % 12
        late.append(copies.start(own_in.at[c], old[c].at[pl.ds(DEEP, plan.own), across]))
        late.append(copies.start(z_in.at[flip], old[c].at[pl.ds(outward, DEEP), across]))
        late.append(copies.start(core_in.at[flip], old[c].at[pl.ds(inner, DEEP), across]))
    clear(plan, old, new, [])
    clear_generation(plan, gen)
    wait(early)
    place_strips(plan, old, [], strips)
    set_media(plan, code, base, silicon)
    wait(late)
    substeps(plan, old, new, base, silicon, charge, gen, coef)
    copies = Copies(sems)
    late = []
    for c in range(6):
        late.append(copies.start(old[6 + c].at[pl.ds(DEEP, plan.own), across], sent.at[c]))
    for c in range(6):
        target = kept[c].at[0, pl.ds(plan.own * k, plan.own)]
        late.append(copies.start(old[c].at[pl.ds(DEEP, plan.own), across], target))
    message[...] = jnp.zeros(message.shape, F32)
    send_generation(plan, copies, late, gen, message, gen_out)
    wait(late)


def second_round(plan, strips, z_in, core_in, own_in, code, charge, coef):
    wide = (plan.cols, plan.lanes)
    nside = len(plan.sides)
    shapes = [(1, plan.planes) + wide] * 6 + [(6, plan.own) + wide, generation_shape(plan)]
    scratch = round_scratch(plan) + [pltpu.VMEM(s.shape, F32) for s in strips]
    return call(
        plan,
        second_kernel,
        "second_round",
        shapes,
        [ANY] * (2 + 3 * nside) + [HBM] * 4,
        scratch,
        39 + 3 * nside + plan.devices,
        round_flops(plan),
        10_000_000,
    )(*strips, z_in, core_in, own_in, code, charge, coef)


def join_kernel(plan, *refs):
    got, outs, (half, sems) = refs[6], refs[7:13], refs[13:]
    copies = Copies(sems)
    rows = pl.ds(plan.own * (1 - lax.axis_index("af")), plan.own)
    early = [copies.start(got.at[c], half.at[c]) for c in range(6)]
    late = []
    for c in range(6):
        early[c].wait()
        late.append(copies.start(half.at[c], outs[c].at[0, rows]))
    wait(late)


def join(plan, halves, got):
    shapes = [h.shape for h in halves]
    aliases = {c: c for c in range(6)}
    scratch = [pltpu.VMEM(got.shape, F32)]
    return call(
        plan, join_kernel, "join", shapes, [HBM] * 6 + [ANY], scratch, 12, moved=3_000_000, aliases=aliases
    )(*halves, got)


def charge_shape(plan):
    return (plan.ext // BLOCK_FACTOR, plan.width, plan.lanes)


def spread_whole(plan, density):
    z, x, k = (lax.axis_index(a) for a in LINE)
    side = plan.width // BLOCK_FACTOR
    padded = jnp.pad(density, ((1, 1), (side, side)))
    top = (plan.planes * z + plan.own * k) // BLOCK_FACTOR
    left = side + (plan.cols * x - plan.first_row()) // BLOCK_FACTOR
    tile = lax.dynamic_slice(padded, (top, left), (plan.ext // BLOCK_FACTOR, side))
    return jnp.broadcast_to(jnp.repeat(tile, BLOCK_FACTOR, 1)[:, :, None], charge_shape(plan))


def carrier_kernel(plan, last, *refs):
    gens_in, refs = refs[0], refs[1:]
    if last:
        density_in, refs = refs[0], refs[1:]
    outs = refs[:1] if last else refs[:2]
    gens, one, two, source, charge, slab_out, sems = refs[len(outs) :]
    copies = Copies(sems)
    rows, cols, lanes = plan.grid_rows, plan.grid_cols, plan.lanes
    z, x, k = (lax.axis_index(a) for a in LINE)
    own = plan.own // BLOCK_FACTOR
    early = [copies.start(gens_in, gens)]
    if last:
        early.append(copies.start(density_in, one))
    zero = jnp.zeros((8, lanes), F32)
    for ref in (two,) if last else (one, two):
        ref[0:8, :] = zero
        ref[8 + rows : 16 + rows, :] = zero
    wait(early)

    def unpack(line, _):
        top = pl.multiple_of(8 * line, 8)
        for dk in range(2):
            tiles = [gens[(line * plan.gx + dx) * 2 + dk, 0:own, :] for dx in range(plan.gx)]
            source[pl.ds(top + own * dk, own), :] = SOURCE_FACTOR * functools.reduce(jnp.add, tiles)
        if not last:
            for dx in range(plan.gx):
                slab = gens[(line * plan.gx + dx) * 2, 4 : 4 + plan.slab, :]
                one[pl.ds(8 + top + plan.slab * dx, plan.slab), :] = slab
        return 0

    lax.fori_loop(0, plan.gz, unpack, 0, unroll=plan.gz <= 4)
    inside = lax.broadcasted_iota(jnp.int32, (8, lanes), 1) < cols
    for step in range(CSTEPS):
        old, new = (one, two) if step % 2 == 0 else (two, one)
        for r in range(8, 8 + rows, 8):
            now, before = old[r : r + 8, :], old[r - 1 : r + 7, :]
            around = (
                old[r + 1 : r + 9, :]
                + before
                + pltpu.roll(now, lanes - 1, 1)
                + pltpu.roll(now, 1, 1)
                - 4.0 * now
            )
            later = (
                now
                + SPREAD_COEFF * around
                - MOBILITY_TERM * (now - before)
                - LIFETIME_DECAY * now
                + source[r - 8 : r, :]
            )
            new[r : r + 8, :] = jnp.where(inside, later, 0.0)
    if last:
        mine = one[pl.ds(8 + (z * plan.gx + x) * plan.slab, plan.slab), :]
        slab_out[...] = mine[:, :cols]
        copies.start(slab_out, outs[0]).wait()
        return
    late = [copies.start(one, outs[0])]
    for a in range(plan.ext // BLOCK_FACTOR):
        top = (plan.planes * z + plan.own * k - DEEP) // BLOCK_FACTOR + a
        spread_row(plan, one[pl.ds(8 + jnp.clip(top, 0, rows - 1), 1), :], charge, a)
    late.append(copies.start(charge, outs[1]))
    wait(late)


def carriers(plan, last, *arrays):
    grid, slab = (plan.grid_rows + 16, plan.lanes), (plan.slab, plan.grid_cols)
    scratch = [
        pltpu.VMEM(arrays[0].shape, F32),
        pltpu.VMEM(grid, F32),
        pltpu.VMEM(grid, F32),
        pltpu.VMEM((plan.grid_rows, plan.lanes), F32),
        pltpu.VMEM(charge_shape(plan), F32),
        pltpu.VMEM(slab, F32),
    ]
    return call(
        plan,
        lambda plan, *refs: carrier_kernel(plan, last, *refs),
        "carriers",
        [slab] if last else [grid, charge_shape(plan)],
        [ANY] + [HBM] * (len(arrays) - 1),
        scratch,
        4,
        2_000_000,
        1_000_000,
    )(*arrays)


def local(ex, ey, ez, hx, hy, hz, medium, table, density):
    raw = (ex, ey, ez, hx, hy, hz)
    plan = Plan(*medium.shape, density.shape[0])

    def send(message, target):
        return lax.ppermute(message, LINE, line_pairs(plan, target))

    def everywhere(message, axes):
        return lax.all_to_all(message, axes, split_axis=0, concat_axis=0, tiled=True)

    core = lambda z, x, k: (z, x, 1 - k)
    beyond = lambda z, k: z - 1 if k == 0 else z + 1

    def exchange(z_msg, strips):
        got = []
        for n, side in enumerate(plan.sides):
            to = functools.partial(across_step, side)
            whole, inner, corner = strips[3 * n : 3 * n + 3]
            got.append(send(whole, lambda z, x, k: (z, to(x), k)))
            got.append(send(inner, lambda z, x, k: (z, to(x), 1 - k)))
            got.append(send(corner, lambda z, x, k: (beyond(z, k), to(x), 1 - k)))
        return send(z_msg, lambda z, x, k: (beyond(z, k), x, 1 - k)), got

    other = [send(r, core) for r in raw]
    slab = jnp.pad(density, ((0, 8 - plan.slab), (0, plan.lanes - plan.grid_cols)))
    packed = pack(plan, raw, other, medium, slab, table)
    z_in, strips = exchange(packed[0], packed[1:-1])
    coef = packed[-1]
    under = slab
    if not plan.paired:
        tiles = plan.gz * plan.gx
        slabs = everywhere(jnp.broadcast_to(density, (tiles,) + density.shape), ("gz", "gx"))
        under = spread_whole(plan, slabs.reshape(plan.grid_rows, plan.grid_cols))
    outs = first_round(plan, strips, z_in, raw, other, medium, slab, under, coef)
    own, z_msg, core_msg, gens, code = outs[:5]
    gens = everywhere(gens, LINE)
    z_in, strips = exchange(z_msg, outs[5:])
    core_in = send(core_msg, core)
    grid, charge = carriers(plan, False, gens)
    outs = second_round(plan, strips, z_in, core_in, own, code, charge, coef)
    halves, sent, gens = outs[:6], outs[6], outs[7]
    gens = everywhere(gens, LINE)
    got = send(sent, core)
    (new_slab,) = carriers(plan, True, gens, grid)
    return tuple(join(plan, halves, got)) + (new_slab,)


def solution(mesh):
    field = P("af", ("group", "gz"), "gx", None)
    slabs = P(("group", "gz", "gx"), None)
    in_specs = (field,) * 6 + (P(("group", "gz"), "gx", None), P(), slabs)
    out_specs = (field,) * 6 + (slabs,)
    return jax.shard_map(local, mesh=mesh, in_specs=in_specs, out_specs=out_specs, check_vma=False)
```

```python
import functools

import jax
import jax.numpy as jnp
from jax import lax
from jax.experimental import pallas as pl
from jax.experimental.pallas import tpu as pltpu
from jax.sharding import PartitionSpec as P

BLOCK_FACTOR = 4
SUBSTEPS = 4
ROUNDS = 2
CSTEPS = 8

COURANT = 0.5
SILICON_PERM = 12.1
OXIDE_PERM = 2.1
SPREAD_COEFF = 0.2
MOBILITY_TERM = 0.1
LIFETIME_DECAY = 0.05
SOURCE_FACTOR = 0.02

DEEP = SUBSTEPS
LINE = ("gz", "gx", "af")
HBM = pl.BlockSpec(memory_space=pltpu.HBM)
ANY = pl.BlockSpec(memory_space=pl.ANY)
SMEM = pl.BlockSpec(memory_space=pltpu.SMEM)
VMEM_LIMIT = 24 * 1024 * 1024
F32 = jnp.float32


class Plan:
    def __init__(self, planes, cols, lanes, slab):
        self.gz = lax.axis_size("gz")
        self.gx = lax.axis_size("gx")
        self.planes, self.cols, self.lanes, self.slab = planes, cols, lanes, slab
        self.own = planes // 2
        self.part = self.own + DEEP
        self.ext = self.own + 2 * DEEP
        self.paired = self.gx == 2
        self.sides = ("face",) if self.paired else ("low", "high")
        self.width = cols + (8 if self.paired else 16)
        self.rows = self.width + 8
        self.tiles = self.width // 8
        self.grid_rows = planes * self.gz // BLOCK_FACTOR
        self.grid_cols = cols * self.gx // BLOCK_FACTOR
        self.devices = self.gz * self.gx * 2

    def first_row(self):
        return 8 * lax.axis_index("gx") if self.paired else 8

    def own_rows(self):
        return pl.ds(pl.multiple_of(self.first_row(), 8), self.cols)


def each_side(plan, act):
    if plan.paired:
        across = lax.axis_index("gx")

        @pl.when(across == 0)
        def _():
            act(0, "high")

        @pl.when(across == 1)
        def _():
            act(0, "low")
    else:
        act(0, "low")
        act(1, "high")


def line_pairs(plan, target):
    pairs = []
    for z in range(plan.gz):
        for x in range(plan.gx):
            for k in range(2):
                tz, tx, tk = target(z, x, k)
                if 0 <= tz < plan.gz and 0 <= tx < plan.gx:
                    pairs.append(((z * plan.gx + x) * 2 + k, (tz * plan.gx + tx) * 2 + tk))
    return pairs


def across_step(side, x):
    if side == "face":
        return 1 - x
    return x + 1 if side == "low" else x - 1


class Copies:
    def __init__(self, sems):
        self.sems, self.made = sems, 0

    def start(self, source, target):
        copy = pltpu.make_async_copy(source, target, self.sems.at[self.made])
        self.made += 1
        copy.start()
        return copy


def wait(copies):
    for copy in copies:
        copy.wait()


def call(plan, body, name, shapes, in_specs, scratch, copies, flops=0, moved=0, aliases=None):
    kernel = pl.pallas_call(
        functools.partial(body, plan),
        out_shape=[pltpu.HBM(s, F32) for s in shapes],
        in_specs=in_specs,
        out_specs=[HBM] * len(shapes),
        scratch_shapes=scratch + [pltpu.SemaphoreType.DMA((copies,))],
        input_output_aliases=aliases or {},
        compiler_params=pltpu.CompilerParams(vmem_limit_bytes=VMEM_LIMIT),
        cost_estimate=pl.CostEstimate(flops=flops, bytes_accessed=moved, transcendentals=0),
        name=name,
    )

    def run(*args):
        placed = []
        for arg, spec in zip(args, in_specs):
            in_hbm = spec.memory_space is pltpu.HBM
            placed.append(pltpu.with_memory_space_constraint(arg, pltpu.HBM) if in_hbm else arg)
        return kernel(*placed)

    return run


def pack_kernel(plan, *refs):
    raw, other, medium, nside = refs[:6], refs[6:12], refs[12], len(plan.sides)
    slab_in, table_in = refs[13:15]
    outs = refs[15 : 18 + 3 * nside]
    edge, edge_code, face, face_code, strips, corners, slab, table, coef, sems = refs[18 + 3 * nside :]
    copies = Copies(sems)
    k = lax.axis_index("af")
    mine = pl.ds(plan.own * k, plan.own)
    outer = pl.ds((plan.planes - DEEP) * k, DEEP)
    if plan.paired:
        tile_rows = [pl.multiple_of((plan.cols - 8) * (1 - lax.axis_index("gx")), 8)]
    else:
        tile_rows = [plan.cols - 8, 0]
    early, late, last = [], [], []
    early.append(copies.start(slab_in, slab))
    early.append(copies.start(table_in, table))
    for n, row in enumerate(tile_rows):
        for c in range(6):
            side = pl.ds(row, 8)
            early.append(copies.start(raw[c].at[0, mine, side, :], edge.at[n, c]))
            early.append(copies.start(other[c].at[0, mine, side, :], edge.at[n, 6 + c]))
        early.append(copies.start(medium.at[mine, pl.ds(row, 8), :], edge_code.at[n]))
    for c in range(6):
        late.append(copies.start(raw[c].at[0, outer], face.at[pl.ds(DEEP * c, DEEP)]))
        late.append(copies.start(other[c].at[0, outer], face.at[pl.ds(DEEP * (6 + c), DEEP)]))
    late.append(copies.start(medium.at[outer], face_code))
    wait(early)
    rows = plan.own // 2

    def fill(slot, low):
        def one(q, _):
            for h in range(2):
                half = slice(4 * h, 4 * h + 4)
                for c in range(12):
                    strips[slot, c * rows + q, half, :] = edge[slot, c, 2 * q + h, low : low + 4, :]
                code = edge_code[slot, 2 * q + h, low : low + 4, :]
                strips[slot, 12 * rows + q, half, :] = code.astype(F32)
            return 0

        lax.fori_loop(0, rows, one, 0)

    each_side(plan, lambda slot, side: fill(slot, 4 if plan.paired == (side == "high") else 0))
    page = slab[...]
    for n in range(nside):
        for extra in range(13 * rows, strip_tiles(plan, 13)):
            strips[n, extra] = page
        corners[n, 0, 13 * DEEP // 2] = page
        corners[n, 1, 13 * DEEP // 2] = page
    send_strips(plan, copies, last, strips, corners, outs[2:-1], 13)
    own, partner = jnp.where(k == 0, table[0:1], table[1:2]), jnp.where(k == 0, table[1:2], table[0:1])
    for s, row in enumerate((own, partner)):
        kerr, two, free = row[:, 0:1], row[:, 1:2], row[:, 2:3]
        for n, value in enumerate((kerr, two, 0.5 * two, 0.5 * free)):
            coef[4 * s + n] = jnp.broadcast_to(value, (8, plan.lanes))
    last.append(copies.start(coef, outs[-1]))
    wait(late)
    face[12 * DEEP : 13 * DEEP] = face_code[...].astype(F32)
    face[13 * DEEP, 0:8, :] = page
    for r in range(8, plan.cols, 8):
        face[13 * DEEP, r : r + 8, :] = page
    send_face(plan, copies, last, face, outs[:2])
    wait(last)


def face_split(plan, pages):
    if pages == 12 * DEEP:
        return ((0, pages),)
    first = (pages + 1) // 2
    return ((0, first), (first, pages - first))


def send_face(plan, copies, started, face, outs):
    for out, (start, count) in zip(outs, face_split(plan, face.shape[0])):
        started.append(copies.start(face.at[pl.ds(start, count)], out))


def get_face(plan, copies, parts, pages, first, targets):
    started = []
    for part, (start, count) in zip(parts, face_split(plan, pages)):
        low, high = max(first, start), min(first + DEEP, start + count)
        if low < high:
            source = part.at[pl.ds(low - start, high - low)]
            started.append(copies.start(source, targets(low - first, high - low)))
    return started


def strip_tiles(plan, comps):
    pages = DEEP * comps + (comps > 12)
    if comps == 12:
        return comps * plan.own // 2
    return max(comps * plan.own // 2, (pages + 1) // 2 * (plan.cols // 8)) + 1


def send_strips(plan, copies, started, strips, corners, outs, comps):
    k = lax.axis_index("af")
    half, top = DEEP // 2, (plan.own - DEEP) // 2
    for n in range(len(plan.sides)):
        started.append(copies.start(strips.at[n], outs[3 * n]))
        for e, begin in enumerate((top * (1 - k), top * k)):
            for c in range(comps):
                for h in range(half):
                    corners[n, e, half * c + h] = strips[n, plan.own // 2 * c + begin + h]
            started.append(copies.start(corners.at[n, e], outs[3 * n + 1 + e]))


def corner_tiles(plan, comps):
    return comps * DEEP // 2 + (comps > 12)


def strip_shapes(plan, comps):
    shapes = []
    for _ in plan.sides:
        tiles = corner_tiles(plan, comps)
        for tiles in (strip_tiles(plan, comps), tiles, tiles):
            shapes.append((tiles, 8, plan.lanes))
    return shapes


def face_shapes(plan, pages):
    return [(count, plan.cols, plan.lanes) for _, count in face_split(plan, pages)]


def pack(plan, raw, other, medium, slab, table):
    wide = (plan.cols, plan.lanes)
    nside = len(plan.sides)
    pages = 13 * DEEP + 1
    scratch = [
        pltpu.VMEM((nside, 12, plan.own, 8, plan.lanes), F32),
        pltpu.VMEM((nside, plan.own, 8, plan.lanes), jnp.int32),
        pltpu.VMEM((pages,) + wide, F32),
        pltpu.VMEM((DEEP,) + wide, jnp.int32),
        pltpu.VMEM((nside, strip_tiles(plan, 13), 8, plan.lanes), F32),
        pltpu.VMEM((nside, 2, corner_tiles(plan, 13), 8, plan.lanes), F32),
        pltpu.VMEM((8, plan.lanes), F32),
        pltpu.VMEM(table.shape, F32),
        pltpu.VMEM((8, 8, plan.lanes), F32),
    ]
    return call(
        plan,
        pack_kernel,
        "pack",
        face_shapes(plan, pages) + strip_shapes(plan, 13) + [(8, 8, plan.lanes)],
        [HBM] * 6 + [ANY] * 6 + [HBM, ANY, ANY],
        scratch,
        16 * nside + 18,
        moved=4_000_000,
    )(*raw, *other, medium, slab, table)


def clear(plan, old, new, code):
    zero = jnp.zeros((8, plan.lanes), F32)

    def halo(slot, side):
        tile = plan.tiles - 1 if side == "high" else 0

        def one(p, _):
            for ref in list(old) + code:
                ref[p, 8 * tile : 8 * tile + 8, :] = zero
            return 0

        lax.fori_loop(0, plan.ext, one, 0)

    each_side(plan, halo)

    def above(p, _):
        for c in (1, 2, 7, 8):
            for ref in (old[c], new[c]):
                ref[p, plan.width : plan.width + 8, :] = zero
        return 0

    lax.fori_loop(0, plan.ext, above, 0)
    for c, ref in enumerate(new):
        plane = DEEP + plan.own if c % 6 < 3 else DEEP - 1
        for t in range(plan.tiles):
            ref[plane, 8 * t : 8 * t + 8, :] = zero


def strip_row(plan, side):
    if side == "low":
        return 4
    return plan.cols if plan.paired else 8 + plan.cols


def spread_strip(refs, strip, each, begin, at, plane, pairs):
    def one(q, _):
        for c, ref in refs:
            for h in range(2):
                tile = c * each + begin + q
                ref[plane + 2 * q + h, at : at + 4, :] = strip[tile, 4 * h : 4 * h + 4, :]
        return 0

    lax.fori_loop(0, pairs, one, 0)


def substeps(plan, first, second, base, silicon, charge, gen, coef):
    lanes = plan.lanes
    tile = (8, lanes)
    lane = lax.broadcasted_iota(jnp.int32, tile, 1)
    row = lax.broadcasted_iota(jnp.int32, tile, 0)
    keep_up, keep_down, at_top = lane < lanes - 1, lane > 0, row == 0
    z, x, k = (lax.axis_index(a) for a in LINE)
    at_low = jnp.logical_and(z == 0, k == 0)
    at_high = jnp.logical_and(z == plan.gz - 1, k == 1)

    def up(v):
        return jnp.where(keep_up, pltpu.roll(v, lanes - 1, 1), 0.0)

    def down(v):
        return jnp.where(keep_down, pltpu.roll(v, 1, 1), 0.0)

    def edge_mask(t):
        if plan.paired or t not in (0, plan.tiles - 1):
            return None
        off = (x == 0) if t == 0 else (x == plan.gx - 1)
        return jnp.where(off, 0.0, 1.0)

    def magnetic(old, new, s, p, t):
        ex, ey, ez, hx, hy, hz = old[6 * s : 6 * s + 6]
        here, beside = slice(8 * t, 8 * t + 8), slice(8 * t + 1, 8 * t + 9)
        vx, vy, vz = ex[p, here, :], ey[p, here, :], ez[p, here, :]
        nx = hx[p, here, :] - COURANT * ((up(vz) - vz) - (ey[p + 1, here, :] - vy))
        ny = hy[p, here, :] - COURANT * ((ex[p + 1, here, :] - vx) - (ez[p, beside, :] - vz))
        nz = hz[p, here, :] - COURANT * ((ey[p, beside, :] - vy) - (up(vx) - vx))
        mask = edge_mask(t)
        if mask is not None:
            nx, ny, nz = nx * mask, ny * mask, nz * mask
        new[6 * s + 3][p, here, :] = nx
        new[6 * s + 4][p, here, :] = ny
        new[6 * s + 5][p, here, :] = nz

    def electric(old, new, p, t):
        coarse = p // BLOCK_FACTOR
        here = slice(8 * t, 8 * t + 8)
        volts = [[old[6 * s + c][p, here, :] for c in range(3)] for s in range(2)]
        strength = [v[0] * v[0] + v[1] * v[1] + v[2] * v[2] for v in volts]
        is_silicon = silicon[p, here, :]
        total = (strength[0] + strength[1]) * is_silicon
        carriers = charge[coarse, here, :] * is_silicon
        ground = base[p, here, :]
        gen[p, here, :] += (coef[1] * strength[0] + coef[5] * strength[1]) * total
        mask = edge_mask(t)
        for s in range(2):
            vx, vy, vz = volts[s]
            hx, hy, hz = new[6 * s + 3 : 6 * s + 6]
            nx, ny, nz = hx[p, here, :], hy[p, here, :], hz[p, here, :]
            if t == 0:
                left_y = jnp.where(at_top, 0.0, pltpu.roll(ny, 1, 0))
                left_z = jnp.where(at_top, 0.0, pltpu.roll(nz, 1, 0))
            else:
                before = slice(8 * t - 1, 8 * t + 7)
                left_y, left_z = hy[p, before, :], hz[p, before, :]
            loss = coef[4 * s + 2] * total + coef[4 * s + 3] * carriers
            perm = ground + coef[4 * s] * total
            inv = pl.reciprocal(perm + loss, approx=True)
            keep = (perm - loss) * inv
            push = COURANT * inv
            if mask is not None:
                push = push * mask
            curl_x = (nz - down(nz)) - (ny - hy[p - 1, here, :])
            curl_y = (nx - hx[p - 1, here, :]) - (nz - left_z)
            curl_z = (ny - left_y) - (nx - down(nx))
            new[6 * s][p, here, :] = keep * vx + push * curl_x
            new[6 * s + 1][p, here, :] = keep * vy + push * curl_y
            new[6 * s + 2][p, here, :] = keep * vz + push * curl_z

    def magnetic_plane(old, new, p):
        for t in range(plan.tiles):
            for s in range(2):
                magnetic(old, new, s, p, t)

    def substep(old, new, n):
        begin = jnp.where(at_low, DEEP, n + 1)
        end = jnp.where(at_high, DEEP + plan.own, plan.ext - 1 - n)
        odd = lax.rem(end - begin, 2)

        @pl.when(jnp.logical_not(at_low))
        def _():
            magnetic_plane(old, new, n)
            magnetic_plane(old, new, n + 1)

        @pl.when(at_low)
        def _():
            magnetic_plane(old, new, DEEP)

        def advance(p):
            for t in range(plan.tiles):
                electric(old, new, p, t)
                for s in range(2):
                    magnetic(old, new, s, p + 1, t)

        @pl.when(odd == 1)
        def _():
            advance(begin)

        def step(m, _):
            p = begin + odd + 2 * m
            advance(p)
            advance(p + 1)
            return 0

        lax.fori_loop(0, (end - begin) // 2, step, 0)

    def pair(m, _):
        substep(first, second, 2 * m)
        substep(second, first, 2 * m + 1)
        return 0

    lax.fori_loop(0, SUBSTEPS // 2, pair, 0)


def set_media(plan, code, base, silicon):
    def one(p, _):
        for t in range(plan.tiles):
            here = slice(8 * t, 8 * t + 8)
            v = code[p, here, :]
            base[p, here, :] = jnp.where(v == 0.0, SILICON_PERM, jnp.where(v == 1.0, OXIDE_PERM, 1.0))
            silicon[p, here, :] = jnp.where(v == 0.0, 1.0, 0.0)
        return 0

    lax.fori_loop(0, plan.ext, one, 0)


def clear_generation(plan, gen):
    def one(p, _):
        gen[p] = jnp.zeros((plan.rows, plan.lanes), F32)
        return 0

    lax.fori_loop(DEEP, DEEP + plan.own, one, 0)


def sum_generation(plan, gen, message):
    blocks = plan.cols // BLOCK_FACTOR
    shape = (blocks, plan.lanes)
    column = lax.broadcasted_iota(jnp.int32, shape, 0) + blocks * lax.axis_index("gx")
    upright = lax.broadcasted_iota(jnp.int32, shape, 1) == column
    across = plan.own_rows()
    for a in range(plan.own // BLOCK_FACTOR):
        p = DEEP + BLOCK_FACTOR * a
        rows = (gen[p, across, :] + gen[p + 1, across, :]) + (
            gen[p + 2, across, :] + gen[p + 3, across, :]
        )
        cells = rows.reshape(blocks, BLOCK_FACTOR, plan.lanes).sum(1)
        mean = cells.sum(1, keepdims=True) * (1.0 / (BLOCK_FACTOR * BLOCK_FACTOR * plan.lanes))
        message[a : a + 1, :] = jnp.where(upright, mean, 0.0).sum(0, keepdims=True)


def round_scratch(plan):
    wide = (plan.ext, plan.rows, plan.lanes)
    return [pltpu.VMEM((plan.ext + 1, plan.rows, plan.lanes), F32)] * 24 + [
        pltpu.VMEM(wide, F32)
    ] * 3 + [
        pltpu.VMEM((plan.ext // BLOCK_FACTOR, plan.width, plan.lanes), F32),
        pltpu.VMEM((8, plan.lanes), F32),
        pltpu.VMEM((8, 8, plan.lanes), F32),
        pltpu.VMEM(wide, F32),
    ]


def round_flops(plan):
    return SUBSTEPS * plan.ext * plan.width * plan.lanes * 150


def generation_shape(plan):
    return (plan.devices, 8, plan.lanes)


def place_strips(plan, old, code, strips):
    k = lax.axis_index("af")
    outward, inner = plan.part * k, plan.part * (1 - k)

    def place(slot, side):
        whole, beside, corner = strips[3 * slot : 3 * slot + 3]
        at = strip_row(plan, side)
        same = list(enumerate(list(old) + code))
        flipped = list(enumerate(list(old[6:]) + list(old[:6]) + code))
        half, rows = DEEP // 2, plan.own // 2
        spread_strip(same, whole, rows, 0, at, DEEP, rows)
        spread_strip(flipped, beside, half, 0, at, inner, half)
        spread_strip(flipped, corner, half, 0, at, outward, half)

    each_side(plan, place)


def send_generation(plan, copies, started, gen, message, gen_out):
    sum_generation(plan, gen, message)
    for d in range(plan.devices):
        started.append(copies.start(message, gen_out.at[d]))


def charge_from_slabs(plan, charge, mine, across, chip, corner):
    across, chip = chip, across
    x, k = lax.axis_index("gx"), lax.axis_index("af")
    slab = plan.slab
    left = jnp.where(x == 0, mine, across)
    right = jnp.where(x == 0, across, mine)
    beyond = jnp.where(x != k, chip, corner)
    body = jnp.where(k == 0, left, right)
    before = jnp.where(k == 0, beyond, left)[slab - 1 : slab]
    after = jnp.where(k == 0, right, beyond)[0:1]
    for a in range(slab + 2):
        row = before if a == 0 else after if a == slab + 1 else body[a - 1 : a]
        spread_row(plan, row, charge, a)


def spread_row(plan, row, charge, a):
    left = (plan.cols * lax.axis_index("gx") - plan.first_row()) // BLOCK_FACTOR
    row = jnp.broadcast_to(row, (8, plan.lanes))
    row = pltpu.roll(row, lax.rem(plan.lanes - left, plan.lanes), 1)
    for c in range(plan.width // BLOCK_FACTOR):
        charge[a, 4 * c : 4 * c + 4, :] = jnp.broadcast_to(row[0:4, c : c + 1], (4, plan.lanes))


def first_kernel(plan, *refs):
    nside = len(plan.sides)
    strips_in, refs = refs[: 3 * nside], refs[3 * nside :]
    z_in, raw, other = refs[:2], refs[2:8], refs[8:14]
    medium, slab_in, under_in, coef_in = refs[14:18]
    own_out, core_out, gen_out, code_out = refs[18:22]
    z_out, strip_out = refs[22], refs[23 : 23 + 3 * nside]
    rest = refs[23 + 3 * nside :]
    old, new, (base, silicon, gen, charge, message, coef, code) = rest[:12], rest[12:24], rest[24:31]
    codes, strips, (strip_mine, corners, slabs, sems) = rest[31], rest[32 : 32 + 3 * nside], rest[-4:]
    copies = Copies(sems)
    k = lax.axis_index("af")
    near = DEEP * (1 - k)
    far = plan.part * k
    across = plan.own_rows()
    here = pl.ds(near, plan.part)
    mine = pl.ds((plan.own - DEEP) * k, plan.part)
    early = [copies.start(medium.at[mine], codes)]
    pages = 13 * DEEP + 1
    early += get_face(
        plan, copies, z_in, pages, 12 * DEEP, lambda p, n: code.at[pl.ds(far + p, n), across]
    )
    early.append(copies.start(slab_in, slabs.at[0]))
    if plan.paired:
        early.append(copies.start(z_in[1].at[z_in[1].shape[0] - 1, pl.ds(0, 8)], slabs.at[1]))
    else:
        early.append(copies.start(under_in, charge))
    early.append(copies.start(coef_in, coef))
    for source, target in zip(strips_in, strips):
        early.append(copies.start(source, target))
    late = []
    for c in range(6):
        late.append(copies.start(raw[c].at[0, mine], old[c].at[here, across]))
        late.append(copies.start(other[c].at[0, mine], old[6 + c].at[here, across]))
    for c in range(12):
        late += get_face(
            plan,
            copies,
            z_in,
            pages,
            DEEP * ((c + 6) % 12),
            lambda p, n, ref=old[c]: ref.at[pl.ds(far + p, n), across],
        )
    clear(plan, old, new, [code])
    clear_generation(plan, gen)
    wait(early)

    def settle(p, _):
        code[near + p, across, :] = codes[p].astype(F32)
        return 0

    lax.fori_loop(0, plan.part, settle, 0)
    place_strips(plan, old, [code], strips)
    set_media(plan, code, base, silicon)
    if plan.paired:
        charge_from_slabs(
            plan, charge, slabs[0], slabs[1], strips[0][13 * plan.own // 2], strips[2][13 * DEEP // 2]
        )
    wait(late)
    substeps(plan, old, new, base, silicon, charge, gen, coef)
    copies = Copies(sems)
    late = []

    def gather(slot, side):
        high_end = (side == "high") if plan.paired else (side == "low")
        low = 0 if plan.paired and side == "high" else 8
        at = low + plan.cols - 4 if high_end else low

        def one(q, _):
            for c in range(12):
                for h in range(2):
                    tile = plan.own // 2 * c + q
                    strip_mine[slot, tile, 4 * h : 4 * h + 4, :] = old[c][
                        DEEP + 2 * q + h, at : at + 4, :
                    ]
            return 0

        lax.fori_loop(0, plan.own // 2, one, 0)

    toward = DEEP + (plan.own - DEEP) * k
    inward = DEEP + (plan.own - DEEP) * (1 - k)
    for c in range(12):
        source = old[c].at[pl.ds(toward, DEEP), across]
        late.append(copies.start(source, z_out.at[pl.ds(DEEP * c, DEEP)]))
        late.append(copies.start(old[c].at[pl.ds(inward, DEEP), across], core_out.at[c]))
        late.append(copies.start(old[c].at[pl.ds(DEEP, plan.own), across], own_out.at[c]))
    late.append(copies.start(code, code_out))
    message[4:8, :] = slabs[0, 0:4, :]
    each_side(plan, gather)
    send_strips(plan, copies, late, strip_mine, corners, strip_out, 12)
    send_generation(plan, copies, late, gen, message, gen_out)
    wait(late)


def first_round(plan, strips, z_in, raw, other, medium, slab, under, coef):
    wide = (plan.cols, plan.lanes)
    nside = len(plan.sides)
    shapes = [
        (12, plan.own) + wide,
        (12, DEEP) + wide,
        generation_shape(plan),
        (plan.ext, plan.rows, plan.lanes),
    ]
    shapes += face_shapes(plan, 12 * DEEP) + strip_shapes(plan, 12)
    scratch = round_scratch(plan) + [pltpu.VMEM((plan.part,) + wide, jnp.int32)]
    scratch += [pltpu.VMEM(s.shape, F32) for s in strips]
    scratch += [
        pltpu.VMEM((nside, strip_tiles(plan, 12), 8, plan.lanes), F32),
        pltpu.VMEM((nside, 2, corner_tiles(plan, 12), 8, plan.lanes), F32),
        pltpu.VMEM((2, 8, plan.lanes), F32),
    ]
    return call(
        plan,
        first_kernel,
        "first_round",
        shapes,
        [ANY] * (2 + 3 * nside) + [HBM] * 6 + [ANY] * 6 + [HBM, ANY, ANY, HBM],
        scratch,
        42 + 3 * nside + plan.devices,
        round_flops(plan),
        10_000_000,
    )(*strips, *z_in, *raw, *other, medium, slab, under, coef)


def second_kernel(plan, *refs):
    nside = len(plan.sides)
    strips_in, refs = refs[: 3 * nside], refs[3 * nside :]
    z_in, (core_in, own_in, code_in, charge_in, coef_in) = refs[:1], refs[1:6]
    kept, sent, gen_out, rest = refs[6:12], refs[12], refs[13], refs[14:]
    old, new, (base, silicon, gen, charge, message, coef, code) = rest[:12], rest[12:24], rest[24:31]
    strips, sems = rest[31:-1], rest[-1]
    copies = Copies(sems)
    k = lax.axis_index("af")
    across = plan.own_rows()
    outward = plan.part * k
    inner = plan.part * (1 - k)
    early = [copies.start(code_in, code), copies.start(charge_in, charge)]
    early.append(copies.start(coef_in, coef))
    for source, target in zip(strips_in, strips):
        early.append(copies.start(source, target))
    late = []
    for c in range(12):
        flip = (c + 6) % 12
        late.append(copies.start(own_in.at[c], old[c].at[pl.ds(DEEP, plan.own), across]))
        late += get_face(
            plan,
            copies,
            z_in,
            12 * DEEP,
            DEEP * flip,
            lambda p, n, ref=old[c]: ref.at[pl.ds(outward + p, n), across],
        )
        late.append(copies.start(core_in.at[flip], old[c].at[pl.ds(inner, DEEP), across]))
    clear(plan, old, new, [])
    clear_generation(plan, gen)
    wait(early)
    place_strips(plan, old, [], strips)
    set_media(plan, code, base, silicon)
    wait(late)
    substeps(plan, old, new, base, silicon, charge, gen, coef)
    copies = Copies(sems)
    late = []
    for c in range(6):
        late.append(copies.start(old[6 + c].at[pl.ds(DEEP, plan.own), across], sent.at[c]))
    for c in range(6):
        target = kept[c].at[0, pl.ds(plan.own * k, plan.own)]
        late.append(copies.start(old[c].at[pl.ds(DEEP, plan.own), across], target))
    message[...] = jnp.zeros(message.shape, F32)
    send_generation(plan, copies, late, gen, message, gen_out)
    wait(late)


def second_round(plan, strips, z_in, core_in, own_in, code, charge, coef):
    wide = (plan.cols, plan.lanes)
    nside = len(plan.sides)
    shapes = [(1, plan.planes) + wide] * 6 + [(6, plan.own) + wide, generation_shape(plan)]
    scratch = round_scratch(plan) + [pltpu.VMEM(s.shape, F32) for s in strips]
    return call(
        plan,
        second_kernel,
        "second_round",
        shapes,
        [ANY] * (2 + 3 * nside) + [HBM] * 4,
        scratch,
        39 + 3 * nside + plan.devices,
        round_flops(plan),
        10_000_000,
    )(*strips, *z_in, core_in, own_in, code, charge, coef)


def join_kernel(plan, *refs):
    got, outs, (half, sems) = refs[6], refs[7:13], refs[13:]
    copies = Copies(sems)
    rows = pl.ds(plan.own * (1 - lax.axis_index("af")), plan.own)
    early = [copies.start(got.at[c], half.at[c]) for c in range(6)]
    late = []
    for c in range(6):
        early[c].wait()
        late.append(copies.start(half.at[c], outs[c].at[0, rows]))
    wait(late)


def join(plan, halves, got):
    shapes = [h.shape for h in halves]
    aliases = {c: c for c in range(6)}
    scratch = [pltpu.VMEM(got.shape, F32)]
    return call(
        plan, join_kernel, "join", shapes, [HBM] * 6 + [ANY], scratch, 12, moved=3_000_000, aliases=aliases
    )(*halves, got)


def charge_shape(plan):
    return (plan.ext // BLOCK_FACTOR, plan.width, plan.lanes)


def spread_whole(plan, density):
    z, x, k = (lax.axis_index(a) for a in LINE)
    side = plan.width // BLOCK_FACTOR
    padded = jnp.pad(density, ((1, 1), (side, side)))
    top = (plan.planes * z + plan.own * k) // BLOCK_FACTOR
    left = side + (plan.cols * x - plan.first_row()) // BLOCK_FACTOR
    tile = lax.dynamic_slice(padded, (top, left), (plan.ext // BLOCK_FACTOR, side))
    return jnp.broadcast_to(jnp.repeat(tile, BLOCK_FACTOR, 1)[:, :, None], charge_shape(plan))


def carrier_kernel(plan, last, *refs):
    gens_in, refs = refs[0], refs[1:]
    if last:
        density_in, refs = refs[0], refs[1:]
    outs = refs[:1] if last else refs[:2]
    gens, one, two, source, charge, slab_out, sems = refs[len(outs) :]
    copies = Copies(sems)
    rows, cols, lanes = plan.grid_rows, plan.grid_cols, plan.lanes
    z, x, k = (lax.axis_index(a) for a in LINE)
    own = plan.own // BLOCK_FACTOR
    early = [copies.start(gens_in, gens)]
    if last:
        early.append(copies.start(density_in, one))
    zero = jnp.zeros((8, lanes), F32)
    for ref in (two,) if last else (one, two):
        ref[0:8, :] = zero
        ref[8 + rows : 16 + rows, :] = zero
    wait(early)

    def unpack(line, _):
        top = pl.multiple_of(8 * line, 8)
        for dk in range(2):
            tiles = [gens[(line * plan.gx + dx) * 2 + dk, 0:own, :] for dx in range(plan.gx)]
            source[pl.ds(top + own * dk, own), :] = SOURCE_FACTOR * functools.reduce(jnp.add, tiles)
        if not last:
            for dx in range(plan.gx):
                slab = gens[(line * plan.gx + dx) * 2, 4 : 4 + plan.slab, :]
                one[pl.ds(8 + top + plan.slab * dx, plan.slab), :] = slab
        return 0

    lax.fori_loop(0, plan.gz, unpack, 0, unroll=plan.gz <= 4)
    inside = lax.broadcasted_iota(jnp.int32, (8, lanes), 1) < cols
    for step in range(CSTEPS):
        old, new = (one, two) if step % 2 == 0 else (two, one)
        for r in range(8, 8 + rows, 8):
            now, before = old[r : r + 8, :], old[r - 1 : r + 7, :]
            around = (
                old[r + 1 : r + 9, :]
                + before
                + pltpu.roll(now, lanes - 1, 1)
                + pltpu.roll(now, 1, 1)
                - 4.0 * now
            )
            later = (
                now
                + SPREAD_COEFF * around
                - MOBILITY_TERM * (now - before)
                - LIFETIME_DECAY * now
                + source[r - 8 : r, :]
            )
            new[r : r + 8, :] = jnp.where(inside, later, 0.0)
    if last:
        mine = one[pl.ds(8 + (z * plan.gx + x) * plan.slab, plan.slab), :]
        slab_out[...] = mine[:, :cols]
        copies.start(slab_out, outs[0]).wait()
        return
    late = [copies.start(one, outs[0])]
    for a in range(plan.ext // BLOCK_FACTOR):
        top = (plan.planes * z + plan.own * k - DEEP) // BLOCK_FACTOR + a
        spread_row(plan, one[pl.ds(8 + jnp.clip(top, 0, rows - 1), 1), :], charge, a)
    late.append(copies.start(charge, outs[1]))
    wait(late)


def carriers(plan, last, *arrays):
    grid, slab = (plan.grid_rows + 16, plan.lanes), (plan.slab, plan.grid_cols)
    scratch = [
        pltpu.VMEM(arrays[0].shape, F32),
        pltpu.VMEM(grid, F32),
        pltpu.VMEM(grid, F32),
        pltpu.VMEM((plan.grid_rows, plan.lanes), F32),
        pltpu.VMEM(charge_shape(plan), F32),
        pltpu.VMEM(slab, F32),
    ]
    return call(
        plan,
        lambda plan, *refs: carrier_kernel(plan, last, *refs),
        "carriers",
        [slab] if last else [grid, charge_shape(plan)],
        [ANY] + [HBM] * (len(arrays) - 1),
        scratch,
        4,
        2_000_000,
        1_000_000,
    )(*arrays)


def local(ex, ey, ez, hx, hy, hz, medium, table, density):
    raw = (ex, ey, ez, hx, hy, hz)
    plan = Plan(*medium.shape, density.shape[0])

    def send(message, target):
        return lax.ppermute(message, LINE, line_pairs(plan, target))

    def everywhere(message, axes):
        return lax.all_to_all(message, axes, split_axis=0, concat_axis=0, tiled=True)

    core = lambda z, x, k: (z, x, 1 - k)
    beyond = lambda z, k: z - 1 if k == 0 else z + 1

    def exchange(face, strips):
        got = []
        for n, side in enumerate(plan.sides):
            to = functools.partial(across_step, side)
            got.append(send(strips[3 * n], lambda z, x, k: (z, to(x), k)))
            got.append(send(strips[3 * n + 1], lambda z, x, k: (z, to(x), 1 - k)))
            got.append(send(strips[3 * n + 2], lambda z, x, k: (beyond(z, k), to(x), 1 - k)))
        return [send(part, lambda z, x, k: (beyond(z, k), x, 1 - k)) for part in face], got

    other = [send(r, core) for r in raw]
    slab = jnp.pad(density, ((0, 8 - plan.slab), (0, plan.lanes - plan.grid_cols)))
    packed = pack(plan, raw, other, medium, slab, table)
    z_in, strips = exchange(packed[:2], packed[2:-1])
    coef = packed[-1]
    under = slab
    if not plan.paired:
        tiles = plan.gz * plan.gx
        slabs = everywhere(jnp.broadcast_to(density, (tiles,) + density.shape), ("gz", "gx"))
        under = spread_whole(plan, slabs.reshape(plan.grid_rows, plan.grid_cols))
    outs = first_round(plan, strips, z_in, raw, other, medium, slab, under, coef)
    own, core_msg, gens, code = outs[:4]
    gens = everywhere(gens, LINE)
    z_in, strips = exchange(outs[4:5], outs[5:])
    core_in = send(core_msg, core)
    grid, charge = carriers(plan, False, gens)
    outs = second_round(plan, strips, z_in, core_in, own, code, charge, coef)
    halves, sent, gens = outs[:6], outs[6], outs[7]
    gens = everywhere(gens, LINE)
    got = send(sent, core)
    (new_slab,) = carriers(plan, True, gens, grid)
    return tuple(join(plan, halves, got)) + (new_slab,)


def solution(mesh):
    field = P("af", ("group", "gz"), "gx", None)
    slabs = P(("group", "gz", "gx"), None)
    in_specs = (field,) * 6 + (P(("group", "gz"), "gx", None), P(), slabs)
    out_specs = (field,) * 6 + (slabs,)
    return jax.shard_map(local, mesh=mesh, in_specs=in_specs, out_specs=out_specs, check_vma=False)
```

```python
import functools

import jax
import jax.numpy as jnp
from jax import lax
from jax.experimental import pallas as pl
from jax.experimental.pallas import tpu as pltpu
from jax.sharding import PartitionSpec as P

BLOCK_FACTOR = 4
SUBSTEPS = 4
ROUNDS = 2
CSTEPS = 8

COURANT = 0.5
SILICON_PERM = 12.1
OXIDE_PERM = 2.1
SPREAD_COEFF = 0.2
MOBILITY_TERM = 0.1
LIFETIME_DECAY = 0.05
SOURCE_FACTOR = 0.02

DEEP = SUBSTEPS
LINE = ("gz", "gx", "af")
HBM = pl.BlockSpec(memory_space=pltpu.HBM)
ANY = pl.BlockSpec(memory_space=pl.ANY)
SMEM = pl.BlockSpec(memory_space=pltpu.SMEM)
VMEM_LIMIT = 24 * 1024 * 1024
F32 = jnp.float32


class Plan:
    def __init__(self, planes, cols, lanes, slab):
        self.gz = lax.axis_size("gz")
        self.gx = lax.axis_size("gx")
        self.planes, self.cols, self.lanes, self.slab = planes, cols, lanes, slab
        self.own = planes // 2
        self.part = self.own + DEEP
        self.ext = self.own + 2 * DEEP
        self.paired = self.gx == 2
        self.sides = ("face",) if self.paired else ("low", "high")
        self.width = cols + (8 if self.paired else 16)
        self.rows = self.width + 8
        self.tiles = self.width // 8
        self.grid_rows = planes * self.gz // BLOCK_FACTOR
        self.grid_cols = cols * self.gx // BLOCK_FACTOR
        self.devices = self.gz * self.gx * 2

    def first_row(self):
        return 8 * lax.axis_index("gx") if self.paired else 8

    def own_rows(self):
        return pl.ds(pl.multiple_of(self.first_row(), 8), self.cols)


def each_side(plan, act):
    if plan.paired:
        across = lax.axis_index("gx")

        @pl.when(across == 0)
        def _():
            act(0, "high")

        @pl.when(across == 1)
        def _():
            act(0, "low")
    else:
        act(0, "low")
        act(1, "high")


def line_pairs(plan, target):
    pairs = []
    for z in range(plan.gz):
        for x in range(plan.gx):
            for k in range(2):
                tz, tx, tk = target(z, x, k)
                if 0 <= tz < plan.gz and 0 <= tx < plan.gx:
                    pairs.append(((z * plan.gx + x) * 2 + k, (tz * plan.gx + tx) * 2 + tk))
    return pairs


def across_step(side, x):
    if side == "face":
        return 1 - x
    return x + 1 if side == "low" else x - 1


class Copies:
    def __init__(self, sems):
        self.sems, self.made = sems, 0

    def start(self, source, target):
        copy = pltpu.make_async_copy(source, target, self.sems.at[self.made])
        self.made += 1
        copy.start()
        return copy


def wait(copies):
    for copy in copies:
        copy.wait()


def call(plan, body, name, shapes, in_specs, scratch, copies, flops=0, moved=0, aliases=None):
    kernel = pl.pallas_call(
        functools.partial(body, plan),
        out_shape=[pltpu.HBM(s, F32) for s in shapes],
        in_specs=in_specs,
        out_specs=[HBM] * len(shapes),
        scratch_shapes=scratch + [pltpu.SemaphoreType.DMA((copies,))],
        input_output_aliases=aliases or {},
        compiler_params=pltpu.CompilerParams(vmem_limit_bytes=VMEM_LIMIT),
        cost_estimate=pl.CostEstimate(flops=flops, bytes_accessed=moved, transcendentals=0),
        name=name,
    )

    def run(*args):
        placed = []
        for arg, spec in zip(args, in_specs):
            in_hbm = spec.memory_space is pltpu.HBM
            placed.append(pltpu.with_memory_space_constraint(arg, pltpu.HBM) if in_hbm else arg)
        return kernel(*placed)

    return run


def pack_kernel(plan, *refs):
    raw, other, medium, nside = refs[:6], refs[6:12], refs[12], len(plan.sides)
    slab_in, table_in = refs[13:15]
    outs = refs[15 : 18 + 2 * nside]
    edge, edge_code, face, face_code, strips, corners, slab, table, coef, sems = refs[18 + 2 * nside :]
    copies = Copies(sems)
    k = lax.axis_index("af")
    mine = pl.ds((plan.own - DEEP) * k, plan.part)
    outer = pl.ds((plan.planes - DEEP) * k, DEEP)
    if plan.paired:
        tile_rows = [pl.multiple_of((plan.cols - 8) * (1 - lax.axis_index("gx")), 8)]
    else:
        tile_rows = [plan.cols - 8, 0]
    early, late, last = [], [], []
    early.append(copies.start(slab_in, slab))
    early.append(copies.start(table_in, table))
    for n, row in enumerate(tile_rows):
        for c in range(6):
            side = pl.ds(row, 8)
            early.append(copies.start(raw[c].at[0, mine, side, :], edge.at[n, c]))
            early.append(copies.start(other[c].at[0, mine, side, :], edge.at[n, 6 + c]))
        early.append(copies.start(medium.at[mine, pl.ds(row, 8), :], edge_code.at[n]))
    for c in range(6):
        late.append(copies.start(raw[c].at[0, outer], face.at[pl.ds(DEEP * c, DEEP)]))
        late.append(copies.start(other[c].at[0, outer], face.at[pl.ds(DEEP * (6 + c), DEEP)]))
    late.append(copies.start(medium.at[outer], face_code))
    wait(early)
    rows = plan.part // 2

    def fill(slot, low):
        def one(q, _):
            for h in range(2):
                four = slice(4 * h, 4 * h + 4)
                for c in range(12):
                    strips[slot, c * rows + q, four, :] = edge[slot, c, 2 * q + h, low : low + 4, :]
                code = edge_code[slot, 2 * q + h, low : low + 4, :]
                strips[slot, 12 * rows + q, four, :] = code.astype(F32)
            return 0

        lax.fori_loop(0, rows, one, 0)

    each_side(plan, lambda slot, side: fill(slot, 4 if plan.paired == (side == "high") else 0))
    page, half = slab[...], DEEP // 2
    for n in range(nside):
        strips[n, 13 * rows] = page
        last.append(copies.start(strips.at[n], outs[2 + 2 * n]))
        corners[n, 13 * half] = page
        for c in range(13):
            for h in range(half):
                corners[n, half * c + h] = strips[n, rows * c + (rows - half) * k + h]
        last.append(copies.start(corners.at[n], outs[3 + 2 * n]))
    own, partner = jnp.where(k == 0, table[0:1], table[1:2]), jnp.where(k == 0, table[1:2], table[0:1])
    for s, row in enumerate((own, partner)):
        kerr, two, free = row[:, 0:1], row[:, 1:2], row[:, 2:3]
        for n, value in enumerate((kerr, two, 0.5 * two, 0.5 * free)):
            coef[4 * s + n] = jnp.broadcast_to(value, (8, plan.lanes))
    last.append(copies.start(coef, outs[-1]))
    wait(late)
    face[12 * DEEP : 13 * DEEP] = face_code[...].astype(F32)
    face[13 * DEEP, 0:8, :] = page
    for r in range(8, plan.cols, 8):
        face[13 * DEEP, r : r + 8, :] = page
    send_face(plan, copies, last, face, outs[:2])
    wait(last)


def face_split(plan, pages):
    if pages == 12 * DEEP:
        return ((0, pages),)
    first = (pages + 1) // 2
    return ((0, first), (first, pages - first))


def send_face(plan, copies, started, face, outs):
    for out, (start, count) in zip(outs, face_split(plan, face.shape[0])):
        started.append(copies.start(face.at[pl.ds(start, count)], out))


def get_face(plan, copies, parts, pages, first, targets):
    started = []
    for part, (start, count) in zip(parts, face_split(plan, pages)):
        low, high = max(first, start), min(first + DEEP, start + count)
        if low < high:
            source = part.at[pl.ds(low - start, high - low)]
            started.append(copies.start(source, targets(low - first, high - low)))
    return started


def strip_tiles(plan, comps):
    if comps == 12:
        return comps * plan.own // 2
    return comps * plan.part // 2 + 1


def send_strips(plan, copies, started, strips, corners, outs, comps):
    k = lax.axis_index("af")
    half, top = DEEP // 2, (plan.own - DEEP) // 2
    for n in range(len(plan.sides)):
        started.append(copies.start(strips.at[n], outs[3 * n]))
        for e, begin in enumerate((top * (1 - k), top * k)):
            for c in range(comps):
                for h in range(half):
                    corners[n, e, half * c + h] = strips[n, plan.own // 2 * c + begin + h]
            started.append(copies.start(corners.at[n, e], outs[3 * n + 1 + e]))


def corner_tiles(plan, comps):
    return comps * DEEP // 2 + (comps > 12)


def strip_shapes(plan, comps):
    tiles = corner_tiles(plan, comps)
    one = [strip_tiles(plan, comps)] + [tiles] * (1 if comps > 12 else 2)
    return [(count, 8, plan.lanes) for count in one * len(plan.sides)]


def face_shapes(plan, pages):
    return [(count, plan.cols, plan.lanes) for _, count in face_split(plan, pages)]


def pack(plan, raw, other, medium, slab, table):
    wide = (plan.cols, plan.lanes)
    nside = len(plan.sides)
    pages = 13 * DEEP + 1
    scratch = [
        pltpu.VMEM((nside, 12, plan.part, 8, plan.lanes), F32),
        pltpu.VMEM((nside, plan.part, 8, plan.lanes), jnp.int32),
        pltpu.VMEM((pages,) + wide, F32),
        pltpu.VMEM((DEEP,) + wide, jnp.int32),
        pltpu.VMEM((nside, strip_tiles(plan, 13), 8, plan.lanes), F32),
        pltpu.VMEM((nside, corner_tiles(plan, 13), 8, plan.lanes), F32),
        pltpu.VMEM((8, plan.lanes), F32),
        pltpu.VMEM(table.shape, F32),
        pltpu.VMEM((8, 8, plan.lanes), F32),
    ]
    return call(
        plan,
        pack_kernel,
        "pack",
        face_shapes(plan, pages) + strip_shapes(plan, 13) + [(8, 8, plan.lanes)],
        [HBM] * 6 + [ANY] * 6 + [HBM, ANY, HBM],
        scratch,
        16 * nside + 18,
        moved=4_000_000,
    )(*raw, *other, medium, slab, table)


def clear(plan, old, new, code):
    zero = jnp.zeros((8, plan.lanes), F32)

    def halo(slot, side):
        tile = plan.tiles - 1 if side == "high" else 0

        def one(p, _):
            for ref in list(old) + code:
                ref[p, 8 * tile : 8 * tile + 8, :] = zero
            return 0

        lax.fori_loop(0, plan.ext, one, 0)

    each_side(plan, halo)

    def above(p, _):
        for c in (1, 2, 7, 8):
            for ref in (old[c], new[c]):
                ref[p, plan.width : plan.width + 8, :] = zero
        return 0

    lax.fori_loop(0, plan.ext, above, 0)
    for c, ref in enumerate(new):
        plane = DEEP + plan.own if c % 6 < 3 else DEEP - 1
        for t in range(plan.tiles):
            ref[plane, 8 * t : 8 * t + 8, :] = zero


def strip_row(plan, side):
    if side == "low":
        return 4
    return plan.cols if plan.paired else 8 + plan.cols


def spread_strip(refs, strip, each, begin, at, plane, pairs):
    def one(q, _):
        for c, ref in refs:
            for h in range(2):
                tile = c * each + begin + q
                ref[plane + 2 * q + h, at : at + 4, :] = strip[tile, 4 * h : 4 * h + 4, :]
        return 0

    lax.fori_loop(0, pairs, one, 0)


def substeps(plan, first, second, base, silicon, charge, gen, coef):
    lanes = plan.lanes
    tile = (8, lanes)
    lane = lax.broadcasted_iota(jnp.int32, tile, 1)
    row = lax.broadcasted_iota(jnp.int32, tile, 0)
    keep_up, keep_down, at_top = lane < lanes - 1, lane > 0, row == 0
    z, x, k = (lax.axis_index(a) for a in LINE)
    at_low = jnp.logical_and(z == 0, k == 0)
    at_high = jnp.logical_and(z == plan.gz - 1, k == 1)

    def up(v):
        return jnp.where(keep_up, pltpu.roll(v, lanes - 1, 1), 0.0)

    def down(v):
        return jnp.where(keep_down, pltpu.roll(v, 1, 1), 0.0)

    def edge_mask(t):
        if plan.paired or t not in (0, plan.tiles - 1):
            return None
        off = (x == 0) if t == 0 else (x == plan.gx - 1)
        return jnp.where(off, 0.0, 1.0)

    def magnetic(old, new, s, p, t):
        ex, ey, ez, hx, hy, hz = old[6 * s : 6 * s + 6]
        here, beside = slice(8 * t, 8 * t + 8), slice(8 * t + 1, 8 * t + 9)
        vx, vy, vz = ex[p, here, :], ey[p, here, :], ez[p, here, :]
        nx = hx[p, here, :] - COURANT * ((up(vz) - vz) - (ey[p + 1, here, :] - vy))
        ny = hy[p, here, :] - COURANT * ((ex[p + 1, here, :] - vx) - (ez[p, beside, :] - vz))
        nz = hz[p, here, :] - COURANT * ((ey[p, beside, :] - vy) - (up(vx) - vx))
        mask = edge_mask(t)
        if mask is not None:
            nx, ny, nz = nx * mask, ny * mask, nz * mask
        new[6 * s + 3][p, here, :] = nx
        new[6 * s + 4][p, here, :] = ny
        new[6 * s + 5][p, here, :] = nz

    def electric(old, new, p, t):
        coarse = p // BLOCK_FACTOR
        here = slice(8 * t, 8 * t + 8)
        volts = [[old[6 * s + c][p, here, :] for c in range(3)] for s in range(2)]
        strength = [v[0] * v[0] + v[1] * v[1] + v[2] * v[2] for v in volts]
        is_silicon = silicon[p, here, :]
        total = (strength[0] + strength[1]) * is_silicon
        carriers = charge[coarse, here, :] * is_silicon
        ground = base[p, here, :]
        gen[p, here, :] += (coef[1] * strength[0] + coef[5] * strength[1]) * total
        mask = edge_mask(t)
        for s in range(2):
            vx, vy, vz = volts[s]
            hx, hy, hz = new[6 * s + 3 : 6 * s + 6]
            nx, ny, nz = hx[p, here, :], hy[p, here, :], hz[p, here, :]
            if t == 0:
                left_y = jnp.where(at_top, 0.0, pltpu.roll(ny, 1, 0))
                left_z = jnp.where(at_top, 0.0, pltpu.roll(nz, 1, 0))
            else:
                before = slice(8 * t - 1, 8 * t + 7)
                left_y, left_z = hy[p, before, :], hz[p, before, :]
            loss = coef[4 * s + 2] * total + coef[4 * s + 3] * carriers
            perm = ground + coef[4 * s] * total
            inv = pl.reciprocal(perm + loss, approx=True)
            keep = (perm - loss) * inv
            push = COURANT * inv
            if mask is not None:
                push = push * mask
            curl_x = (nz - down(nz)) - (ny - hy[p - 1, here, :])
            curl_y = (nx - hx[p - 1, here, :]) - (nz - left_z)
            curl_z = (ny - left_y) - (nx - down(nx))
            new[6 * s][p, here, :] = keep * vx + push * curl_x
            new[6 * s + 1][p, here, :] = keep * vy + push * curl_y
            new[6 * s + 2][p, here, :] = keep * vz + push * curl_z

    def magnetic_plane(old, new, p):
        for t in range(plan.tiles):
            for s in range(2):
                magnetic(old, new, s, p, t)

    def substep(old, new, n):
        begin = jnp.where(at_low, DEEP, n + 1)
        end = jnp.where(at_high, DEEP + plan.own, plan.ext - 1 - n)
        odd = lax.rem(end - begin, 2)

        @pl.when(jnp.logical_not(at_low))
        def _():
            magnetic_plane(old, new, n)
            magnetic_plane(old, new, n + 1)

        @pl.when(at_low)
        def _():
            magnetic_plane(old, new, DEEP)

        def advance(p):
            for t in range(plan.tiles):
                electric(old, new, p, t)
                for s in range(2):
                    magnetic(old, new, s, p + 1, t)

        @pl.when(odd == 1)
        def _():
            advance(begin)

        def step(m, _):
            p = begin + odd + 2 * m
            advance(p)
            advance(p + 1)
            return 0

        lax.fori_loop(0, (end - begin) // 2, step, 0)

    def pair(m, _):
        substep(first, second, 2 * m)
        substep(second, first, 2 * m + 1)
        return 0

    lax.fori_loop(0, SUBSTEPS // 2, pair, 0)


def set_media(plan, code, base, silicon):
    def one(p, _):
        for t in range(plan.tiles):
            here = slice(8 * t, 8 * t + 8)
            v = code[p, here, :]
            base[p, here, :] = jnp.where(v == 0.0, SILICON_PERM, jnp.where(v == 1.0, OXIDE_PERM, 1.0))
            silicon[p, here, :] = jnp.where(v == 0.0, 1.0, 0.0)
        return 0

    lax.fori_loop(0, plan.ext, one, 0)


def clear_generation(plan, gen):
    def one(p, _):
        gen[p] = jnp.zeros((plan.rows, plan.lanes), F32)
        return 0

    lax.fori_loop(DEEP, DEEP + plan.own, one, 0)


def sum_generation(plan, gen, message):
    blocks = plan.cols // BLOCK_FACTOR
    shape = (blocks, plan.lanes)
    column = lax.broadcasted_iota(jnp.int32, shape, 0) + blocks * lax.axis_index("gx")
    upright = lax.broadcasted_iota(jnp.int32, shape, 1) == column
    across = plan.own_rows()
    for a in range(plan.own // BLOCK_FACTOR):
        p = DEEP + BLOCK_FACTOR * a
        rows = (gen[p, across, :] + gen[p + 1, across, :]) + (
            gen[p + 2, across, :] + gen[p + 3, across, :]
        )
        cells = rows.reshape(blocks, BLOCK_FACTOR, plan.lanes).sum(1)
        mean = cells.sum(1, keepdims=True) * (1.0 / (BLOCK_FACTOR * BLOCK_FACTOR * plan.lanes))
        message[a : a + 1, :] = jnp.where(upright, mean, 0.0).sum(0, keepdims=True)


def round_scratch(plan):
    wide = (plan.ext, plan.rows, plan.lanes)
    return [pltpu.VMEM((plan.ext + 1, plan.rows, plan.lanes), F32)] * 24 + [
        pltpu.VMEM(wide, F32)
    ] * 3 + [
        pltpu.VMEM((plan.ext // BLOCK_FACTOR, plan.width, plan.lanes), F32),
        pltpu.VMEM((8, plan.lanes), F32),
        pltpu.VMEM((8, 8, plan.lanes), F32),
        pltpu.VMEM(wide, F32),
    ]


def round_flops(plan):
    return SUBSTEPS * plan.ext * plan.width * plan.lanes * 150


def generation_shape(plan):
    return (plan.devices, 8, plan.lanes)


def place_strips(plan, old, code, strips):
    k = lax.axis_index("af")
    outward, inner = plan.part * k, plan.part * (1 - k)

    def place(slot, side):
        at = strip_row(plan, side)
        same = list(enumerate(list(old) + code))
        flipped = list(enumerate(list(old[6:]) + list(old[:6]) + code))
        half, rows = DEEP // 2, plan.own // 2
        if code:
            whole, corner = strips[2 * slot : 2 * slot + 2]
            near, rows = DEEP * (1 - k), plan.part // 2
            spread_strip(same, whole, rows, 0, at, near, rows)
            spread_strip(flipped, corner, half, 0, at, outward, half)
            return
        whole, beside, corner = strips[3 * slot : 3 * slot + 3]
        spread_strip(same, whole, rows, 0, at, DEEP, rows)
        spread_strip(flipped, beside, half, 0, at, inner, half)
        spread_strip(flipped, corner, half, 0, at, outward, half)

    each_side(plan, place)


def send_generation(plan, copies, started, gen, message, gen_out):
    sum_generation(plan, gen, message)
    for d in range(plan.devices):
        started.append(copies.start(message, gen_out.at[d]))


def charge_from_slabs(plan, charge, mine, across, chip, corner):
    across, chip = chip, across
    x, k = lax.axis_index("gx"), lax.axis_index("af")
    slab = plan.slab
    left = jnp.where(x == 0, mine, across)
    right = jnp.where(x == 0, across, mine)
    beyond = jnp.where(x != k, chip, corner)
    body = jnp.where(k == 0, left, right)
    before = jnp.where(k == 0, beyond, left)[slab - 1 : slab]
    after = jnp.where(k == 0, right, beyond)[0:1]
    for a in range(slab + 2):
        row = before if a == 0 else after if a == slab + 1 else body[a - 1 : a]
        spread_row(plan, row, charge, a)


def spread_row(plan, row, charge, a):
    left = (plan.cols * lax.axis_index("gx") - plan.first_row()) // BLOCK_FACTOR
    row = jnp.broadcast_to(row, (8, plan.lanes))
    row = pltpu.roll(row, lax.rem(plan.lanes - left, plan.lanes), 1)
    for c in range(plan.width // BLOCK_FACTOR):
        charge[a, 4 * c : 4 * c + 4, :] = jnp.broadcast_to(row[0:4, c : c + 1], (4, plan.lanes))


def first_kernel(plan, *refs):
    nside = len(plan.sides)
    strips_in, refs = refs[: 2 * nside], refs[2 * nside :]
    z_in, raw, other = refs[:2], refs[2:8], refs[8:14]
    medium, slab_in, under_in, coef_in = refs[14:18]
    own_out, core_out, gen_out, code_out = refs[18:22]
    z_out, strip_out = refs[22], refs[23 : 23 + 3 * nside]
    rest = refs[23 + 3 * nside :]
    old, new, (base, silicon, gen, charge, message, coef, code) = rest[:12], rest[12:24], rest[24:31]
    codes, strips, (strip_mine, corners, slabs, sems) = rest[31], rest[32 : 32 + 2 * nside], rest[-4:]
    copies = Copies(sems)
    k = lax.axis_index("af")
    near = DEEP * (1 - k)
    far = plan.part * k
    across = plan.own_rows()
    here = pl.ds(near, plan.part)
    mine = pl.ds((plan.own - DEEP) * k, plan.part)
    early = [copies.start(medium.at[mine], codes)]
    pages = 13 * DEEP + 1
    early += get_face(
        plan, copies, z_in, pages, 12 * DEEP, lambda p, n: code.at[pl.ds(far + p, n), across]
    )
    early.append(copies.start(slab_in, slabs.at[0]))
    if plan.paired:
        early.append(copies.start(z_in[1].at[z_in[1].shape[0] - 1, pl.ds(0, 8)], slabs.at[1]))
    else:
        early.append(copies.start(under_in, charge))
    early.append(copies.start(coef_in, coef))
    for source, target in zip(strips_in, strips):
        early.append(copies.start(source, target))
    late = []
    for c in range(6):
        late.append(copies.start(raw[c].at[0, mine], old[c].at[here, across]))
        late.append(copies.start(other[c].at[0, mine], old[6 + c].at[here, across]))
    for c in range(12):
        late += get_face(
            plan,
            copies,
            z_in,
            pages,
            DEEP * ((c + 6) % 12),
            lambda p, n, ref=old[c]: ref.at[pl.ds(far + p, n), across],
        )
    clear(plan, old, new, [code])
    clear_generation(plan, gen)
    wait(early)

    def settle(p, _):
        code[near + p, across, :] = codes[p].astype(F32)
        return 0

    lax.fori_loop(0, plan.part, settle, 0)
    place_strips(plan, old, [code], strips)
    set_media(plan, code, base, silicon)
    if plan.paired:
        charge_from_slabs(
            plan, charge, slabs[0], slabs[1], strips[0][13 * plan.part // 2], strips[1][13 * DEEP // 2]
        )
    wait(late)
    substeps(plan, old, new, base, silicon, charge, gen, coef)
    copies = Copies(sems)
    late = []

    def gather(slot, side):
        high_end = (side == "high") if plan.paired else (side == "low")
        low = 0 if plan.paired and side == "high" else 8
        at = low + plan.cols - 4 if high_end else low

        def one(q, _):
            for c in range(12):
                for h in range(2):
                    tile = plan.own // 2 * c + q
                    strip_mine[slot, tile, 4 * h : 4 * h + 4, :] = old[c][
                        DEEP + 2 * q + h, at : at + 4, :
                    ]
            return 0

        lax.fori_loop(0, plan.own // 2, one, 0)

    toward = DEEP + (plan.own - DEEP) * k
    inward = DEEP + (plan.own - DEEP) * (1 - k)
    for c in range(12):
        source = old[c].at[pl.ds(toward, DEEP), across]
        late.append(copies.start(source, z_out.at[pl.ds(DEEP * c, DEEP)]))
        late.append(copies.start(old[c].at[pl.ds(inward, DEEP), across], core_out.at[c]))
        late.append(copies.start(old[c].at[pl.ds(DEEP, plan.own), across], own_out.at[c]))
    late.append(copies.start(code, code_out))
    message[4:8, :] = slabs[0, 0:4, :]
    each_side(plan, gather)
    send_strips(plan, copies, late, strip_mine, corners, strip_out, 12)
    send_generation(plan, copies, late, gen, message, gen_out)
    wait(late)


def first_round(plan, strips, z_in, raw, other, medium, slab, under, coef):
    wide = (plan.cols, plan.lanes)
    nside = len(plan.sides)
    shapes = [
        (12, plan.own) + wide,
        (12, DEEP) + wide,
        generation_shape(plan),
        (plan.ext, plan.rows, plan.lanes),
    ]
    shapes += face_shapes(plan, 12 * DEEP) + strip_shapes(plan, 12)
    scratch = round_scratch(plan) + [pltpu.VMEM((plan.part,) + wide, jnp.int32)]
    scratch += [pltpu.VMEM(s.shape, F32) for s in strips]
    scratch += [
        pltpu.VMEM((nside, strip_tiles(plan, 12), 8, plan.lanes), F32),
        pltpu.VMEM((nside, 2, corner_tiles(plan, 12), 8, plan.lanes), F32),
        pltpu.VMEM((2, 8, plan.lanes), F32),
    ]
    return call(
        plan,
        first_kernel,
        "first_round",
        shapes,
        [ANY] * (2 + 2 * nside) + [HBM] * 6 + [ANY] * 6 + [HBM, ANY, ANY, HBM],
        scratch,
        42 + 3 * nside + plan.devices,
        round_flops(plan),
        10_000_000,
    )(*strips, *z_in, *raw, *other, medium, slab, under, coef)


def second_kernel(plan, *refs):
    nside = len(plan.sides)
    strips_in, refs = refs[: 3 * nside], refs[3 * nside :]
    z_in, (core_in, own_in, code_in, charge_in, coef_in) = refs[:1], refs[1:6]
    kept, sent, gen_out, rest = refs[6:12], refs[12], refs[13], refs[14:]
    old, new, (base, silicon, gen, charge, message, coef, code) = rest[:12], rest[12:24], rest[24:31]
    strips, sems = rest[31:-1], rest[-1]
    copies = Copies(sems)
    k = lax.axis_index("af")
    across = plan.own_rows()
    outward = plan.part * k
    inner = plan.part * (1 - k)
    early = [copies.start(code_in, code), copies.start(charge_in, charge)]
    early.append(copies.start(coef_in, coef))
    for source, target in zip(strips_in, strips):
        early.append(copies.start(source, target))
    late = []
    for c in range(12):
        flip = (c + 6) % 12
        late.append(copies.start(own_in.at[c], old[c].at[pl.ds(DEEP, plan.own), across]))
        late += get_face(
            plan,
            copies,
            z_in,
            12 * DEEP,
            DEEP * flip,
            lambda p, n, ref=old[c]: ref.at[pl.ds(outward + p, n), across],
        )
        late.append(copies.start(core_in.at[flip], old[c].at[pl.ds(inner, DEEP), across]))
    clear(plan, old, new, [])
    clear_generation(plan, gen)
    wait(early)
    place_strips(plan, old, [], strips)
    set_media(plan, code, base, silicon)
    wait(late)
    substeps(plan, old, new, base, silicon, charge, gen, coef)
    copies = Copies(sems)
    late = []
    for c in range(6):
        late.append(copies.start(old[6 + c].at[pl.ds(DEEP, plan.own), across], sent.at[c]))
    for c in range(6):
        target = kept[c].at[0, pl.ds(plan.own * k, plan.own)]
        late.append(copies.start(old[c].at[pl.ds(DEEP, plan.own), across], target))
    message[...] = jnp.zeros(message.shape, F32)
    send_generation(plan, copies, late, gen, message, gen_out)
    wait(late)


def second_round(plan, strips, z_in, core_in, own_in, code, charge, coef):
    wide = (plan.cols, plan.lanes)
    nside = len(plan.sides)
    shapes = [(1, plan.planes) + wide] * 6 + [(6, plan.own) + wide, generation_shape(plan)]
    scratch = round_scratch(plan) + [pltpu.VMEM(s.shape, F32) for s in strips]
    return call(
        plan,
        second_kernel,
        "second_round",
        shapes,
        [ANY] * (2 + 3 * nside) + [HBM] * 4,
        scratch,
        39 + 3 * nside + plan.devices,
        round_flops(plan),
        10_000_000,
    )(*strips, *z_in, core_in, own_in, code, charge, coef)


def join_kernel(plan, *refs):
    got, outs, (half, sems) = refs[6], refs[7:13], refs[13:]
    copies = Copies(sems)
    rows = pl.ds(plan.own * (1 - lax.axis_index("af")), plan.own)
    early = [copies.start(got.at[c], half.at[c]) for c in range(6)]
    late = []
    for c in range(6):
        early[c].wait()
        late.append(copies.start(half.at[c], outs[c].at[0, rows]))
    wait(late)


def join(plan, halves, got):
    shapes = [h.shape for h in halves]
    aliases = {c: c for c in range(6)}
    scratch = [pltpu.VMEM(got.shape, F32)]
    return call(
        plan, join_kernel, "join", shapes, [HBM] * 6 + [ANY], scratch, 12, moved=3_000_000, aliases=aliases
    )(*halves, got)


def charge_shape(plan):
    return (plan.ext // BLOCK_FACTOR, plan.width, plan.lanes)


def spread_whole(plan, density):
    z, x, k = (lax.axis_index(a) for a in LINE)
    side = plan.width // BLOCK_FACTOR
    padded = jnp.pad(density, ((1, 1), (side, side)))
    top = (plan.planes * z + plan.own * k) // BLOCK_FACTOR
    left = side + (plan.cols * x - plan.first_row()) // BLOCK_FACTOR
    tile = lax.dynamic_slice(padded, (top, left), (plan.ext // BLOCK_FACTOR, side))
    return jnp.broadcast_to(jnp.repeat(tile, BLOCK_FACTOR, 1)[:, :, None], charge_shape(plan))


def carrier_kernel(plan, last, *refs):
    gens_in, refs = refs[0], refs[1:]
    if last:
        density_in, refs = refs[0], refs[1:]
    outs = refs[:1] if last else refs[:2]
    gens, one, two, source, charge, slab_out, sems = refs[len(outs) :]
    copies = Copies(sems)
    rows, cols, lanes = plan.grid_rows, plan.grid_cols, plan.lanes
    z, x, k = (lax.axis_index(a) for a in LINE)
    own = plan.own // BLOCK_FACTOR
    early = [copies.start(gens_in, gens)]
    if last:
        early.append(copies.start(density_in, one))
    zero = jnp.zeros((8, lanes), F32)
    for ref in (two,) if last else (one, two):
        ref[0:8, :] = zero
        ref[8 + rows : 16 + rows, :] = zero
    wait(early)

    def unpack(line, _):
        top = pl.multiple_of(8 * line, 8)
        for dk in range(2):
            tiles = [gens[(line * plan.gx + dx) * 2 + dk, 0:own, :] for dx in range(plan.gx)]
            source[pl.ds(top + own * dk, own), :] = SOURCE_FACTOR * functools.reduce(jnp.add, tiles)
        if not last:
            for dx in range(plan.gx):
                slab = gens[(line * plan.gx + dx) * 2, 4 : 4 + plan.slab, :]
                one[pl.ds(8 + top + plan.slab * dx, plan.slab), :] = slab
        return 0

    lax.fori_loop(0, plan.gz, unpack, 0, unroll=plan.gz <= 4)
    inside = lax.broadcasted_iota(jnp.int32, (8, lanes), 1) < cols
    for step in range(CSTEPS):
        old, new = (one, two) if step % 2 == 0 else (two, one)
        for r in range(8, 8 + rows, 8):
            now, before = old[r : r + 8, :], old[r - 1 : r + 7, :]
            around = (
                old[r + 1 : r + 9, :]
                + before
                + pltpu.roll(now, lanes - 1, 1)
                + pltpu.roll(now, 1, 1)
                - 4.0 * now
            )
            later = (
                now
                + SPREAD_COEFF * around
                - MOBILITY_TERM * (now - before)
                - LIFETIME_DECAY * now
                + source[r - 8 : r, :]
            )
            new[r : r + 8, :] = jnp.where(inside, later, 0.0)
    if last:
        mine = one[pl.ds(8 + (z * plan.gx + x) * plan.slab, plan.slab), :]
        slab_out[...] = mine[:, :cols]
        copies.start(slab_out, outs[0]).wait()
        return
    late = [copies.start(one, outs[0])]
    for a in range(plan.ext // BLOCK_FACTOR):
        top = (plan.planes * z + plan.own * k - DEEP) // BLOCK_FACTOR + a
        spread_row(plan, one[pl.ds(8 + jnp.clip(top, 0, rows - 1), 1), :], charge, a)
    late.append(copies.start(charge, outs[1]))
    wait(late)


def carriers(plan, last, *arrays):
    grid, slab = (plan.grid_rows + 16, plan.lanes), (plan.slab, plan.grid_cols)
    scratch = [
        pltpu.VMEM(arrays[0].shape, F32),
        pltpu.VMEM(grid, F32),
        pltpu.VMEM(grid, F32),
        pltpu.VMEM((plan.grid_rows, plan.lanes), F32),
        pltpu.VMEM(charge_shape(plan), F32),
        pltpu.VMEM(slab, F32),
    ]
    return call(
        plan,
        lambda plan, *refs: carrier_kernel(plan, last, *refs),
        "carriers",
        [slab] if last else [grid, charge_shape(plan)],
        [ANY] + [HBM] * (len(arrays) - 1),
        scratch,
        4,
        2_000_000,
        1_000_000,
    )(*arrays)


def local(ex, ey, ez, hx, hy, hz, medium, table, density):
    raw = (ex, ey, ez, hx, hy, hz)
    plan = Plan(*medium.shape, density.shape[0])

    def send(message, target):
        return lax.ppermute(message, LINE, line_pairs(plan, target))

    def everywhere(message, axes):
        return lax.all_to_all(message, axes, split_axis=0, concat_axis=0, tiled=True)

    core = lambda z, x, k: (z, x, 1 - k)
    beyond = lambda z, k: z - 1 if k == 0 else z + 1

    def exchange(face, strips):
        got, each = [], len(strips) // len(plan.sides)
        for n, side in enumerate(plan.sides):
            to = functools.partial(across_step, side)
            mine = strips[each * n : each * n + each]
            got.append(send(mine[0], lambda z, x, k: (z, to(x), k)))
            if each == 3:
                got.append(send(mine[1], lambda z, x, k: (z, to(x), 1 - k)))
            got.append(send(mine[-1], lambda z, x, k: (beyond(z, k), to(x), 1 - k)))
        return [send(part, lambda z, x, k: (beyond(z, k), x, 1 - k)) for part in face], got

    other = [send(r, core) for r in raw]
    slab = jnp.pad(density, ((0, 8 - plan.slab), (0, plan.lanes - plan.grid_cols)))
    packed = pack(plan, raw, other, medium, slab, table)
    z_in, strips = exchange(packed[:2], packed[2:-1])
    coef = packed[-1]
    under = slab
    if not plan.paired:
        tiles = plan.gz * plan.gx
        slabs = everywhere(jnp.broadcast_to(density, (tiles,) + density.shape), ("gz", "gx"))
        under = spread_whole(plan, slabs.reshape(plan.grid_rows, plan.grid_cols))
    outs = first_round(plan, strips, z_in, raw, other, medium, slab, under, coef)
    own, core_msg, gens, code = outs[:4]
    gens = everywhere(gens, LINE)
    z_in, strips = exchange(outs[4:5], outs[5:])
    core_in = send(core_msg, core)
    grid, charge = carriers(plan, False, gens)
    outs = second_round(plan, strips, z_in, core_in, own, code, charge, coef)
    halves, sent, gens = outs[:6], outs[6], outs[7]
    gens = everywhere(gens, LINE)
    got = send(sent, core)
    (new_slab,) = carriers(plan, True, gens, grid)
    return tuple(join(plan, halves, got)) + (new_slab,)


def solution(mesh):
    field = P("af", ("group", "gz"), "gx", None)
    slabs = P(("group", "gz", "gx"), None)
    in_specs = (field,) * 6 + (P(("group", "gz"), "gx", None), P(), slabs)
    out_specs = (field,) * 6 + (slabs,)
    return jax.shard_map(local, mesh=mesh, in_specs=in_specs, out_specs=out_specs, check_vma=False)
```

```python
import functools

import jax
import jax.numpy as jnp
from jax import lax
from jax.experimental import pallas as pl
from jax.experimental.pallas import tpu as pltpu
from jax.sharding import PartitionSpec as P

BLOCK_FACTOR = 4
SUBSTEPS = 4
ROUNDS = 2
CSTEPS = 8

COURANT = 0.5
SILICON_PERM = 12.1
OXIDE_PERM = 2.1
SPREAD_COEFF = 0.2
MOBILITY_TERM = 0.1
LIFETIME_DECAY = 0.05
SOURCE_FACTOR = 0.02

DEEP = SUBSTEPS
LINE = ("gz", "gx", "af")
HBM = pl.BlockSpec(memory_space=pltpu.HBM)
ANY = pl.BlockSpec(memory_space=pl.ANY)
SMEM = pl.BlockSpec(memory_space=pltpu.SMEM)
VMEM_LIMIT = 24 * 1024 * 1024
F32 = jnp.float32


class Plan:
    def __init__(self, planes, cols, lanes, slab):
        self.gz = lax.axis_size("gz")
        self.gx = lax.axis_size("gx")
        self.planes, self.cols, self.lanes, self.slab = planes, cols, lanes, slab
        self.own = planes // 2
        self.part = self.own + DEEP
        self.ext = self.own + 2 * DEEP
        self.paired = self.gx == 2
        self.sides = ("face",) if self.paired else ("low", "high")
        self.width = cols + (8 if self.paired else 16)
        self.rows = self.width + 8
        self.tiles = self.width // 8
        self.grid_rows = planes * self.gz // BLOCK_FACTOR
        self.grid_cols = cols * self.gx // BLOCK_FACTOR
        self.devices = self.gz * self.gx * 2

    def first_row(self):
        return 8 * lax.axis_index("gx") if self.paired else 8

    def own_rows(self):
        return pl.ds(pl.multiple_of(self.first_row(), 8), self.cols)


def each_side(plan, act):
    if plan.paired:
        across = lax.axis_index("gx")

        @pl.when(across == 0)
        def _():
            act(0, "high")

        @pl.when(across == 1)
        def _():
            act(0, "low")
    else:
        act(0, "low")
        act(1, "high")


def line_pairs(plan, target):
    pairs = []
    for z in range(plan.gz):
        for x in range(plan.gx):
            for k in range(2):
                tz, tx, tk = target(z, x, k)
                if 0 <= tz < plan.gz and 0 <= tx < plan.gx:
                    pairs.append(((z * plan.gx + x) * 2 + k, (tz * plan.gx + tx) * 2 + tk))
    return pairs


def across_step(side, x):
    if side == "face":
        return 1 - x
    return x + 1 if side == "low" else x - 1


class Copies:
    def __init__(self, sems):
        self.sems, self.made = sems, 0

    def start(self, source, target):
        copy = pltpu.make_async_copy(source, target, self.sems.at[self.made])
        self.made += 1
        copy.start()
        return copy


def wait(copies):
    for copy in copies:
        copy.wait()


def call(plan, body, name, shapes, in_specs, scratch, copies, flops=0, moved=0, aliases=None):
    kernel = pl.pallas_call(
        functools.partial(body, plan),
        out_shape=[pltpu.HBM(s, F32) for s in shapes],
        in_specs=in_specs,
        out_specs=[HBM] * len(shapes),
        scratch_shapes=scratch + [pltpu.SemaphoreType.DMA((copies,))],
        input_output_aliases=aliases or {},
        compiler_params=pltpu.CompilerParams(vmem_limit_bytes=VMEM_LIMIT),
        cost_estimate=pl.CostEstimate(flops=flops, bytes_accessed=moved, transcendentals=0),
        name=name,
    )

    def run(*args):
        placed = []
        for arg, spec in zip(args, in_specs):
            in_hbm = spec.memory_space is pltpu.HBM
            placed.append(pltpu.with_memory_space_constraint(arg, pltpu.HBM) if in_hbm else arg)
        return kernel(*placed)

    return run


def pack_kernel(plan, *refs):
    raw, other, medium, nside = refs[:6], refs[6:12], refs[12], len(plan.sides)
    slab_in, table_in = refs[13:15]
    outs = refs[15 : 18 + 2 * nside]
    edge, edge_code, face, face_code, strips, corners, slab, table, coef, sems = refs[18 + 2 * nside :]
    copies = Copies(sems)
    k = lax.axis_index("af")
    mine = pl.ds((plan.own - DEEP) * k, plan.part)
    outer = pl.ds((plan.planes - DEEP) * k, DEEP)
    if plan.paired:
        tile_rows = [pl.multiple_of((plan.cols - 8) * (1 - lax.axis_index("gx")), 8)]
    else:
        tile_rows = [plan.cols - 8, 0]
    early, late, last = [], [], []
    early.append(copies.start(slab_in, slab))
    early.append(copies.start(table_in, table))
    for n, row in enumerate(tile_rows):
        for c in range(6):
            side = pl.ds(row, 8)
            early.append(copies.start(raw[c].at[0, mine, side, :], edge.at[n, c]))
            early.append(copies.start(other[c].at[0, mine, side, :], edge.at[n, 6 + c]))
        early.append(copies.start(medium.at[mine, pl.ds(row, 8), :], edge_code.at[n]))
    for c in range(6):
        late.append(copies.start(raw[c].at[0, outer], face.at[pl.ds(DEEP * c, DEEP)]))
        late.append(copies.start(other[c].at[0, outer], face.at[pl.ds(DEEP * (6 + c), DEEP)]))
    late.append(copies.start(medium.at[outer], face_code))
    wait(early)
    rows = plan.part // 2

    def fill(slot, low):
        def one(q, _):
            for h in range(2):
                four = slice(4 * h, 4 * h + 4)
                for c in range(12):
                    strips[slot, c * rows + q, four, :] = edge[slot, c, 2 * q + h, low : low + 4, :]
                code = edge_code[slot, 2 * q + h, low : low + 4, :]
                strips[slot, 12 * rows + q, four, :] = code.astype(F32)
            return 0

        lax.fori_loop(0, rows, one, 0)

    each_side(plan, lambda slot, side: fill(slot, 4 if plan.paired == (side == "high") else 0))
    page, half = slab[...], DEEP // 2
    for n in range(nside):
        strips[n, 13 * rows] = page
        last.append(copies.start(strips.at[n], outs[2 + 2 * n]))
        corners[n, 13 * half] = page
        for c in range(13):
            for h in range(half):
                corners[n, half * c + h] = strips[n, rows * c + (rows - half) * k + h]
        last.append(copies.start(corners.at[n], outs[3 + 2 * n]))
    own, partner = jnp.where(k == 0, table[0:1], table[1:2]), jnp.where(k == 0, table[1:2], table[0:1])
    for s, row in enumerate((own, partner)):
        kerr, two, free = row[:, 0:1], row[:, 1:2], row[:, 2:3]
        for n, value in enumerate((kerr, two, 0.5 * two, 0.5 * free)):
            coef[4 * s + n] = jnp.broadcast_to(value, (8, plan.lanes))
    last.append(copies.start(coef, outs[-1]))
    wait(late)
    face[12 * DEEP : 13 * DEEP] = face_code[...].astype(F32)
    face[13 * DEEP, 0:8, :] = page
    for r in range(8, plan.cols, 8):
        face[13 * DEEP, r : r + 8, :] = page
    send_face(plan, copies, last, face, outs[:2])
    wait(last)


def face_split(plan, pages):
    if pages == 12 * DEEP:
        return ((0, pages),)
    first = (pages + 1) // 2
    return ((0, first), (first, pages - first))


def send_face(plan, copies, started, face, outs):
    for out, (start, count) in zip(outs, face_split(plan, face.shape[0])):
        started.append(copies.start(face.at[pl.ds(start, count)], out))


def get_face(plan, copies, parts, pages, first, targets):
    started = []
    for part, (start, count) in zip(parts, face_split(plan, pages)):
        low, high = max(first, start), min(first + DEEP, start + count)
        if low < high:
            source = part.at[pl.ds(low - start, high - low)]
            started.append(copies.start(source, targets(low - first, high - low)))
    return started


def strip_tiles(plan, comps):
    if comps == 12:
        return comps * plan.own // 2
    return comps * plan.part // 2 + 1


def send_strips(plan, copies, started, strips, corners, outs, comps):
    k = lax.axis_index("af")
    half, top = DEEP // 2, (plan.own - DEEP) // 2
    for n in range(len(plan.sides)):
        started.append(copies.start(strips.at[n], outs[3 * n]))
        for e, begin in enumerate((top * (1 - k), top * k)):
            for c in range(comps):
                for h in range(half):
                    corners[n, e, half * c + h] = strips[n, plan.own // 2 * c + begin + h]
            started.append(copies.start(corners.at[n, e], outs[3 * n + 1 + e]))


def corner_tiles(plan, comps):
    return comps * DEEP // 2 + (comps > 12)


def strip_shapes(plan, comps):
    tiles = corner_tiles(plan, comps)
    one = [strip_tiles(plan, comps)] + [tiles] * (1 if comps > 12 else 2)
    return [(count, 8, plan.lanes) for count in one * len(plan.sides)]


def face_shapes(plan, pages):
    return [(count, plan.cols, plan.lanes) for _, count in face_split(plan, pages)]


def pack(plan, raw, other, medium, slab, table):
    wide = (plan.cols, plan.lanes)
    nside = len(plan.sides)
    pages = 13 * DEEP + 1
    scratch = [
        pltpu.VMEM((nside, 12, plan.part, 8, plan.lanes), F32),
        pltpu.VMEM((nside, plan.part, 8, plan.lanes), jnp.int32),
        pltpu.VMEM((pages,) + wide, F32),
        pltpu.VMEM((DEEP,) + wide, jnp.int32),
        pltpu.VMEM((nside, strip_tiles(plan, 13), 8, plan.lanes), F32),
        pltpu.VMEM((nside, corner_tiles(plan, 13), 8, plan.lanes), F32),
        pltpu.VMEM((8, plan.lanes), F32),
        pltpu.VMEM(table.shape, F32),
        pltpu.VMEM((8, 8, plan.lanes), F32),
    ]
    return call(
        plan,
        pack_kernel,
        "pack",
        face_shapes(plan, pages) + strip_shapes(plan, 13) + [(8, 8, plan.lanes)],
        [HBM] * 6 + [ANY] * 6 + [HBM, ANY, HBM],
        scratch,
        16 * nside + 18,
        moved=4_000_000,
    )(*raw, *other, medium, slab, table)


def clear(plan, old, new, code):
    zero = jnp.zeros((8, plan.lanes), F32)

    def halo(slot, side):
        tile = plan.tiles - 1 if side == "high" else 0

        def one(p, _):
            for ref in list(old) + code:
                ref[p, 8 * tile : 8 * tile + 8, :] = zero
            return 0

        lax.fori_loop(0, plan.ext, one, 0)

    each_side(plan, halo)

    def above(p, _):
        for c in (1, 2, 7, 8):
            for ref in (old[c], new[c]):
                ref[p, plan.width : plan.width + 8, :] = zero
        return 0

    lax.fori_loop(0, plan.ext, above, 0)
    for c, ref in enumerate(new):
        plane = DEEP + plan.own if c % 6 < 3 else DEEP - 1
        for t in range(plan.tiles):
            ref[plane, 8 * t : 8 * t + 8, :] = zero


def strip_row(plan, side):
    if side == "low":
        return 4
    return plan.cols if plan.paired else 8 + plan.cols


def spread_strip(refs, strip, each, begin, at, plane, pairs):
    def one(q, _):
        for c, ref in refs:
            for h in range(2):
                tile = c * each + begin + q
                ref[plane + 2 * q + h, at : at + 4, :] = strip[tile, 4 * h : 4 * h + 4, :]
        return 0

    lax.fori_loop(0, pairs, one, 0)


def substeps(plan, first, second, base, silicon, charge, gen, coef):
    lanes = plan.lanes
    tile = (8, lanes)
    lane = lax.broadcasted_iota(jnp.int32, tile, 1)
    row = lax.broadcasted_iota(jnp.int32, tile, 0)
    keep_up, keep_down, at_top = lane < lanes - 1, lane > 0, row == 0
    z, x, k = (lax.axis_index(a) for a in LINE)
    at_low = jnp.logical_and(z == 0, k == 0)
    at_high = jnp.logical_and(z == plan.gz - 1, k == 1)

    def up(v):
        return jnp.where(keep_up, pltpu.roll(v, lanes - 1, 1), 0.0)

    def down(v):
        return jnp.where(keep_down, pltpu.roll(v, 1, 1), 0.0)

    def edge_mask(t):
        if plan.paired or t not in (0, plan.tiles - 1):
            return None
        off = (x == 0) if t == 0 else (x == plan.gx - 1)
        return jnp.where(off, 0.0, 1.0)

    def magnetic(old, new, s, p, t):
        ex, ey, ez, hx, hy, hz = old[6 * s : 6 * s + 6]
        here, beside = slice(8 * t, 8 * t + 8), slice(8 * t + 1, 8 * t + 9)
        vx, vy, vz = ex[p, here, :], ey[p, here, :], ez[p, here, :]
        nx = hx[p, here, :] - COURANT * ((up(vz) - vz) - (ey[p + 1, here, :] - vy))
        ny = hy[p, here, :] - COURANT * ((ex[p + 1, here, :] - vx) - (ez[p, beside, :] - vz))
        nz = hz[p, here, :] - COURANT * ((ey[p, beside, :] - vy) - (up(vx) - vx))
        mask = edge_mask(t)
        if mask is not None:
            nx, ny, nz = nx * mask, ny * mask, nz * mask
        new[6 * s + 3][p, here, :] = nx
        new[6 * s + 4][p, here, :] = ny
        new[6 * s + 5][p, here, :] = nz

    def electric(old, new, p, t):
        coarse = p // BLOCK_FACTOR
        here = slice(8 * t, 8 * t + 8)
        volts = [[old[6 * s + c][p, here, :] for c in range(3)] for s in range(2)]
        strength = [v[0] * v[0] + v[1] * v[1] + v[2] * v[2] for v in volts]
        is_silicon = silicon[p, here, :]
        total = (strength[0] + strength[1]) * is_silicon
        carriers = charge[coarse, here, :] * is_silicon
        ground = base[p, here, :]
        gen[p, here, :] += (coef[1] * strength[0] + coef[5] * strength[1]) * total
        mask = edge_mask(t)
        for s in range(2):
            vx, vy, vz = volts[s]
            hx, hy, hz = new[6 * s + 3 : 6 * s + 6]
            nx, ny, nz = hx[p, here, :], hy[p, here, :], hz[p, here, :]
            if t == 0:
                left_y = jnp.where(at_top, 0.0, pltpu.roll(ny, 1, 0))
                left_z = jnp.where(at_top, 0.0, pltpu.roll(nz, 1, 0))
            else:
                before = slice(8 * t - 1, 8 * t + 7)
                left_y, left_z = hy[p, before, :], hz[p, before, :]
            loss = coef[4 * s + 2] * total + coef[4 * s + 3] * carriers
            perm = ground + coef[4 * s] * total
            inv = pl.reciprocal(perm + loss, approx=True)
            keep = (perm - loss) * inv
            push = COURANT * inv
            if mask is not None:
                push = push * mask
            curl_x = (nz - down(nz)) - (ny - hy[p - 1, here, :])
            curl_y = (nx - hx[p - 1, here, :]) - (nz - left_z)
            curl_z = (ny - left_y) - (nx - down(nx))
            new[6 * s][p, here, :] = keep * vx + push * curl_x
            new[6 * s + 1][p, here, :] = keep * vy + push * curl_y
            new[6 * s + 2][p, here, :] = keep * vz + push * curl_z

    def magnetic_plane(old, new, p):
        for t in range(plan.tiles):
            for s in range(2):
                magnetic(old, new, s, p, t)

    def substep(old, new, n):
        begin = jnp.where(at_low, DEEP, n + 1)
        end = jnp.where(at_high, DEEP + plan.own, plan.ext - 1 - n)
        rest = lax.rem(end - begin, 4)

        @pl.when(jnp.logical_not(at_low))
        def _():
            magnetic_plane(old, new, n)
            magnetic_plane(old, new, n + 1)

        @pl.when(at_low)
        def _():
            magnetic_plane(old, new, DEEP)

        def advance(p):
            for t in range(plan.tiles):
                electric(old, new, p, t)
                for s in range(2):
                    magnetic(old, new, s, p + 1, t)

        def one(m, _):
            advance(begin + m)
            return 0

        def four(m, _):
            for h in range(4):
                advance(begin + rest + 4 * m + h)
            return 0

        lax.fori_loop(0, rest, one, 0)
        lax.fori_loop(0, (end - begin) // 4, four, 0)

    def pair(m, _):
        substep(first, second, 2 * m)
        substep(second, first, 2 * m + 1)
        return 0

    lax.fori_loop(0, SUBSTEPS // 2, pair, 0)


def set_media(plan, code, base, silicon):
    def one(p, _):
        for t in range(plan.tiles):
            here = slice(8 * t, 8 * t + 8)
            v = code[p, here, :]
            base[p, here, :] = jnp.where(v == 0.0, SILICON_PERM, jnp.where(v == 1.0, OXIDE_PERM, 1.0))
            silicon[p, here, :] = jnp.where(v == 0.0, 1.0, 0.0)
        return 0

    lax.fori_loop(0, plan.ext, one, 0)


def clear_generation(plan, gen):
    def one(p, _):
        gen[p] = jnp.zeros((plan.rows, plan.lanes), F32)
        return 0

    lax.fori_loop(DEEP, DEEP + plan.own, one, 0)


def sum_generation(plan, gen, message):
    blocks = plan.cols // BLOCK_FACTOR
    shape = (blocks, plan.lanes)
    column = lax.broadcasted_iota(jnp.int32, shape, 0) + blocks * lax.axis_index("gx")
    upright = lax.broadcasted_iota(jnp.int32, shape, 1) == column
    across = plan.own_rows()
    for a in range(plan.own // BLOCK_FACTOR):
        p = DEEP + BLOCK_FACTOR * a
        rows = (gen[p, across, :] + gen[p + 1, across, :]) + (
            gen[p + 2, across, :] + gen[p + 3, across, :]
        )
        cells = rows.reshape(blocks, BLOCK_FACTOR, plan.lanes).sum(1)
        mean = cells.sum(1, keepdims=True) * (1.0 / (BLOCK_FACTOR * BLOCK_FACTOR * plan.lanes))
        message[a : a + 1, :] = jnp.where(upright, mean, 0.0).sum(0, keepdims=True)


def round_scratch(plan):
    wide = (plan.ext, plan.rows, plan.lanes)
    return [pltpu.VMEM((plan.ext + 1, plan.rows, plan.lanes), F32)] * 24 + [
        pltpu.VMEM(wide, F32)
    ] * 3 + [
        pltpu.VMEM((plan.ext // BLOCK_FACTOR, plan.width, plan.lanes), F32),
        pltpu.VMEM((8, plan.lanes), F32),
        pltpu.VMEM((8, 8, plan.lanes), F32),
        pltpu.VMEM(wide, F32),
    ]


def round_flops(plan):
    return SUBSTEPS * plan.ext * plan.width * plan.lanes * 150


def generation_shape(plan):
    return (plan.devices, 8, plan.lanes)


def place_strips(plan, old, code, strips):
    k = lax.axis_index("af")
    outward, inner = plan.part * k, plan.part * (1 - k)

    def place(slot, side):
        at = strip_row(plan, side)
        same = list(enumerate(list(old) + code))
        flipped = list(enumerate(list(old[6:]) + list(old[:6]) + code))
        half, rows = DEEP // 2, plan.own // 2
        if code:
            whole, corner = strips[2 * slot : 2 * slot + 2]
            near, rows = DEEP * (1 - k), plan.part // 2
            spread_strip(same, whole, rows, 0, at, near, rows)
            spread_strip(flipped, corner, half, 0, at, outward, half)
            return
        whole, beside, corner = strips[3 * slot : 3 * slot + 3]
        spread_strip(same, whole, rows, 0, at, DEEP, rows)
        spread_strip(flipped, beside, half, 0, at, inner, half)
        spread_strip(flipped, corner, half, 0, at, outward, half)

    each_side(plan, place)


def send_generation(plan, copies, started, gen, message, gen_out):
    sum_generation(plan, gen, message)
    for d in range(plan.devices):
        started.append(copies.start(message, gen_out.at[d]))


def charge_from_slabs(plan, charge, mine, across, chip, corner):
    across, chip = chip, across
    x, k = lax.axis_index("gx"), lax.axis_index("af")
    slab = plan.slab
    left = jnp.where(x == 0, mine, across)
    right = jnp.where(x == 0, across, mine)
    beyond = jnp.where(x != k, chip, corner)
    body = jnp.where(k == 0, left, right)
    before = jnp.where(k == 0, beyond, left)[slab - 1 : slab]
    after = jnp.where(k == 0, right, beyond)[0:1]
    for a in range(slab + 2):
        row = before if a == 0 else after if a == slab + 1 else body[a - 1 : a]
        spread_row(plan, row, charge, a)


def spread_row(plan, row, charge, a):
    left = (plan.cols * lax.axis_index("gx") - plan.first_row()) // BLOCK_FACTOR
    row = jnp.broadcast_to(row, (8, plan.lanes))
    row = pltpu.roll(row, lax.rem(plan.lanes - left, plan.lanes), 1)
    for c in range(plan.width // BLOCK_FACTOR):
        charge[a, 4 * c : 4 * c + 4, :] = jnp.broadcast_to(row[0:4, c : c + 1], (4, plan.lanes))


def first_kernel(plan, *refs):
    nside = len(plan.sides)
    strips_in, refs = refs[: 2 * nside], refs[2 * nside :]
    z_in, raw, other = refs[:2], refs[2:8], refs[8:14]
    medium, slab_in, under_in, coef_in = refs[14:18]
    own_out, core_out, gen_out, code_out = refs[18:22]
    z_out, strip_out = refs[22], refs[23 : 23 + 3 * nside]
    rest = refs[23 + 3 * nside :]
    old, new, (base, silicon, gen, charge, message, coef, code) = rest[:12], rest[12:24], rest[24:31]
    codes, strips, (strip_mine, corners, slabs, sems) = rest[31], rest[32 : 32 + 2 * nside], rest[-4:]
    copies = Copies(sems)
    k = lax.axis_index("af")
    near = DEEP * (1 - k)
    far = plan.part * k
    across = plan.own_rows()
    here = pl.ds(near, plan.part)
    mine = pl.ds((plan.own - DEEP) * k, plan.part)
    early = [copies.start(medium.at[mine], codes)]
    pages = 13 * DEEP + 1
    early += get_face(
        plan, copies, z_in, pages, 12 * DEEP, lambda p, n: code.at[pl.ds(far + p, n), across]
    )
    early.append(copies.start(slab_in, slabs.at[0]))
    if plan.paired:
        early.append(copies.start(z_in[1].at[z_in[1].shape[0] - 1, pl.ds(0, 8)], slabs.at[1]))
    else:
        early.append(copies.start(under_in, charge))
    early.append(copies.start(coef_in, coef))
    for source, target in zip(strips_in, strips):
        early.append(copies.start(source, target))
    late = []
    for c in range(6):
        late.append(copies.start(raw[c].at[0, mine], old[c].at[here, across]))
        late.append(copies.start(other[c].at[0, mine], old[6 + c].at[here, across]))
    for c in range(12):
        late += get_face(
            plan,
            copies,
            z_in,
            pages,
            DEEP * ((c + 6) % 12),
            lambda p, n, ref=old[c]: ref.at[pl.ds(far + p, n), across],
        )
    clear(plan, old, new, [code])
    clear_generation(plan, gen)
    wait(early)

    def settle(p, _):
        code[near + p, across, :] = codes[p].astype(F32)
        return 0

    lax.fori_loop(0, plan.part, settle, 0)
    place_strips(plan, old, [code], strips)
    set_media(plan, code, base, silicon)
    if plan.paired:
        charge_from_slabs(
            plan, charge, slabs[0], slabs[1], strips[0][13 * plan.part // 2], strips[1][13 * DEEP // 2]
        )
    wait(late)
    substeps(plan, old, new, base, silicon, charge, gen, coef)
    copies = Copies(sems)
    late = []

    def gather(slot, side):
        high_end = (side == "high") if plan.paired else (side == "low")
        low = 0 if plan.paired and side == "high" else 8
        at = low + plan.cols - 4 if high_end else low

        def one(q, _):
            for c in range(12):
                for h in range(2):
                    tile = plan.own // 2 * c + q
                    strip_mine[slot, tile, 4 * h : 4 * h + 4, :] = old[c][
                        DEEP + 2 * q + h, at : at + 4, :
                    ]
            return 0

        lax.fori_loop(0, plan.own // 2, one, 0)

    toward = DEEP + (plan.own - DEEP) * k
    inward = DEEP + (plan.own - DEEP) * (1 - k)
    for c in range(12):
        source = old[c].at[pl.ds(toward, DEEP), across]
        late.append(copies.start(source, z_out.at[pl.ds(DEEP * c, DEEP)]))
        late.append(copies.start(old[c].at[pl.ds(inward, DEEP), across], core_out.at[c]))
        late.append(copies.start(old[c].at[pl.ds(DEEP, plan.own), across], own_out.at[c]))
    late.append(copies.start(code, code_out))
    message[4:8, :] = slabs[0, 0:4, :]
    each_side(plan, gather)
    send_strips(plan, copies, late, strip_mine, corners, strip_out, 12)
    send_generation(plan, copies, late, gen, message, gen_out)
    wait(late)


def first_round(plan, strips, z_in, raw, other, medium, slab, under, coef):
    wide = (plan.cols, plan.lanes)
    nside = len(plan.sides)
    shapes = [
        (12, plan.own) + wide,
        (12, DEEP) + wide,
        generation_shape(plan),
        (plan.ext, plan.rows, plan.lanes),
    ]
    shapes += face_shapes(plan, 12 * DEEP) + strip_shapes(plan, 12)
    scratch = round_scratch(plan) + [pltpu.VMEM((plan.part,) + wide, jnp.int32)]
    scratch += [pltpu.VMEM(s.shape, F32) for s in strips]
    scratch += [
        pltpu.VMEM((nside, strip_tiles(plan, 12), 8, plan.lanes), F32),
        pltpu.VMEM((nside, 2, corner_tiles(plan, 12), 8, plan.lanes), F32),
        pltpu.VMEM((2, 8, plan.lanes), F32),
    ]
    return call(
        plan,
        first_kernel,
        "first_round",
        shapes,
        [ANY] * (2 + 2 * nside) + [HBM] * 6 + [ANY] * 6 + [HBM, ANY, ANY, HBM],
        scratch,
        42 + 3 * nside + plan.devices,
        round_flops(plan),
        10_000_000,
    )(*strips, *z_in, *raw, *other, medium, slab, under, coef)


def second_kernel(plan, *refs):
    nside = len(plan.sides)
    strips_in, refs = refs[: 3 * nside], refs[3 * nside :]
    z_in, (core_in, own_in, code_in, charge_in, coef_in) = refs[:1], refs[1:6]
    kept, sent, gen_out, rest = refs[6:12], refs[12], refs[13], refs[14:]
    old, new, (base, silicon, gen, charge, message, coef, code) = rest[:12], rest[12:24], rest[24:31]
    strips, sems = rest[31:-1], rest[-1]
    copies = Copies(sems)
    k = lax.axis_index("af")
    across = plan.own_rows()
    outward = plan.part * k
    inner = plan.part * (1 - k)
    early = [copies.start(code_in, code), copies.start(charge_in, charge)]
    early.append(copies.start(coef_in, coef))
    for source, target in zip(strips_in, strips):
        early.append(copies.start(source, target))
    late = []
    for c in range(12):
        flip = (c + 6) % 12
        late.append(copies.start(own_in.at[c], old[c].at[pl.ds(DEEP, plan.own), across]))
        late += get_face(
            plan,
            copies,
            z_in,
            12 * DEEP,
            DEEP * flip,
            lambda p, n, ref=old[c]: ref.at[pl.ds(outward + p, n), across],
        )
        late.append(copies.start(core_in.at[flip], old[c].at[pl.ds(inner, DEEP), across]))
    clear(plan, old, new, [])
    clear_generation(plan, gen)
    wait(early)
    place_strips(plan, old, [], strips)
    set_media(plan, code, base, silicon)
    wait(late)
    substeps(plan, old, new, base, silicon, charge, gen, coef)
    copies = Copies(sems)
    late = []
    for c in range(6):
        late.append(copies.start(old[6 + c].at[pl.ds(DEEP, plan.own), across], sent.at[c]))
    for c in range(6):
        target = kept[c].at[0, pl.ds(plan.own * k, plan.own)]
        late.append(copies.start(old[c].at[pl.ds(DEEP, plan.own), across], target))
    message[...] = jnp.zeros(message.shape, F32)
    send_generation(plan, copies, late, gen, message, gen_out)
    wait(late)


def second_round(plan, strips, z_in, core_in, own_in, code, charge, coef):
    wide = (plan.cols, plan.lanes)
    nside = len(plan.sides)
    shapes = [(1, plan.planes) + wide] * 6 + [(6, plan.own) + wide, generation_shape(plan)]
    scratch = round_scratch(plan) + [pltpu.VMEM(s.shape, F32) for s in strips]
    return call(
        plan,
        second_kernel,
        "second_round",
        shapes,
        [ANY] * (2 + 3 * nside) + [HBM] * 4,
        scratch,
        39 + 3 * nside + plan.devices,
        round_flops(plan),
        10_000_000,
    )(*strips, *z_in, core_in, own_in, code, charge, coef)


def join_kernel(plan, *refs):
    got, outs, (half, sems) = refs[6], refs[7:13], refs[13:]
    copies = Copies(sems)
    rows = pl.ds(plan.own * (1 - lax.axis_index("af")), plan.own)
    early = [copies.start(got.at[c], half.at[c]) for c in range(6)]
    late = []
    for c in range(6):
        early[c].wait()
        late.append(copies.start(half.at[c], outs[c].at[0, rows]))
    wait(late)


def join(plan, halves, got):
    shapes = [h.shape for h in halves]
    aliases = {c: c for c in range(6)}
    scratch = [pltpu.VMEM(got.shape, F32)]
    return call(
        plan, join_kernel, "join", shapes, [HBM] * 6 + [ANY], scratch, 12, moved=3_000_000, aliases=aliases
    )(*halves, got)


def charge_shape(plan):
    return (plan.ext // BLOCK_FACTOR, plan.width, plan.lanes)


def spread_whole(plan, density):
    z, x, k = (lax.axis_index(a) for a in LINE)
    side = plan.width // BLOCK_FACTOR
    padded = jnp.pad(density, ((1, 1), (side, side)))
    top = (plan.planes * z + plan.own * k) // BLOCK_FACTOR
    left = side + (plan.cols * x - plan.first_row()) // BLOCK_FACTOR
    tile = lax.dynamic_slice(padded, (top, left), (plan.ext // BLOCK_FACTOR, side))
    return jnp.broadcast_to(jnp.repeat(tile, BLOCK_FACTOR, 1)[:, :, None], charge_shape(plan))


def carrier_kernel(plan, last, *refs):
    gens_in, refs = refs[0], refs[1:]
    if last:
        density_in, refs = refs[0], refs[1:]
    outs = refs[:1] if last else refs[:2]
    gens, one, two, source, charge, slab_out, sems = refs[len(outs) :]
    copies = Copies(sems)
    rows, cols, lanes = plan.grid_rows, plan.grid_cols, plan.lanes
    z, x, k = (lax.axis_index(a) for a in LINE)
    own = plan.own // BLOCK_FACTOR
    early = [copies.start(gens_in, gens)]
    if last:
        early.append(copies.start(density_in, one))
    zero = jnp.zeros((8, lanes), F32)
    for ref in (two,) if last else (one, two):
        ref[0:8, :] = zero
        ref[8 + rows : 16 + rows, :] = zero
    wait(early)

    def unpack(line, _):
        top = pl.multiple_of(8 * line, 8)
        for dk in range(2):
            tiles = [gens[(line * plan.gx + dx) * 2 + dk, 0:own, :] for dx in range(plan.gx)]
            source[pl.ds(top + own * dk, own), :] = SOURCE_FACTOR * functools.reduce(jnp.add, tiles)
        if not last:
            for dx in range(plan.gx):
                slab = gens[(line * plan.gx + dx) * 2, 4 : 4 + plan.slab, :]
                one[pl.ds(8 + top + plan.slab * dx, plan.slab), :] = slab
        return 0

    lax.fori_loop(0, plan.gz, unpack, 0, unroll=plan.gz <= 4)
    inside = lax.broadcasted_iota(jnp.int32, (8, lanes), 1) < cols
    for step in range(CSTEPS):
        old, new = (one, two) if step % 2 == 0 else (two, one)
        for r in range(8, 8 + rows, 8):
            now, before = old[r : r + 8, :], old[r - 1 : r + 7, :]
            around = (
                old[r + 1 : r + 9, :]
                + before
                + pltpu.roll(now, lanes - 1, 1)
                + pltpu.roll(now, 1, 1)
                - 4.0 * now
            )
            later = (
                now
                + SPREAD_COEFF * around
                - MOBILITY_TERM * (now - before)
                - LIFETIME_DECAY * now
                + source[r - 8 : r, :]
            )
            new[r : r + 8, :] = jnp.where(inside, later, 0.0)
    if last:
        mine = one[pl.ds(8 + (z * plan.gx + x) * plan.slab, plan.slab), :]
        slab_out[...] = mine[:, :cols]
        copies.start(slab_out, outs[0]).wait()
        return
    late = [copies.start(one, outs[0])]
    for a in range(plan.ext // BLOCK_FACTOR):
        top = (plan.planes * z + plan.own * k - DEEP) // BLOCK_FACTOR + a
        spread_row(plan, one[pl.ds(8 + jnp.clip(top, 0, rows - 1), 1), :], charge, a)
    late.append(copies.start(charge, outs[1]))
    wait(late)


def carriers(plan, last, *arrays):
    grid, slab = (plan.grid_rows + 16, plan.lanes), (plan.slab, plan.grid_cols)
    scratch = [
        pltpu.VMEM(arrays[0].shape, F32),
        pltpu.VMEM(grid, F32),
        pltpu.VMEM(grid, F32),
        pltpu.VMEM((plan.grid_rows, plan.lanes), F32),
        pltpu.VMEM(charge_shape(plan), F32),
        pltpu.VMEM(slab, F32),
    ]
    return call(
        plan,
        lambda plan, *refs: carrier_kernel(plan, last, *refs),
        "carriers",
        [slab] if last else [grid, charge_shape(plan)],
        [ANY] + [HBM] * (len(arrays) - 1),
        scratch,
        4,
        2_000_000,
        1_000_000,
    )(*arrays)


def local(ex, ey, ez, hx, hy, hz, medium, table, density):
    raw = (ex, ey, ez, hx, hy, hz)
    plan = Plan(*medium.shape, density.shape[0])

    def send(message, target):
        return lax.ppermute(message, LINE, line_pairs(plan, target))

    def everywhere(message, axes):
        return lax.all_to_all(message, axes, split_axis=0, concat_axis=0, tiled=True)

    core = lambda z, x, k: (z, x, 1 - k)
    beyond = lambda z, k: z - 1 if k == 0 else z + 1

    def exchange(face, strips):
        got, each = [], len(strips) // len(plan.sides)
        for n, side in enumerate(plan.sides):
            to = functools.partial(across_step, side)
            mine = strips[each * n : each * n + each]
            got.append(send(mine[0], lambda z, x, k: (z, to(x), k)))
            if each == 3:
                got.append(send(mine[1], lambda z, x, k: (z, to(x), 1 - k)))
            got.append(send(mine[-1], lambda z, x, k: (beyond(z, k), to(x), 1 - k)))
        return [send(part, lambda z, x, k: (beyond(z, k), x, 1 - k)) for part in face], got

    other = [send(r, core) for r in raw]
    slab = jnp.pad(density, ((0, 8 - plan.slab), (0, plan.lanes - plan.grid_cols)))
    packed = pack(plan, raw, other, medium, slab, table)
    z_in, strips = exchange(packed[:2], packed[2:-1])
    coef = packed[-1]
    under = slab
    if not plan.paired:
        tiles = plan.gz * plan.gx
        slabs = everywhere(jnp.broadcast_to(density, (tiles,) + density.shape), ("gz", "gx"))
        under = spread_whole(plan, slabs.reshape(plan.grid_rows, plan.grid_cols))
    outs = first_round(plan, strips, z_in, raw, other, medium, slab, under, coef)
    own, core_msg, gens, code = outs[:4]
    gens = everywhere(gens, LINE)
    z_in, strips = exchange(outs[4:5], outs[5:])
    core_in = send(core_msg, core)
    grid, charge = carriers(plan, False, gens)
    outs = second_round(plan, strips, z_in, core_in, own, code, charge, coef)
    halves, sent, gens = outs[:6], outs[6], outs[7]
    gens = everywhere(gens, LINE)
    got = send(sent, core)
    (new_slab,) = carriers(plan, True, gens, grid)
    return tuple(join(plan, halves, got)) + (new_slab,)


def solution(mesh):
    field = P("af", ("group", "gz"), "gx", None)
    slabs = P(("group", "gz", "gx"), None)
    in_specs = (field,) * 6 + (P(("group", "gz"), "gx", None), P(), slabs)
    out_specs = (field,) * 6 + (slabs,)
    return jax.shard_map(local, mesh=mesh, in_specs=in_specs, out_specs=out_specs, check_vma=False)
```

```python
import functools

import jax
import jax.numpy as jnp
from jax import lax
from jax.experimental import pallas as pl
from jax.experimental.pallas import tpu as pltpu
from jax.sharding import PartitionSpec as P

BLOCK_FACTOR = 4
SUBSTEPS = 4
ROUNDS = 2
CSTEPS = 8

COURANT = 0.5
SILICON_PERM = 12.1
OXIDE_PERM = 2.1
SPREAD_COEFF = 0.2
MOBILITY_TERM = 0.1
LIFETIME_DECAY = 0.05
SOURCE_FACTOR = 0.02

DEEP = SUBSTEPS
LINE = ("gz", "gx", "af")
HBM = pl.BlockSpec(memory_space=pltpu.HBM)
ANY = pl.BlockSpec(memory_space=pl.ANY)
SMEM = pl.BlockSpec(memory_space=pltpu.SMEM)
VMEM_LIMIT = 24 * 1024 * 1024
F32 = jnp.float32


class Plan:
    def __init__(self, planes, cols, lanes, slab):
        self.gz = lax.axis_size("gz")
        self.gx = lax.axis_size("gx")
        self.planes, self.cols, self.lanes, self.slab = planes, cols, lanes, slab
        self.own = planes // 2
        self.part = self.own + DEEP
        self.ext = self.own + 2 * DEEP
        self.paired = self.gx == 2
        self.sides = ("face",) if self.paired else ("low", "high")
        self.width = cols + (8 if self.paired else 16)
        self.rows = self.width + 8
        self.tiles = self.width // 8
        self.grid_rows = planes * self.gz // BLOCK_FACTOR
        self.grid_cols = cols * self.gx // BLOCK_FACTOR
        self.devices = self.gz * self.gx * 2

    def first_row(self):
        return 8 * lax.axis_index("gx") if self.paired else 8

    def own_rows(self):
        return pl.ds(pl.multiple_of(self.first_row(), 8), self.cols)


def each_side(plan, act):
    if plan.paired:
        across = lax.axis_index("gx")

        @pl.when(across == 0)
        def _():
            act(0, "high")

        @pl.when(across == 1)
        def _():
            act(0, "low")
    else:
        act(0, "low")
        act(1, "high")


def line_pairs(plan, target):
    pairs = []
    for z in range(plan.gz):
        for x in range(plan.gx):
            for k in range(2):
                tz, tx, tk = target(z, x, k)
                if 0 <= tz < plan.gz and 0 <= tx < plan.gx:
                    pairs.append(((z * plan.gx + x) * 2 + k, (tz * plan.gx + tx) * 2 + tk))
    return pairs


def across_step(side, x):
    if side == "face":
        return 1 - x
    return x + 1 if side == "low" else x - 1


class Copies:
    def __init__(self, sems):
        self.sems, self.made = sems, 0

    def start(self, source, target):
        copy = pltpu.make_async_copy(source, target, self.sems.at[self.made])
        self.made += 1
        copy.start()
        return copy


def wait(copies):
    for copy in copies:
        copy.wait()


def call(plan, body, name, shapes, in_specs, scratch, copies, flops=0, moved=0, aliases=None):
    kernel = pl.pallas_call(
        functools.partial(body, plan),
        out_shape=[pltpu.HBM(s, F32) for s in shapes],
        in_specs=in_specs,
        out_specs=[HBM] * len(shapes),
        scratch_shapes=scratch + [pltpu.SemaphoreType.DMA((copies,))],
        input_output_aliases=aliases or {},
        compiler_params=pltpu.CompilerParams(vmem_limit_bytes=VMEM_LIMIT),
        cost_estimate=pl.CostEstimate(flops=flops, bytes_accessed=moved, transcendentals=0),
        name=name,
    )

    def run(*args):
        placed = []
        for arg, spec in zip(args, in_specs):
            in_hbm = spec.memory_space is pltpu.HBM
            placed.append(pltpu.with_memory_space_constraint(arg, pltpu.HBM) if in_hbm else arg)
        return kernel(*placed)

    return run


def pack_kernel(plan, *refs):
    raw, other, medium, nside = refs[:6], refs[6:12], refs[12], len(plan.sides)
    slab_in, table_in = refs[13:15]
    outs = refs[15 : 18 + 2 * nside]
    edge, edge_code, face, face_code, strips, corners, slab, table, coef, sems = refs[18 + 2 * nside :]
    copies = Copies(sems)
    k = lax.axis_index("af")
    mine = pl.ds((plan.own - DEEP) * k, plan.part)
    outer = pl.ds((plan.planes - DEEP) * k, DEEP)
    if plan.paired:
        tile_rows = [pl.multiple_of((plan.cols - 8) * (1 - lax.axis_index("gx")), 8)]
    else:
        tile_rows = [plan.cols - 8, 0]
    early, late, last = [], [], []
    early.append(copies.start(slab_in, slab))
    early.append(copies.start(table_in, table))
    for n, row in enumerate(tile_rows):
        for c in range(6):
            side = pl.ds(row, 8)
            early.append(copies.start(raw[c].at[0, mine, side, :], edge.at[n, c]))
            early.append(copies.start(other[c].at[0, mine, side, :], edge.at[n, 6 + c]))
        early.append(copies.start(medium.at[mine, pl.ds(row, 8), :], edge_code.at[n]))
    for c in range(6):
        late.append(copies.start(raw[c].at[0, outer], face.at[pl.ds(DEEP * c, DEEP)]))
        late.append(copies.start(other[c].at[0, outer], face.at[pl.ds(DEEP * (6 + c), DEEP)]))
    late.append(copies.start(medium.at[outer], face_code))
    wait(early)
    rows = plan.part // 2

    def fill(slot, low):
        def one(q, _):
            for h in range(2):
                four = slice(4 * h, 4 * h + 4)
                for c in range(12):
                    strips[slot, c * rows + q, four, :] = edge[slot, c, 2 * q + h, low : low + 4, :]
                code = edge_code[slot, 2 * q + h, low : low + 4, :]
                strips[slot, 12 * rows + q, four, :] = code.astype(F32)
            return 0

        lax.fori_loop(0, rows, one, 0)

    each_side(plan, lambda slot, side: fill(slot, 4 if plan.paired == (side == "high") else 0))
    page, half = slab[...], DEEP // 2
    for n in range(nside):
        strips[n, 13 * rows] = page
        last.append(copies.start(strips.at[n], outs[2 + 2 * n]))
        corners[n, 13 * half] = page
        for c in range(13):
            for h in range(half):
                corners[n, half * c + h] = strips[n, rows * c + (rows - half) * k + h]
        last.append(copies.start(corners.at[n], outs[3 + 2 * n]))
    own, partner = jnp.where(k == 0, table[0:1], table[1:2]), jnp.where(k == 0, table[1:2], table[0:1])
    for s, row in enumerate((own, partner)):
        kerr, two, free = row[:, 0:1], row[:, 1:2], row[:, 2:3]
        for n, value in enumerate((kerr, two, 0.5 * two, 0.5 * free)):
            coef[4 * s + n] = jnp.broadcast_to(value, (8, plan.lanes))
    last.append(copies.start(coef, outs[-1]))
    wait(late)
    face[12 * DEEP : 13 * DEEP] = face_code[...].astype(F32)
    face[13 * DEEP, 0:8, :] = page
    for r in range(8, plan.cols, 8):
        face[13 * DEEP, r : r + 8, :] = page
    send_face(plan, copies, last, face, outs[:2])
    wait(last)


def face_split(plan, pages):
    if pages == 12 * DEEP:
        return ((0, pages),)
    first = (pages + 1) // 2
    return ((0, first), (first, pages - first))


def send_face(plan, copies, started, face, outs):
    for out, (start, count) in zip(outs, face_split(plan, face.shape[0])):
        started.append(copies.start(face.at[pl.ds(start, count)], out))


def get_face(plan, copies, parts, pages, first, targets):
    started = []
    for part, (start, count) in zip(parts, face_split(plan, pages)):
        low, high = max(first, start), min(first + DEEP, start + count)
        if low < high:
            source = part.at[pl.ds(low - start, high - low)]
            started.append(copies.start(source, targets(low - first, high - low)))
    return started


def strip_tiles(plan, comps):
    if comps == 12:
        return comps * plan.own // 2
    return comps * plan.part // 2 + 1


def send_strips(plan, copies, started, strips, corners, outs, comps):
    k = lax.axis_index("af")
    half, top = DEEP // 2, (plan.own - DEEP) // 2
    for n in range(len(plan.sides)):
        started.append(copies.start(strips.at[n], outs[3 * n]))
        for e, begin in enumerate((top * (1 - k), top * k)):
            for c in range(comps):
                for h in range(half):
                    corners[n, e, half * c + h] = strips[n, plan.own // 2 * c + begin + h]
            started.append(copies.start(corners.at[n, e], outs[3 * n + 1 + e]))


def corner_tiles(plan, comps):
    return comps * DEEP // 2 + (comps > 12)


def strip_shapes(plan, comps):
    tiles = corner_tiles(plan, comps)
    one = [strip_tiles(plan, comps)] + [tiles] * (1 if comps > 12 else 2)
    return [(count, 8, plan.lanes) for count in one * len(plan.sides)]


def face_shapes(plan, pages):
    return [(count, plan.cols, plan.lanes) for _, count in face_split(plan, pages)]


def pack(plan, raw, other, medium, slab, table):
    wide = (plan.cols, plan.lanes)
    nside = len(plan.sides)
    pages = 13 * DEEP + 1
    scratch = [
        pltpu.VMEM((nside, 12, plan.part, 8, plan.lanes), F32),
        pltpu.VMEM((nside, plan.part, 8, plan.lanes), jnp.int32),
        pltpu.VMEM((pages,) + wide, F32),
        pltpu.VMEM((DEEP,) + wide, jnp.int32),
        pltpu.VMEM((nside, strip_tiles(plan, 13), 8, plan.lanes), F32),
        pltpu.VMEM((nside, corner_tiles(plan, 13), 8, plan.lanes), F32),
        pltpu.VMEM((8, plan.lanes), F32),
        pltpu.VMEM(table.shape, F32),
        pltpu.VMEM((8, 8, plan.lanes), F32),
    ]
    return call(
        plan,
        pack_kernel,
        "pack",
        face_shapes(plan, pages) + strip_shapes(plan, 13) + [(8, 8, plan.lanes)],
        [HBM] * 6 + [ANY] * 6 + [HBM, ANY, HBM],
        scratch,
        16 * nside + 18,
        moved=4_000_000,
    )(*raw, *other, medium, slab, table)


def clear(plan, old, new, code):
    zero = jnp.zeros((8, plan.lanes), F32)

    def halo(slot, side):
        tile = plan.tiles - 1 if side == "high" else 0

        def one(p, _):
            for ref in list(old) + code:
                ref[p, 8 * tile : 8 * tile + 8, :] = zero
            return 0

        lax.fori_loop(0, plan.ext, one, 0)

    each_side(plan, halo)

    def above(p, _):
        for c in (1, 2, 7, 8):
            for ref in (old[c], new[c]):
                ref[p, plan.width : plan.width + 8, :] = zero
        return 0

    lax.fori_loop(0, plan.ext, above, 0)
    for c, ref in enumerate(new):
        plane = DEEP + plan.own if c % 6 < 3 else DEEP - 1
        for t in range(plan.tiles):
            ref[plane, 8 * t : 8 * t + 8, :] = zero


def strip_row(plan, side):
    if side == "low":
        return 4
    return plan.cols if plan.paired else 8 + plan.cols


def spread_strip(refs, strip, each, begin, at, plane, pairs):
    def one(q, _):
        for c, ref in refs:
            for h in range(2):
                tile = c * each + begin + q
                ref[plane + 2 * q + h, at : at + 4, :] = strip[tile, 4 * h : 4 * h + 4, :]
        return 0

    lax.fori_loop(0, pairs, one, 0)


def substeps(plan, first, second, base, silicon, charge, gen, coef):
    lanes = plan.lanes
    tile = (8, lanes)
    lane = lax.broadcasted_iota(jnp.int32, tile, 1)
    row = lax.broadcasted_iota(jnp.int32, tile, 0)
    keep_up, keep_down, at_top = lane < lanes - 1, lane > 0, row == 0
    z, x, k = (lax.axis_index(a) for a in LINE)
    at_low = jnp.logical_and(z == 0, k == 0)
    at_high = jnp.logical_and(z == plan.gz - 1, k == 1)

    def up(v):
        return jnp.where(keep_up, pltpu.roll(v, lanes - 1, 1), 0.0)

    def down(v):
        return jnp.where(keep_down, pltpu.roll(v, 1, 1), 0.0)

    def edge_mask(t):
        if plan.paired or t not in (0, plan.tiles - 1):
            return None
        off = (x == 0) if t == 0 else (x == plan.gx - 1)
        return jnp.where(off, 0.0, 1.0)

    def magnetic(old, new, s, p, t):
        ex, ey, ez, hx, hy, hz = old[6 * s : 6 * s + 6]
        here, beside = slice(8 * t, 8 * t + 8), slice(8 * t + 1, 8 * t + 9)
        vx, vy, vz = ex[p, here, :], ey[p, here, :], ez[p, here, :]
        nx = hx[p, here, :] - COURANT * ((up(vz) - vz) - (ey[p + 1, here, :] - vy))
        ny = hy[p, here, :] - COURANT * ((ex[p + 1, here, :] - vx) - (ez[p, beside, :] - vz))
        nz = hz[p, here, :] - COURANT * ((ey[p, beside, :] - vy) - (up(vx) - vx))
        mask = edge_mask(t)
        if mask is not None:
            nx, ny, nz = nx * mask, ny * mask, nz * mask
        new[6 * s + 3][p, here, :] = nx
        new[6 * s + 4][p, here, :] = ny
        new[6 * s + 5][p, here, :] = nz

    def electric(old, new, p, t):
        coarse = p // BLOCK_FACTOR
        here = slice(8 * t, 8 * t + 8)
        volts = [[old[6 * s + c][p, here, :] for c in range(3)] for s in range(2)]
        strength = [v[0] * v[0] + v[1] * v[1] + v[2] * v[2] for v in volts]
        is_silicon = silicon[p, here, :]
        total = (strength[0] + strength[1]) * is_silicon
        carriers = charge[coarse, here, :] * is_silicon
        ground = base[p, here, :]
        gen[p, here, :] += (coef[1] * strength[0] + coef[5] * strength[1]) * total
        mask = edge_mask(t)
        for s in range(2):
            vx, vy, vz = volts[s]
            hx, hy, hz = new[6 * s + 3 : 6 * s + 6]
            nx, ny, nz = hx[p, here, :], hy[p, here, :], hz[p, here, :]
            if t == 0:
                left_y = jnp.where(at_top, 0.0, pltpu.roll(ny, 1, 0))
                left_z = jnp.where(at_top, 0.0, pltpu.roll(nz, 1, 0))
            else:
                before = slice(8 * t - 1, 8 * t + 7)
                left_y, left_z = hy[p, before, :], hz[p, before, :]
            loss = coef[4 * s + 2] * total + coef[4 * s + 3] * carriers
            perm = ground + coef[4 * s] * total
            inv = pl.reciprocal(perm + loss, approx=True)
            keep = (perm - loss) * inv
            push = COURANT * inv
            if mask is not None:
                push = push * mask
            curl_x = (nz - down(nz)) - (ny - hy[p - 1, here, :])
            curl_y = (nx - hx[p - 1, here, :]) - (nz - left_z)
            curl_z = (ny - left_y) - (nx - down(nx))
            new[6 * s][p, here, :] = keep * vx + push * curl_x
            new[6 * s + 1][p, here, :] = keep * vy + push * curl_y
            new[6 * s + 2][p, here, :] = keep * vz + push * curl_z

    def magnetic_plane(old, new, p):
        for t in range(plan.tiles):
            for s in range(2):
                magnetic(old, new, s, p, t)

    def substep(old, new, n):
        begin = jnp.where(at_low, DEEP, n + 1)
        end = jnp.where(at_high, DEEP + plan.own, plan.ext - 1 - n)
        rest = lax.rem(end - begin, 4)

        @pl.when(jnp.logical_not(at_low))
        def _():
            magnetic_plane(old, new, n)
            magnetic_plane(old, new, n + 1)

        @pl.when(at_low)
        def _():
            magnetic_plane(old, new, DEEP)

        def advance(p):
            for t in range(plan.tiles):
                for s in range(2):
                    magnetic(old, new, s, p + 1, t)
                electric(old, new, p, t)

        def one(m, _):
            advance(begin + m)
            return 0

        def four(m, _):
            for h in range(4):
                advance(begin + rest + 4 * m + h)
            return 0

        lax.fori_loop(0, rest, one, 0)
        lax.fori_loop(0, (end - begin) // 4, four, 0)

    def pair(m, _):
        substep(first, second, 2 * m)
        substep(second, first, 2 * m + 1)
        return 0

    lax.fori_loop(0, SUBSTEPS // 2, pair, 0)


def set_media(plan, code, base, silicon):
    def one(p, _):
        for t in range(plan.tiles):
            here = slice(8 * t, 8 * t + 8)
            v = code[p, here, :]
            base[p, here, :] = jnp.where(v == 0.0, SILICON_PERM, jnp.where(v == 1.0, OXIDE_PERM, 1.0))
            silicon[p, here, :] = jnp.where(v == 0.0, 1.0, 0.0)
        return 0

    lax.fori_loop(0, plan.ext, one, 0)


def clear_generation(plan, gen):
    def one(p, _):
        gen[p] = jnp.zeros((plan.rows, plan.lanes), F32)
        return 0

    lax.fori_loop(DEEP, DEEP + plan.own, one, 0)


def sum_generation(plan, gen, message):
    blocks = plan.cols // BLOCK_FACTOR
    shape = (blocks, plan.lanes)
    column = lax.broadcasted_iota(jnp.int32, shape, 0) + blocks * lax.axis_index("gx")
    upright = lax.broadcasted_iota(jnp.int32, shape, 1) == column
    across = plan.own_rows()
    for a in range(plan.own // BLOCK_FACTOR):
        p = DEEP + BLOCK_FACTOR * a
        rows = (gen[p, across, :] + gen[p + 1, across, :]) + (
            gen[p + 2, across, :] + gen[p + 3, across, :]
        )
        cells = rows.reshape(blocks, BLOCK_FACTOR, plan.lanes).sum(1)
        mean = cells.sum(1, keepdims=True) * (1.0 / (BLOCK_FACTOR * BLOCK_FACTOR * plan.lanes))
        message[a : a + 1, :] = jnp.where(upright, mean, 0.0).sum(0, keepdims=True)


def round_scratch(plan):
    wide = (plan.ext, plan.rows, plan.lanes)
    return [pltpu.VMEM((plan.ext + 1, plan.rows, plan.lanes), F32)] * 24 + [
        pltpu.VMEM(wide, F32)
    ] * 3 + [
        pltpu.VMEM((plan.ext // BLOCK_FACTOR, plan.width, plan.lanes), F32),
        pltpu.VMEM((8, plan.lanes), F32),
        pltpu.VMEM((8, 8, plan.lanes), F32),
        pltpu.VMEM(wide, F32),
    ]


def round_flops(plan):
    return SUBSTEPS * plan.ext * plan.width * plan.lanes * 150


def generation_shape(plan):
    return (plan.devices, 8, plan.lanes)


def place_strips(plan, old, code, strips):
    k = lax.axis_index("af")
    outward, inner = plan.part * k, plan.part * (1 - k)

    def place(slot, side):
        at = strip_row(plan, side)
        same = list(enumerate(list(old) + code))
        flipped = list(enumerate(list(old[6:]) + list(old[:6]) + code))
        half, rows = DEEP // 2, plan.own // 2
        if code:
            whole, corner = strips[2 * slot : 2 * slot + 2]
            near, rows = DEEP * (1 - k), plan.part // 2
            spread_strip(same, whole, rows, 0, at, near, rows)
            spread_strip(flipped, corner, half, 0, at, outward, half)
            return
        whole, beside, corner = strips[3 * slot : 3 * slot + 3]
        spread_strip(same, whole, rows, 0, at, DEEP, rows)
        spread_strip(flipped, beside, half, 0, at, inner, half)
        spread_strip(flipped, corner, half, 0, at, outward, half)

    each_side(plan, place)


def send_generation(plan, copies, started, gen, message, gen_out):
    sum_generation(plan, gen, message)
    for d in range(plan.devices):
        started.append(copies.start(message, gen_out.at[d]))


def charge_from_slabs(plan, charge, mine, across, chip, corner):
    across, chip = chip, across
    x, k = lax.axis_index("gx"), lax.axis_index("af")
    slab = plan.slab
    left = jnp.where(x == 0, mine, across)
    right = jnp.where(x == 0, across, mine)
    beyond = jnp.where(x != k, chip, corner)
    body = jnp.where(k == 0, left, right)
    before = jnp.where(k == 0, beyond, left)[slab - 1 : slab]
    after = jnp.where(k == 0, right, beyond)[0:1]
    for a in range(slab + 2):
        row = before if a == 0 else after if a == slab + 1 else body[a - 1 : a]
        spread_row(plan, row, charge, a)


def spread_row(plan, row, charge, a):
    left = (plan.cols * lax.axis_index("gx") - plan.first_row()) // BLOCK_FACTOR
    row = jnp.broadcast_to(row, (8, plan.lanes))
    row = pltpu.roll(row, lax.rem(plan.lanes - left, plan.lanes), 1)
    for c in range(plan.width // BLOCK_FACTOR):
        charge[a, 4 * c : 4 * c + 4, :] = jnp.broadcast_to(row[0:4, c : c + 1], (4, plan.lanes))


def first_kernel(plan, *refs):
    nside = len(plan.sides)
    strips_in, refs = refs[: 2 * nside], refs[2 * nside :]
    z_in, raw, other = refs[:2], refs[2:8], refs[8:14]
    medium, slab_in, under_in, coef_in = refs[14:18]
    own_out, core_out, gen_out, code_out = refs[18:22]
    z_out, strip_out = refs[22], refs[23 : 23 + 3 * nside]
    rest = refs[23 + 3 * nside :]
    old, new, (base, silicon, gen, charge, message, coef, code) = rest[:12], rest[12:24], rest[24:31]
    codes, strips, (strip_mine, corners, slabs, sems) = rest[31], rest[32 : 32 + 2 * nside], rest[-4:]
    copies = Copies(sems)
    k = lax.axis_index("af")
    near = DEEP * (1 - k)
    far = plan.part * k
    across = plan.own_rows()
    here = pl.ds(near, plan.part)
    mine = pl.ds((plan.own - DEEP) * k, plan.part)
    early = [copies.start(medium.at[mine], codes)]
    pages = 13 * DEEP + 1
    early += get_face(
        plan, copies, z_in, pages, 12 * DEEP, lambda p, n: code.at[pl.ds(far + p, n), across]
    )
    early.append(copies.start(slab_in, slabs.at[0]))
    if plan.paired:
        early.append(copies.start(z_in[1].at[z_in[1].shape[0] - 1, pl.ds(0, 8)], slabs.at[1]))
    else:
        early.append(copies.start(under_in, charge))
    early.append(copies.start(coef_in, coef))
    for source, target in zip(strips_in, strips):
        early.append(copies.start(source, target))
    late = []
    for c in range(6):
        late.append(copies.start(raw[c].at[0, mine], old[c].at[here, across]))
        late.append(copies.start(other[c].at[0, mine], old[6 + c].at[here, across]))
    for c in range(12):
        late += get_face(
            plan,
            copies,
            z_in,
            pages,
            DEEP * ((c + 6) % 12),
            lambda p, n, ref=old[c]: ref.at[pl.ds(far + p, n), across],
        )
    clear(plan, old, new, [code])
    clear_generation(plan, gen)
    wait(early)

    def settle(p, _):
        code[near + p, across, :] = codes[p].astype(F32)
        return 0

    lax.fori_loop(0, plan.part, settle, 0)
    place_strips(plan, old, [code], strips)
    set_media(plan, code, base, silicon)
    if plan.paired:
        charge_from_slabs(
            plan, charge, slabs[0], slabs[1], strips[0][13 * plan.part // 2], strips[1][13 * DEEP // 2]
        )
    wait(late)
    substeps(plan, old, new, base, silicon, charge, gen, coef)
    copies = Copies(sems)
    late = []

    def gather(slot, side):
        high_end = (side == "high") if plan.paired else (side == "low")
        low = 0 if plan.paired and side == "high" else 8
        at = low + plan.cols - 4 if high_end else low

        def one(q, _):
            for c in range(12):
                for h in range(2):
                    tile = plan.own // 2 * c + q
                    strip_mine[slot, tile, 4 * h : 4 * h + 4, :] = old[c][
                        DEEP + 2 * q + h, at : at + 4, :
                    ]
            return 0

        lax.fori_loop(0, plan.own // 2, one, 0)

    toward = DEEP + (plan.own - DEEP) * k
    inward = DEEP + (plan.own - DEEP) * (1 - k)
    for c in range(12):
        source = old[c].at[pl.ds(toward, DEEP), across]
        late.append(copies.start(source, z_out.at[pl.ds(DEEP * c, DEEP)]))
        late.append(copies.start(old[c].at[pl.ds(inward, DEEP), across], core_out.at[c]))
        late.append(copies.start(old[c].at[pl.ds(DEEP, plan.own), across], own_out.at[c]))
    late.append(copies.start(code, code_out))
    message[4:8, :] = slabs[0, 0:4, :]
    each_side(plan, gather)
    send_strips(plan, copies, late, strip_mine, corners, strip_out, 12)
    send_generation(plan, copies, late, gen, message, gen_out)
    wait(late)


def first_round(plan, strips, z_in, raw, other, medium, slab, under, coef):
    wide = (plan.cols, plan.lanes)
    nside = len(plan.sides)
    shapes = [
        (12, plan.own) + wide,
        (12, DEEP) + wide,
        generation_shape(plan),
        (plan.ext, plan.rows, plan.lanes),
    ]
    shapes += face_shapes(plan, 12 * DEEP) + strip_shapes(plan, 12)
    scratch = round_scratch(plan) + [pltpu.VMEM((plan.part,) + wide, jnp.int32)]
    scratch += [pltpu.VMEM(s.shape, F32) for s in strips]
    scratch += [
        pltpu.VMEM((nside, strip_tiles(plan, 12), 8, plan.lanes), F32),
        pltpu.VMEM((nside, 2, corner_tiles(plan, 12), 8, plan.lanes), F32),
        pltpu.VMEM((2, 8, plan.lanes), F32),
    ]
    return call(
        plan,
        first_kernel,
        "first_round",
        shapes,
        [ANY] * (2 + 2 * nside) + [HBM] * 6 + [ANY] * 6 + [HBM, ANY, ANY, HBM],
        scratch,
        42 + 3 * nside + plan.devices,
        round_flops(plan),
        10_000_000,
    )(*strips, *z_in, *raw, *other, medium, slab, under, coef)


def second_kernel(plan, *refs):
    nside = len(plan.sides)
    strips_in, refs = refs[: 3 * nside], refs[3 * nside :]
    z_in, (core_in, own_in, code_in, charge_in, coef_in) = refs[:1], refs[1:6]
    kept, sent, gen_out, rest = refs[6:12], refs[12], refs[13], refs[14:]
    old, new, (base, silicon, gen, charge, message, coef, code) = rest[:12], rest[12:24], rest[24:31]
    strips, sems = rest[31:-1], rest[-1]
    copies = Copies(sems)
    k = lax.axis_index("af")
    across = plan.own_rows()
    outward = plan.part * k
    inner = plan.part * (1 - k)
    early = [copies.start(code_in, code), copies.start(charge_in, charge)]
    early.append(copies.start(coef_in, coef))
    for source, target in zip(strips_in, strips):
        early.append(copies.start(source, target))
    late = []
    for c in range(12):
        flip = (c + 6) % 12
        late.append(copies.start(own_in.at[c], old[c].at[pl.ds(DEEP, plan.own), across]))
        late += get_face(
            plan,
            copies,
            z_in,
            12 * DEEP,
            DEEP * flip,
            lambda p, n, ref=old[c]: ref.at[pl.ds(outward + p, n), across],
        )
        late.append(copies.start(core_in.at[flip], old[c].at[pl.ds(inner, DEEP), across]))
    clear(plan, old, new, [])
    clear_generation(plan, gen)
    wait(early)
    place_strips(plan, old, [], strips)
    set_media(plan, code, base, silicon)
    wait(late)
    substeps(plan, old, new, base, silicon, charge, gen, coef)
    copies = Copies(sems)
    late = []
    for c in range(6):
        late.append(copies.start(old[6 + c].at[pl.ds(DEEP, plan.own), across], sent.at[c]))
    for c in range(6):
        target = kept[c].at[0, pl.ds(plan.own * k, plan.own)]
        late.append(copies.start(old[c].at[pl.ds(DEEP, plan.own), across], target))
    message[...] = jnp.zeros(message.shape, F32)
    send_generation(plan, copies, late, gen, message, gen_out)
    wait(late)


def second_round(plan, strips, z_in, core_in, own_in, code, charge, coef):
    wide = (plan.cols, plan.lanes)
    nside = len(plan.sides)
    shapes = [(1, plan.planes) + wide] * 6 + [(6, plan.own) + wide, generation_shape(plan)]
    scratch = round_scratch(plan) + [pltpu.VMEM(s.shape, F32) for s in strips]
    return call(
        plan,
        second_kernel,
        "second_round",
        shapes,
        [ANY] * (2 + 3 * nside) + [HBM] * 4,
        scratch,
        39 + 3 * nside + plan.devices,
        round_flops(plan),
        10_000_000,
    )(*strips, *z_in, core_in, own_in, code, charge, coef)


def join_kernel(plan, *refs):
    got, outs, (half, sems) = refs[6], refs[7:13], refs[13:]
    copies = Copies(sems)
    rows = pl.ds(plan.own * (1 - lax.axis_index("af")), plan.own)
    early = [copies.start(got.at[c], half.at[c]) for c in range(6)]
    late = []
    for c in range(6):
        early[c].wait()
        late.append(copies.start(half.at[c], outs[c].at[0, rows]))
    wait(late)


def join(plan, halves, got):
    shapes = [h.shape for h in halves]
    aliases = {c: c for c in range(6)}
    scratch = [pltpu.VMEM(got.shape, F32)]
    return call(
        plan, join_kernel, "join", shapes, [HBM] * 6 + [ANY], scratch, 12, moved=3_000_000, aliases=aliases
    )(*halves, got)


def charge_shape(plan):
    return (plan.ext // BLOCK_FACTOR, plan.width, plan.lanes)


def spread_whole(plan, density):
    z, x, k = (lax.axis_index(a) for a in LINE)
    side = plan.width // BLOCK_FACTOR
    padded = jnp.pad(density, ((1, 1), (side, side)))
    top = (plan.planes * z + plan.own * k) // BLOCK_FACTOR
    left = side + (plan.cols * x - plan.first_row()) // BLOCK_FACTOR
    tile = lax.dynamic_slice(padded, (top, left), (plan.ext // BLOCK_FACTOR, side))
    return jnp.broadcast_to(jnp.repeat(tile, BLOCK_FACTOR, 1)[:, :, None], charge_shape(plan))


def carrier_kernel(plan, last, *refs):
    gens_in, refs = refs[0], refs[1:]
    if last:
        density_in, refs = refs[0], refs[1:]
    outs = refs[:1] if last else refs[:2]
    gens, one, two, source, charge, slab_out, sems = refs[len(outs) :]
    copies = Copies(sems)
    rows, cols, lanes = plan.grid_rows, plan.grid_cols, plan.lanes
    z, x, k = (lax.axis_index(a) for a in LINE)
    own = plan.own // BLOCK_FACTOR
    early = [copies.start(gens_in, gens)]
    if last:
        early.append(copies.start(density_in, one))
    zero = jnp.zeros((8, lanes), F32)
    for ref in (two,) if last else (one, two):
        ref[0:8, :] = zero
        ref[8 + rows : 16 + rows, :] = zero
    wait(early)

    def unpack(line, _):
        top = pl.multiple_of(8 * line, 8)
        for dk in range(2):
            tiles = [gens[(line * plan.gx + dx) * 2 + dk, 0:own, :] for dx in range(plan.gx)]
            source[pl.ds(top + own * dk, own), :] = SOURCE_FACTOR * functools.reduce(jnp.add, tiles)
        if not last:
            for dx in range(plan.gx):
                slab = gens[(line * plan.gx + dx) * 2, 4 : 4 + plan.slab, :]
                one[pl.ds(8 + top + plan.slab * dx, plan.slab), :] = slab
        return 0

    lax.fori_loop(0, plan.gz, unpack, 0, unroll=plan.gz <= 4)
    inside = lax.broadcasted_iota(jnp.int32, (8, lanes), 1) < cols
    for step in range(CSTEPS):
        old, new = (one, two) if step % 2 == 0 else (two, one)
        for r in range(8, 8 + rows, 8):
            now, before = old[r : r + 8, :], old[r - 1 : r + 7, :]
            around = (
                old[r + 1 : r + 9, :]
                + before
                + pltpu.roll(now, lanes - 1, 1)
                + pltpu.roll(now, 1, 1)
                - 4.0 * now
            )
            later = (
                now
                + SPREAD_COEFF * around
                - MOBILITY_TERM * (now - before)
                - LIFETIME_DECAY * now
                + source[r - 8 : r, :]
            )
            new[r : r + 8, :] = jnp.where(inside, later, 0.0)
    if last:
        mine = one[pl.ds(8 + (z * plan.gx + x) * plan.slab, plan.slab), :]
        slab_out[...] = mine[:, :cols]
        copies.start(slab_out, outs[0]).wait()
        return
    late = [copies.start(one, outs[0])]
    for a in range(plan.ext // BLOCK_FACTOR):
        top = (plan.planes * z + plan.own * k - DEEP) // BLOCK_FACTOR + a
        spread_row(plan, one[pl.ds(8 + jnp.clip(top, 0, rows - 1), 1), :], charge, a)
    late.append(copies.start(charge, outs[1]))
    wait(late)


def carriers(plan, last, *arrays):
    grid, slab = (plan.grid_rows + 16, plan.lanes), (plan.slab, plan.grid_cols)
    scratch = [
        pltpu.VMEM(arrays[0].shape, F32),
        pltpu.VMEM(grid, F32),
        pltpu.VMEM(grid, F32),
        pltpu.VMEM((plan.grid_rows, plan.lanes), F32),
        pltpu.VMEM(charge_shape(plan), F32),
        pltpu.VMEM(slab, F32),
    ]
    return call(
        plan,
        lambda plan, *refs: carrier_kernel(plan, last, *refs),
        "carriers",
        [slab] if last else [grid, charge_shape(plan)],
        [ANY] + [HBM] * (len(arrays) - 1),
        scratch,
        4,
        2_000_000,
        1_000_000,
    )(*arrays)


def local(ex, ey, ez, hx, hy, hz, medium, table, density):
    raw = (ex, ey, ez, hx, hy, hz)
    plan = Plan(*medium.shape, density.shape[0])

    def send(message, target):
        return lax.ppermute(message, LINE, line_pairs(plan, target))

    def everywhere(message, axes):
        return lax.all_to_all(message, axes, split_axis=0, concat_axis=0, tiled=True)

    core = lambda z, x, k: (z, x, 1 - k)
    beyond = lambda z, k: z - 1 if k == 0 else z + 1

    def exchange(face, strips):
        got, each = [], len(strips) // len(plan.sides)
        for n, side in enumerate(plan.sides):
            to = functools.partial(across_step, side)
            mine = strips[each * n : each * n + each]
            got.append(send(mine[0], lambda z, x, k: (z, to(x), k)))
            if each == 3:
                got.append(send(mine[1], lambda z, x, k: (z, to(x), 1 - k)))
            got.append(send(mine[-1], lambda z, x, k: (beyond(z, k), to(x), 1 - k)))
        return [send(part, lambda z, x, k: (beyond(z, k), x, 1 - k)) for part in face], got

    other = [send(r, core) for r in raw]
    slab = jnp.pad(density, ((0, 8 - plan.slab), (0, plan.lanes - plan.grid_cols)))
    packed = pack(plan, raw, other, medium, slab, table)
    z_in, strips = exchange(packed[:2], packed[2:-1])
    coef = packed[-1]
    under = slab
    if not plan.paired:
        tiles = plan.gz * plan.gx
        slabs = everywhere(jnp.broadcast_to(density, (tiles,) + density.shape), ("gz", "gx"))
        under = spread_whole(plan, slabs.reshape(plan.grid_rows, plan.grid_cols))
    outs = first_round(plan, strips, z_in, raw, other, medium, slab, under, coef)
    own, core_msg, gens, code = outs[:4]
    gens = everywhere(gens, LINE)
    z_in, strips = exchange(outs[4:5], outs[5:])
    core_in = send(core_msg, core)
    grid, charge = carriers(plan, False, gens)
    outs = second_round(plan, strips, z_in, core_in, own, code, charge, coef)
    halves, sent, gens = outs[:6], outs[6], outs[7]
    gens = everywhere(gens, LINE)
    got = send(sent, core)
    (new_slab,) = carriers(plan, True, gens, grid)
    return tuple(join(plan, halves, got)) + (new_slab,)


def solution(mesh):
    field = P("af", ("group", "gz"), "gx", None)
    slabs = P(("group", "gz", "gx"), None)
    in_specs = (field,) * 6 + (P(("group", "gz"), "gx", None), P(), slabs)
    out_specs = (field,) * 6 + (slabs,)
    return jax.shard_map(local, mesh=mesh, in_specs=in_specs, out_specs=out_specs, check_vma=False)
```
